32 devices in a mesh: groups: 2 (over y), wide: 8 (over z, x), narrow: 2 (over core).
Axes of the slice: x: 2, y: 2, z: 4, core: 2. Of those that a mesh axis runs over, the one named last changes fastest.
Arguments:
- candidates: bfloat16 [16, 2048, 512], P('groups', ('wide', 'narrow')), parts along dimension 0, may hold values from -6 to 6
- pre_inner: bfloat16 [512, 512], replicated, may hold values from -0.25 to 0.25
- pre_bias: float32 [512], replicated, may hold values from -3 to 3
- pre_outer: bfloat16 [512, 512], replicated, may hold values from -0.25 to 0.25
- user_vector: bfloat16 [16, 512], P('groups'), parts along dimension 0, may hold values from -0.25 to 0.25
- kept_index: int32 [16, 512], P('groups'), parts along dimension 0, may hold values from 0 to 2047, as said below
- slot_request: int32 [16], P('groups'), parts along dimension 0, may hold values from 0 to 7, each once
- history_kv: bfloat16 [16, 2, 512, 512], P(('groups', 'wide'), None, None, 'narrow'), parts along dimension 0, may hold values from -6 to 6
- history_bias: float32 [16, 8, 512], P(('groups', 'wide'), 'narrow'), parts along dimension 0, may hold values from -8 to 404
- history_length: int32 [16], P(('groups', 'wide')), parts along dimension 0, may hold values from 64 to 512, as said below
- query_weight: bfloat16 [512, 512], replicated, may hold values from -0.25 to 0.25
- norm_gain: float32 [512], replicated, may hold values from 0.1 to 1.9
- expert_weight: bfloat16 [8, 512, 256], P('narrow'), may hold values from -0.25 to 0.25
- gate_weight: bfloat16 [512, 64], replicated, may hold values from -0.25 to 0.25
- gate_bias: float32 [8, 8], replicated, may hold values from -4 to 401
- tower_inner: bfloat16 [8, 256, 128], P('narrow'), may hold values from -0.375 to 0.375
- tower_outer: bfloat16 [8, 128], P('narrow'), may hold values from -0.5 to 0.5
Outputs:
- prerank_score: float32 [16, 2048], P('groups', ('wide', 'narrow')), parts along dimension 0
- rank_score: float32 [8, 16, 2048], P(None, 'groups', ('wide', 'narrow')), parts along dimension 1
The draws below stay inside these ranges and needn't reach their ends.
There are 2 independent parts, one for each index of `groups`. The reference program is written for one: setup_inputs(seed, part) draws one part's arguments, and reference() takes and returns one part's arrays. A program takes and returns all parts, laid end to end along the dimension named above; an argument that names none is the same for every part. Nothing has to cross between parts.
Inputs may be any that keep to these rules, and one draw needn't show every extreme that they name: `kept_index`: each row holds 512 distinct candidate numbers; of the candidates of one request in one aligned block of 128 numbers at most 64 are kept, and exactly 64 in some block of every request. `slot_request`: a permutation; slot s belongs to ranking group s. `history_length`: at least one entry equals 512.
All inputs are finite; a program needn't handle non-finite values.
Results may differ from the reference program's by a relative error of at most 0.0085.
Values may be sent and summed in bfloat16 or wider, within the bound.
No kernel may reach another device: no remote copies, remote signals or barrier semaphores. Data moves between devices by JAX's collectives and lax.ppermute only.
A program may use at most 64 MiB of HBM per device.

```python
import jax
import jax.numpy as jnp
from jax import lax

F = 512
PH = 512
D = 512
H = 8
DH = 64
EXPERTS = 8
TASKS = 8
EH = 256
TH = 128
KEEP = 512
C = 2048
L = 512
R = 8
N_WIDE = 8
N_NARROW = 2


def draw_kept_index(key, part):
    shards = N_WIDE * N_NARROW
    shard_len = C // shards
    mean_kept = KEEP // shards
    order_key = jax.random.fold_in(key, 11)
    pair_key = jax.random.fold_in(key, 12)
    inner_key = jax.random.fold_in(key, 13)
    list_key = jax.random.fold_in(key, 14)
    order_score = jax.random.randint(order_key, (R, shards), 0, 1 << 20) * shards + jnp.arange(shards, dtype=jnp.int32)[None, :]
    shard_order = jnp.argsort(order_score, axis=1, stable=True)
    placed = jnp.argsort(shard_order, axis=1, stable=True)
    shifts = jax.random.randint(pair_key, (R, shards // 2), -mean_kept, mean_kept + 1)
    shifts = jnp.where(jnp.arange(shards // 2)[None, :] == 0, mean_kept, shifts)
    paired = jnp.concatenate([mean_kept + shifts, mean_kept - shifts], axis=1)
    counts = jnp.take_along_axis(paired, placed, axis=1)
    inner_score = jax.random.randint(inner_key, (R, shards, shard_len), 0, 1 << 20) * shard_len + jnp.arange(shard_len, dtype=jnp.int32)[None, None, :]
    inner_rank = jnp.argsort(jnp.argsort(inner_score, axis=2, stable=True), axis=2, stable=True)
    chosen = (inner_rank < counts[:, :, None]).reshape(R, C)
    ordered = jnp.argsort(jnp.where(chosen, 0, 1), axis=1, stable=True)[:, :KEEP]
    list_score = jax.random.randint(list_key, (R, KEEP), 0, 1 << 20) * KEEP + jnp.arange(KEEP, dtype=jnp.int32)[None, :]
    shuffle = jnp.argsort(list_score, axis=1, stable=True)
    return jnp.take_along_axis(ordered, shuffle, axis=1).astype(jnp.int32)


def draw_history_length(key, part):
    lengths = jax.random.randint(jax.random.fold_in(key, 21), (R,), L // 8, L + 1)
    longest = jax.random.randint(jax.random.fold_in(key, 22), (), 0, R)
    return jnp.where(jnp.arange(R) == longest, L, lengths).astype(jnp.int32)


def draw_history_bias(key, part):
    noise_key = jax.random.fold_in(key, 31)
    return jnp.clip(2.0 * jax.random.normal(noise_key, (R, H, L), jnp.float32), -8.0, 8.0)


def draw_gate_bias(key, part):
    noise_key = jax.random.fold_in(key, 41)
    return jnp.clip(jax.random.normal(noise_key, (TASKS, EXPERTS), jnp.float32), -4.0, 4.0)


def shard_levels(key, extent, pieces, low, high):
    loudness, own = 1.0, jax.random.fold_in(key, 6)
    for axis_at, parts in pieces:
        draws = jnp.exp(jax.random.uniform(jax.random.fold_in(own, axis_at), (parts,), jnp.float32, low / len(pieces), high / len(pieces)))
        loudness = loudness * jnp.repeat(draws, extent[axis_at] // parts).reshape([-1 if axis == axis_at else 1 for axis in range(len(extent))])
    return loudness


def centred(rng, extent, width, most, cuts=(), kind=jnp.bfloat16):
    values = jax.random.normal(rng, extent, jnp.float32) * width
    if len(cuts) > 0:
        values = shard_levels(rng, extent, cuts, -0.22, 0.18) * values
    return jnp.clip(values, min=-most, max=most).astype(kind)


def setup_inputs(seed: int = 0, part: int = 0) -> dict:
    splits = jax.random.split(jax.random.key(seed), 18)
    part_keys = jax.random.split(jax.random.fold_in(splits[17], part), 18)
    candidates = centred(part_keys[0], (R, C, F), 1.0, 6.0, ((1, 16),))
    pre_inner = centred(splits[1], (F, PH), F ** -0.5, 0.25)
    pre_bias = centred(splits[2], (PH,), 0.5, 3.0, (), jnp.float32)
    pre_outer = centred(splits[3], (PH, D), PH ** -0.5, 0.25)
    user_vector = centred(part_keys[4], (R, D), D ** -0.5, 0.25)
    kept_index = draw_kept_index(jax.random.fold_in(jax.random.fold_in(splits[17], part), 71), part)
    slot_request = jax.random.permutation(part_keys[6], R).astype(jnp.int32)
    history_kv = centred(part_keys[7], (R, 2, L, H * DH), 1.0, 6.0, ((0, 8), (3, 2)))
    history_bias = draw_history_bias(jax.random.fold_in(jax.random.fold_in(splits[17], part), 71), part)
    history_length = draw_history_length(jax.random.fold_in(jax.random.fold_in(splits[17], part), 71), part)
    query_weight = centred(splits[10], (D, H * DH), D ** -0.5, 0.25)
    norm_gain = jnp.clip(1.0 + 0.18 * jax.random.normal(splits[11], (D,), jnp.float32), 0.1, 1.9)
    expert_weight = centred(splits[12], (EXPERTS, D, EH), D ** -0.5, 0.25, ((0, 2),))
    gate_weight = centred(splits[13], (D, TASKS * EXPERTS), D ** -0.5, 0.25)
    gate_bias = draw_gate_bias(jax.random.fold_in(splits[17], 71), part)
    tower_inner = centred(splits[15], (TASKS, EH, TH), EH ** -0.5, 0.375, ((0, 2),))
    tower_outer = centred(splits[16], (TASKS, TH), TH ** -0.5, 0.5, ((0, 2),))
    return dict(candidates=candidates, pre_inner=pre_inner, pre_bias=pre_bias, pre_outer=pre_outer, user_vector=user_vector, kept_index=kept_index, slot_request=slot_request, history_kv=history_kv, history_bias=history_bias, history_length=history_length, query_weight=query_weight, norm_gain=norm_gain, expert_weight=expert_weight, gate_weight=gate_weight, gate_bias=gate_bias, tower_inner=tower_inner, tower_outer=tower_outer)


def reference(candidates, pre_inner, pre_bias, pre_outer, user_vector, kept_index, slot_request, history_kv, history_bias, history_length, query_weight, norm_gain, expert_weight, gate_weight, gate_bias, tower_inner, tower_outer):
    score_scale = float(DH) ** (-0.5)

    def per_slot(slot_index):
        request = slot_request[slot_index]
        features = candidates[request]
        hidden_pre = jax.nn.relu(jnp.dot(features, pre_inner, preferred_element_type=jnp.float32) + pre_bias).astype(jnp.bfloat16)
        embedded = jnp.dot(hidden_pre, pre_outer, preferred_element_type=jnp.float32).astype(jnp.bfloat16)
        pre_row = jnp.dot(embedded, user_vector[request], preferred_element_type=jnp.float32)
        kept_ids = kept_index[request].astype(jnp.int32)
        kept_rows = embedded[kept_ids]
        queries = jnp.dot(kept_rows, query_weight, preferred_element_type=jnp.float32).astype(jnp.bfloat16).reshape(KEEP, H, DH)
        history_keys = history_kv[slot_index, 0].reshape(L, H, DH)
        history_values = history_kv[slot_index, 1].reshape(L, H, DH)
        scores = jnp.einsum('khd,lhd->hkl', queries.astype(jnp.float32), history_keys.astype(jnp.float32)) * score_scale
        scores = scores + history_bias[slot_index][:, None, :]
        visible = jnp.arange(L, dtype=jnp.int32) < history_length[slot_index]
        scores = jnp.where(visible[None, None, :], scores, -jnp.inf)
        row_max = lax.optimization_barrier(jnp.max(scores, axis=2, keepdims=True))
        powers = jnp.exp(scores - row_max)
        weights = (powers / lax.optimization_barrier(jnp.sum(powers, axis=2, keepdims=True))).astype(jnp.bfloat16)
        attended = jnp.einsum('hkl,lhd->khd', weights.astype(jnp.float32), history_values.astype(jnp.float32)).astype(jnp.bfloat16).reshape(KEEP, H * DH)
        mixed_in = kept_rows.astype(jnp.float32) + attended.astype(jnp.float32)
        normed = (mixed_in * lax.rsqrt(lax.optimization_barrier(jnp.mean(mixed_in * mixed_in, axis=1, keepdims=True)) + 1e-06) * norm_gain).astype(jnp.bfloat16)
        expert_out = jax.nn.relu(jnp.einsum('kd,edh->keh', normed.astype(jnp.float32), expert_weight.astype(jnp.float32))).astype(jnp.bfloat16)
        logits = jnp.dot(normed, gate_weight, preferred_element_type=jnp.float32).reshape(KEEP, TASKS, EXPERTS) + gate_bias[None]
        logit_max = lax.optimization_barrier(jnp.max(logits, axis=2, keepdims=True))
        gate_pow = jnp.exp(logits - logit_max)
        gate_probs = (gate_pow / lax.optimization_barrier(jnp.sum(gate_pow, axis=2, keepdims=True))).astype(jnp.bfloat16)
        mixture = jnp.einsum('kte,keh->kth', gate_probs.astype(jnp.float32), expert_out.astype(jnp.float32)).astype(jnp.bfloat16)
        tower_act = jax.nn.relu(jnp.einsum('kth,thj->ktj', mixture.astype(jnp.float32), tower_inner.astype(jnp.float32))).astype(jnp.bfloat16)
        task_logit = jnp.einsum('ktj,tj->kt', tower_act.astype(jnp.float32), tower_outer.astype(jnp.float32))
        rank_row = jnp.zeros((TASKS, C), jnp.float32).at[:, kept_ids].set(task_logit.T)
        return (pre_row, rank_row)
    pre_rows, rank_rows = lax.map(per_slot, jnp.arange(R, dtype=jnp.int32))
    order_ids = slot_request.astype(jnp.int32)
    prerank_score = jnp.zeros((R, C), jnp.float32).at[order_ids].set(pre_rows)
    rank_full = jnp.zeros((R, TASKS, C), jnp.float32).at[order_ids].set(rank_rows)
    return (prerank_score, jnp.transpose(rank_full, (1, 0, 2)))
```

```python
import functools

import jax
import jax.numpy as jnp
from jax import lax
from jax.experimental import pallas as pl
from jax.experimental.pallas import tpu as pltpu
from jax.sharding import PartitionSpec as P

NT = (((1,), (1,)), ((), ()))
VMEM = pl.BlockSpec(memory_space=pltpu.VMEM)
SMEM = pl.BlockSpec(memory_space=pltpu.SMEM)
ANY = pl.BlockSpec(memory_space=pl.ANY)
VMEM_LIMIT = 40 * 1024 * 1024


def dot_f32(a, b):
    return jnp.dot(a, b, preferred_element_type=jnp.float32)


def dot_nt(a, b):
    return lax.dot_general(a, b, NT, preferred_element_type=jnp.float32)


def split_by(values, divisor):
    if divisor & (divisor - 1) == 0:
        shift = divisor.bit_length() - 1
        return lax.shift_right_logical(values, shift), values & (divisor - 1)
    quotient = lax.div(values, divisor)
    return quotient, values - quotient * divisor


def three_parts(values):
    high = values.astype(jnp.bfloat16)
    rest = values - high.astype(jnp.float32)
    middle = rest.astype(jnp.bfloat16)
    low = (rest - middle.astype(jnp.float32)).astype(jnp.bfloat16)
    return jnp.concatenate([high, middle, low], axis=0)


def sum_parts(stacked, rows):
    return stacked[:rows] + stacked[rows : 2 * rows] + stacked[2 * rows :]


def pack_body(narrow_count, half, where_ref, slot_ref, kept_ref, cand_hbm, out_ref, lane_ref, cand_ref, sems):
    requests, shard_len, _ = cand_ref.shape
    kept_count = kept_ref.shape[1]
    copies = [
        pltpu.make_async_copy(cand_hbm.at[r], cand_ref.at[r], sems.at[r]) for r in range(requests)
    ]
    for copy in copies:
        copy.start()
    base = where_ref[0] * shard_len
    ids = base + lax.broadcasted_iota(jnp.int32, (shard_len, kept_count), 0)
    request_rows = lax.broadcasted_iota(jnp.int32, (requests, kept_count), 0)
    flags = jnp.zeros((requests, shard_len), jnp.float32)
    for r in range(requests):
        hits = jnp.where(kept_ref[r : r + 1, :] == ids, 1.0, 0.0).astype(jnp.bfloat16)
        row = jnp.where(request_rows == r, 1.0, 0.0).astype(jnp.bfloat16)
        flags = flags + dot_nt(row, hits)
    earlier = lax.broadcasted_iota(jnp.int32, (shard_len, shard_len), 0) < lax.broadcasted_iota(
        jnp.int32, (shard_len, shard_len), 1
    )
    places = dot_f32(
        flags.astype(jnp.bfloat16), jnp.where(earlier, 1.0, 0.0).astype(jnp.bfloat16)
    ).astype(jnp.int32)
    before = jnp.sum((kept_ref[...] < base).astype(jnp.int32), axis=1, keepdims=True)
    _, owner = split_by(before + places, narrow_count)
    within, _ = split_by(places, narrow_count)
    lane_ref[...] = jnp.where(flags > 0.5, owner * half + within, -1)
    rows = narrow_count * half
    row_at = lax.broadcasted_iota(jnp.int32, (rows, shard_len), 0)
    for copy in copies:
        copy.wait()
    for s in range(requests):
        r = slot_ref[s]
        pick = jnp.where(lane_ref[pl.ds(r, 1), :] == row_at, 1.0, 0.0).astype(jnp.bfloat16)
        out_ref[s * rows : (s + 1) * rows, :] = dot_f32(pick, cand_ref[r]).astype(jnp.bfloat16)


def pack_rows(where, slot_request, kept_index, candidates, narrow_count, half):
    requests, shard_len, features = candidates.shape
    rows = requests * narrow_count * half
    return pl.pallas_call(
        functools.partial(pack_body, narrow_count, half),
        out_shape=(
            jax.ShapeDtypeStruct((rows, features), jnp.bfloat16),
            jax.ShapeDtypeStruct((requests, shard_len), jnp.int32),
        ),
        in_specs=[SMEM, SMEM, VMEM, ANY],
        out_specs=(VMEM, VMEM),
        scratch_shapes=[
            pltpu.VMEM((requests, shard_len, features), jnp.bfloat16),
            pltpu.SemaphoreType.DMA((requests,)),
        ],
        compiler_params=pltpu.CompilerParams(vmem_limit_bytes=VMEM_LIMIT),
        cost_estimate=pl.CostEstimate(
            flops=2 * rows * shard_len * features, bytes_accessed=4 * rows * features, transcendentals=0
        ),
        name="pack_rows",
    )(where, slot_request, kept_index, candidates)


def prerank_body(shard_len, cand_ref, inner_ref, bias_ref, outer_ref, user_ref, lane_ref, out_ref):
    requests = user_ref.shape[0]
    step = 2 if requests % 2 == 0 else 1
    for r in range(0, requests, step):
        rows = cand_ref[r * shard_len : (r + step) * shard_len, :]
        hidden = jnp.maximum(dot_f32(rows, inner_ref[...]) + bias_ref[...], 0.0).astype(jnp.bfloat16)
        embedded = dot_f32(hidden, outer_ref[...]).astype(jnp.bfloat16)
        scores = dot_nt(user_ref[...], embedded)
        for i in range(step):
            out_ref[r + i : r + i + 1, :] = scores[r + i : r + i + 1, i * shard_len : (i + 1) * shard_len]


def prerank(candidates, pre_inner, pre_bias, pre_outer, user_vector, lanes):
    requests, shard_len, features = candidates.shape
    rows = requests * shard_len
    return pl.pallas_call(
        functools.partial(prerank_body, shard_len),
        out_shape=jax.ShapeDtypeStruct((requests, shard_len), jnp.float32),
        in_specs=[VMEM] * 6,
        out_specs=VMEM,
        compiler_params=pltpu.CompilerParams(vmem_limit_bytes=VMEM_LIMIT),
        cost_estimate=pl.CostEstimate(
            flops=4 * rows * features * pre_inner.shape[1], bytes_accessed=4 * rows * features, transcendentals=0
        ),
        name="prerank",
    )(
        candidates.reshape(rows, features),
        pre_inner,
        pre_bias.reshape(1, -1),
        pre_outer,
        user_vector,
        lanes,
    )


def rank_body(
    narrow_count,
    shards,
    shard_len,
    spread,
    where_ref,
    kept_ref,
    arrived_hbm,
    inner_hbm,
    bias_ref,
    outer_hbm,
    query_hbm,
    gain_ref,
    gate_hbm,
    gate_bias_ref,
    *rest,
):
    history_hbm = rest[:narrow_count]
    history_bias_refs = rest[narrow_count : 2 * narrow_count]
    expert_hbm = rest[2 * narrow_count : 3 * narrow_count]
    tower_hbm = rest[3 * narrow_count : 4 * narrow_count]
    tower_outer_refs = rest[4 * narrow_count : 5 * narrow_count]
    (
        out_ref,
        arrived_ref,
        inner_ref,
        outer_ref,
        query_ref,
        gate_ref,
        history_ref,
        expert_ref,
        tower_ref,
        embed_ref,
        queries_ref,
        attended_ref,
        expert_out_ref,
        gates_ref,
        mixture_ref,
        logit_ref,
        sems,
    ) = rest[5 * narrow_count :]
    rows_in = arrived_ref.shape[0]
    width = arrived_ref.shape[1]
    half = rows_in // shards
    rows = embed_ref.shape[0]
    span = history_ref.shape[2]
    head_columns = history_ref.shape[3]
    heads_here = history_bias_refs[0].shape[0]
    head_size = head_columns // heads_here
    experts_here = expert_ref.shape[1]
    experts = narrow_count * experts_here
    tasks_here = tower_ref.shape[1]
    tasks = narrow_count * tasks_here
    block = rows // experts
    expert_width = expert_ref.shape[3]

    me = where_ref[0]
    length = where_ref[1]
    pairs = [
        (arrived_hbm, arrived_ref),
        (inner_hbm, inner_ref),
        (outer_hbm, outer_ref),
        (query_hbm, query_ref),
        (gate_hbm, gate_ref),
    ]
    pairs += [(history_hbm[i], history_ref.at[i]) for i in range(narrow_count)]
    pairs += [(expert_hbm[i], expert_ref.at[i]) for i in range(narrow_count)]
    pairs += [(tower_hbm[i], tower_ref.at[i]) for i in range(narrow_count)]
    copies = [pltpu.make_async_copy(src, dst, sems.at[i]) for i, (src, dst) in enumerate(pairs)]
    for copy in copies:
        copy.start()

    kept_row = kept_ref[...]
    sources = lax.broadcasted_iota(jnp.int32, (shards, kept_row.shape[1]), 0)
    edge = sources * shard_len
    starts = jnp.sum((kept_row < edge).astype(jnp.int32), axis=1, keepdims=True)
    ends = jnp.sum((kept_row < edge + shard_len).astype(jnp.int32), axis=1, keepdims=True)
    first, _ = split_by(starts + (narrow_count - 1) - me, narrow_count)
    last, _ = split_by(ends + (narrow_count - 1) - me, narrow_count)
    lane_source, lane_within = split_by(lax.broadcasted_iota(jnp.int32, (shards, rows_in), 1), half)
    mine = lane_source == lax.broadcasted_iota(jnp.int32, (shards, rows_in), 0)
    target = jnp.where(mine & (first + lane_within < last), first + lane_within + 1, 0)
    target = jnp.sum(target, axis=0, keepdims=True) - 1
    placing = jnp.where(
        target == lax.broadcasted_iota(jnp.int32, (rows, rows_in), 0), 1.0, 0.0
    ).astype(jnp.bfloat16)

    copies[0].wait()
    packed = dot_f32(placing, arrived_ref[...]).astype(jnp.bfloat16)
    copies[1].wait()
    hidden = jnp.maximum(dot_f32(packed, inner_ref[...]) + bias_ref[...], 0.0).astype(jnp.bfloat16)
    copies[2].wait()
    embed = dot_f32(hidden, outer_ref[...]).astype(jnp.bfloat16)
    embed_ref[...] = embed
    copies[3].wait()
    queries = dot_f32(embed, query_ref[...]).astype(jnp.bfloat16)
    queries_ref[...] = queries

    tile = max(head_size, 128)
    in_tile = tile // head_size
    lane_head, _ = split_by(lax.broadcasted_iota(jnp.int32, (1, tile), 1), head_size)
    visible = lax.broadcasted_iota(jnp.int32, (1, span), 1) < length
    scale = float(head_size) ** (-0.5)
    for i in range(narrow_count):
        copies[5 + i].wait()
        at = lax.rem(me + i, narrow_count) * head_columns
        for t in range(head_columns // tile):
            columns = pl.ds(pl.multiple_of(at + t * tile, tile), tile)
            query_tile = queries_ref[:, columns]
            keys = history_ref[i, 0, :, t * tile : (t + 1) * tile]
            values = history_ref[i, 1, :, t * tile : (t + 1) * tile]
            merged = None
            for h in range(in_tile):
                own = lane_head == h
                head = t * in_tile + h
                masked = jnp.where(own, query_tile, jnp.zeros_like(query_tile))
                scores = dot_nt(masked, keys) * scale
                offset = jnp.where(visible, history_bias_refs[i][head : head + 1, :], -jnp.inf)
                scores = scores + offset
                powers = jnp.exp(scores - jnp.max(scores, axis=1, keepdims=True))
                total = jnp.sum(powers, axis=1, keepdims=True)
                result = dot_f32(powers.astype(jnp.bfloat16), values) / total
                merged = result if merged is None else jnp.where(own, result, merged)
            attended_ref[:, columns] = merged.astype(jnp.bfloat16)

    mixed_in = embed_ref[...].astype(jnp.float32) + attended_ref[...].astype(jnp.float32)
    normed = (
        mixed_in
        * lax.rsqrt(jnp.mean(mixed_in * mixed_in, axis=1, keepdims=True) + 1e-06)
        * gain_ref[...]
    ).astype(jnp.bfloat16)

    copies[4].wait()
    logits = dot_f32(normed, gate_ref[...]) + gate_bias_ref[...]
    by_task = jnp.transpose(logits).reshape(tasks, experts, rows)
    gate_pow = jnp.exp(by_task - jnp.max(by_task, axis=1, keepdims=True))
    gate_probs = gate_pow / jnp.sum(gate_pow, axis=1, keepdims=True)
    gates = jnp.transpose(gate_probs.reshape(tasks * experts, rows)).astype(jnp.bfloat16)

    blocks = rows // block
    for i in range(narrow_count):
        copies[5 + narrow_count + i].wait()
        for e in range(experts_here):
            result = jnp.maximum(dot_f32(normed, expert_ref[i, e]), 0.0).astype(jnp.bfloat16)
            at = (i * experts_here + e) * block
            for b in range(blocks):
                expert_out_ref[b, at : at + block, :] = result[b * block : (b + 1) * block, :]

    gate_at = lax.broadcasted_iota(jnp.int32, (tasks * experts, experts * block), 0)
    column = lax.broadcasted_iota(jnp.int32, (tasks * experts, experts * block), 1)
    column_expert, _ = split_by(column, block)
    _, column_expert = split_by(column_expert + me * experts_here, experts)
    _, row_in_block = split_by(lax.broadcasted_iota(jnp.int32, (rows, experts * block), 0), block)
    _, column_row = split_by(lax.broadcasted_iota(jnp.int32, (rows, experts * block), 1), block)
    diagonal = row_in_block == column_row
    for t in range(tasks):
        expand = jnp.where(gate_at == column_expert + t * experts, 1.0, 0.0).astype(jnp.bfloat16)
        wide = jnp.where(diagonal, dot_f32(gates, expand), 0.0).astype(jnp.bfloat16)
        for b in range(blocks):
            gates_ref[b, t * block : (t + 1) * block, :] = wide[b * block : (b + 1) * block, :]
    for b in range(blocks):
        mixture = dot_f32(gates_ref[b], expert_out_ref[b]).astype(jnp.bfloat16)
        for t in range(tasks):
            mixture_ref[t, b * block : (b + 1) * block, :] = mixture[t * block : (t + 1) * block, :]

    for i in range(narrow_count):
        copies[5 + 2 * narrow_count + i].wait()
        first_task = lax.rem(me + i, narrow_count) * tasks_here
        for t in range(tasks_here):
            task = first_task + t
            act = jnp.maximum(dot_f32(mixture_ref[task], tower_ref[i, t]), 0.0).astype(jnp.bfloat16)
            logit = dot_nt(tower_outer_refs[i][...], act)
            logit_ref[pl.ds(task, 1), :] = logit[t : t + 1, :]

    parts = three_parts(logit_ref[...])
    returned = sum_parts(dot_f32(parts, placing), tasks)
    if not spread:
        out_ref[...] = returned
        return
    lanes = out_ref.shape[2]
    lane = lax.broadcasted_iota(jnp.int32, (tasks, lanes), 1)
    keep = (lane >= me * half) & (lane < (me + 1) * half)
    per_tile = lanes // half
    for s in range(shards):
        tile_at, place = divmod(s, per_tile)
        values = returned[:, tile_at * lanes : (tile_at + 1) * lanes]
        moved = pltpu.roll(values, lax.rem(me * half + (lanes - place * half), lanes), 1)
        out_ref[s] = jnp.where(keep, moved, 0.0)


def rank_slot(
    where,
    kept,
    arrived,
    pre_inner,
    pre_bias,
    pre_outer,
    query_weight,
    norm_gain,
    gate_weight,
    gate_bias,
    history,
    history_bias,
    experts,
    towers,
    tower_outer,
    shards,
    shard_len,
    spread,
):
    narrow_count = len(history)
    rows_in, width = arrived.shape
    kept_count = kept.shape[1]
    rows = kept_count // narrow_count
    tasks = narrow_count * towers[0].shape[0]
    expert_count = narrow_count * experts[0].shape[0]
    expert_width = experts[0].shape[2]
    block = rows // expert_count
    if spread:
        out_shape = jax.ShapeDtypeStruct((shards, tasks, 128), jnp.float32)
    else:
        out_shape = jax.ShapeDtypeStruct((tasks, rows_in), jnp.float32)
    bf16 = jnp.bfloat16
    flops = 2 * rows * (rows_in * width + 3 * width * width + 2 * expert_count * width * expert_width)
    return pl.pallas_call(
        functools.partial(rank_body, narrow_count, shards, shard_len, spread),
        out_shape=out_shape,
        in_specs=[SMEM, VMEM, ANY, ANY, VMEM, ANY, ANY, VMEM, ANY, VMEM]
        + [ANY] * narrow_count
        + [VMEM] * narrow_count
        + [ANY] * narrow_count
        + [ANY] * narrow_count
        + [VMEM] * narrow_count,
        out_specs=VMEM,
        scratch_shapes=[
            pltpu.VMEM(arrived.shape, bf16),
            pltpu.VMEM(pre_inner.shape, bf16),
            pltpu.VMEM(pre_outer.shape, bf16),
            pltpu.VMEM(query_weight.shape, bf16),
            pltpu.VMEM(gate_weight.shape, bf16),
            pltpu.VMEM((narrow_count,) + history[0].shape, bf16),
            pltpu.VMEM((narrow_count,) + experts[0].shape, bf16),
            pltpu.VMEM((narrow_count,) + towers[0].shape, bf16),
            pltpu.VMEM((rows, pre_outer.shape[1]), bf16),
            pltpu.VMEM((rows, query_weight.shape[1]), bf16),
            pltpu.VMEM((rows, query_weight.shape[1]), bf16),
            pltpu.VMEM((rows // block, expert_count * block, expert_width), bf16),
            pltpu.VMEM((rows // block, tasks * block, expert_count * block), bf16),
            pltpu.VMEM((tasks, rows, expert_width), bf16),
            pltpu.VMEM((tasks, rows), jnp.float32),
            pltpu.SemaphoreType.DMA((5 + 3 * narrow_count,)),
        ],
        compiler_params=pltpu.CompilerParams(vmem_limit_bytes=VMEM_LIMIT),
        cost_estimate=pl.CostEstimate(flops=flops, bytes_accessed=6 * 1024 * 1024, transcendentals=0),
        name="rank_slot",
    )(
        where,
        kept,
        arrived,
        pre_inner,
        pre_bias.reshape(1, -1),
        pre_outer,
        query_weight,
        norm_gain.reshape(1, -1),
        gate_weight,
        gate_bias.reshape(1, -1),
        *history,
        *history_bias,
        *experts,
        *towers,
        *tower_outer,
    )


def unpack_body(narrow_count, half, slot_ref, lane_ref, returned_ref, out_ref):
    requests, shard_len = lane_ref.shape
    _, tasks, lanes = returned_ref.shape
    row_at = lax.broadcasted_iota(jnp.int32, (lanes, shard_len), 0)
    for s in range(requests):
        r = slot_ref[s]
        values = returned_ref[s * narrow_count]
        for i in range(1, narrow_count):
            values = values + returned_ref[s * narrow_count + i]
        pick = jnp.where(lane_ref[pl.ds(r, 1), :] == row_at, 1.0, 0.0).astype(jnp.bfloat16)
        result = sum_parts(dot_f32(three_parts(values), pick), tasks)
        for t in range(tasks):
            out_ref[t, pl.ds(r, 1), :] = result[t : t + 1, :]


def unpack_rows(slot_request, lanes, returned, narrow_count, half):
    requests, shard_len = lanes.shape
    tasks = returned.shape[1]
    return pl.pallas_call(
        functools.partial(unpack_body, narrow_count, half),
        out_shape=jax.ShapeDtypeStruct((tasks, requests, shard_len), jnp.float32),
        in_specs=[SMEM, VMEM, VMEM],
        out_specs=VMEM,
        compiler_params=pltpu.CompilerParams(vmem_limit_bytes=VMEM_LIMIT),
        name="unpack_rows",
    )(slot_request, lanes, returned)


def lanes_of(kept_index, device_rank, shard_len, narrow_count, half):
    base = device_rank * shard_len
    ids = base + jnp.arange(shard_len, dtype=jnp.int32)
    flags = jnp.any(kept_index[:, :, None] == ids[None, None, :], axis=1)
    places = jnp.cumsum(flags.astype(jnp.int32), axis=1) - flags.astype(jnp.int32)
    before = jnp.sum((kept_index < base).astype(jnp.int32), axis=1, keepdims=True)
    return jnp.where(flags, (before + places) % narrow_count * half + places // narrow_count, -1)


def from_others(values, narrow_count):
    pieces = [values]
    for shift in range(1, narrow_count):
        steps = [((i + shift) % narrow_count, i) for i in range(narrow_count)]
        pieces.append(lax.ppermute(values, "narrow", steps))
    return pieces


def on_device(
    candidates,
    pre_inner,
    pre_bias,
    pre_outer,
    user_vector,
    kept_index,
    slot_request,
    history_kv,
    history_bias,
    history_length,
    query_weight,
    norm_gain,
    expert_weight,
    gate_weight,
    gate_bias,
    tower_inner,
    tower_outer,
):
    wide_count = lax.axis_size("wide")
    narrow_count = lax.axis_size("narrow")
    shards = wide_count * narrow_count
    wide_rank = lax.axis_index("wide")
    narrow_rank = lax.axis_index("narrow")
    device_rank = wide_rank * narrow_count + narrow_rank
    requests, shard_len, features = candidates.shape
    kept_count = kept_index.shape[1]
    capacity = 2 * kept_count // shards
    half = -(-capacity // narrow_count)
    group_size = history_kv.shape[0]
    tasks = narrow_count * tower_inner.shape[0]
    width = pre_outer.shape[1]
    both = ("wide", "narrow")
    blocked = (
        shard_len % 128 == 0
        and requests % 8 == 0
        and half % 16 == 0
        and narrow_count * half <= 128
        and 128 % half == 0
        and group_size == 1
    )

    if blocked:
        packed, lanes = pack_rows(
            device_rank.reshape(1), slot_request, kept_index, candidates, narrow_count, half
        )
    else:
        lanes = lanes_of(kept_index, device_rank, shard_len, narrow_count, half)
        picks = lanes[:, None, :] == jnp.arange(narrow_count * half, dtype=jnp.int32)[None, :, None]
        packed = jnp.einsum(
            "rcs,rsd->rcd", picks.astype(jnp.bfloat16), candidates, preferred_element_type=jnp.float32
        ).astype(jnp.bfloat16)[slot_request]
    packed = packed.reshape(wide_count, group_size, narrow_count, half, features)
    packed = jnp.swapaxes(packed, 1, 2).reshape(shards, group_size * half, features)
    arrived = lax.all_to_all(packed, both, split_axis=0, concat_axis=0, tiled=True)
    arrived = jnp.swapaxes(arrived.reshape(shards, group_size, half, features), 0, 1)
    arrived = arrived.reshape(group_size, shards * half, features)

    history = from_others(history_kv, narrow_count)
    biases = from_others(history_bias, narrow_count)
    experts = from_others(expert_weight, narrow_count)
    towers = from_others(tower_inner, narrow_count)
    tower_outs = from_others(tower_outer, narrow_count)

    if blocked:
        prerank_score = prerank(candidates, pre_inner, pre_bias, pre_outer, user_vector, lanes)
    else:
        hidden = jax.nn.relu(
            dot_f32(candidates.reshape(requests * shard_len, features), pre_inner) + pre_bias
        ).astype(jnp.bfloat16)
        embedded = dot_f32(hidden, pre_outer).astype(jnp.bfloat16)
        prerank_score = jnp.einsum(
            "rsd,rd->rs",
            embedded.reshape(requests, shard_len, width),
            user_vector,
            preferred_element_type=jnp.float32,
        )

    results = []
    for g in range(group_size):
        request = slot_request[wide_rank * group_size + g]
        results.append(
            rank_slot(
                jnp.stack([narrow_rank, history_length[g]]),
                lax.dynamic_slice_in_dim(kept_index, request, 1, 0),
                arrived[g],
                pre_inner,
                pre_bias,
                pre_outer,
                query_weight,
                norm_gain,
                gate_weight,
                gate_bias,
                [piece[g] for piece in history],
                [piece[g] for piece in biases],
                experts,
                towers,
                tower_outs,
                shards,
                shard_len,
                blocked,
            )
        )

    if blocked:
        returned = lax.all_to_all(results[0], both, split_axis=0, concat_axis=0, tiled=True)
        return (prerank_score, unpack_rows(slot_request, lanes, returned, narrow_count, half))
    sending = jnp.stack(results).reshape(group_size, tasks, shards, half)
    sending = jnp.transpose(sending, (2, 0, 1, 3)).reshape(shards, -1)
    returned = lax.all_to_all(sending, both, split_axis=0, concat_axis=0, tiled=True)
    returned = returned.reshape(wide_count, narrow_count, group_size, tasks, half)
    returned = jnp.transpose(returned, (0, 2, 3, 1, 4)).reshape(requests, tasks, narrow_count * half)
    request_ids = jnp.arange(requests, dtype=jnp.int32)
    slot_of = jnp.sum(
        jnp.where(slot_request[None, :] == request_ids[:, None], request_ids[None, :], 0), axis=1
    )
    rank_score = jnp.einsum(
        "rcs,rtc->trs",
        picks.astype(jnp.float32),
        returned[slot_of],
        precision=lax.Precision.HIGHEST,
    )
    return (prerank_score, rank_score)


def solution(mesh):
    return jax.shard_map(
        on_device,
        mesh=mesh,
        in_specs=(
            P("groups", ("wide", "narrow"), None),
            P(),
            P(),
            P(),
            P("groups", None),
            P("groups", None),
            P("groups"),
            P(("groups", "wide"), None, None, "narrow"),
            P(("groups", "wide"), "narrow", None),
            P(("groups", "wide")),
            P(),
            P(),
            P("narrow", None, None),
            P(),
            P(),
            P("narrow", None, None),
            P("narrow", None),
        ),
        out_specs=(P("groups", ("wide", "narrow")), P(None, "groups", ("wide", "narrow"))),
        check_vma=False,
    )
```

```python
import functools

import jax
import jax.numpy as jnp
from jax import lax
from jax.experimental import pallas as pl
from jax.experimental.pallas import tpu as pltpu
from jax.sharding import PartitionSpec as P

NT = (((1,), (1,)), ((), ()))
VMEM = pl.BlockSpec(memory_space=pltpu.VMEM)
SMEM = pl.BlockSpec(memory_space=pltpu.SMEM)
ANY = pl.BlockSpec(memory_space=pl.ANY)
VMEM_LIMIT = 16 * 1024 * 1024
LANES = 128
BRIEF = pl.CostEstimate(flops=1, bytes_accessed=1, transcendentals=0)


def in_hbm(values):
    return pltpu.with_memory_space_constraint(values, pltpu.HBM)


def in_vmem(values):
    return pltpu.with_memory_space_constraint(values, pltpu.VMEM)


def dot_f32(a, b):
    return jnp.dot(a, b, preferred_element_type=jnp.float32)


def dot_nt(a, b):
    return lax.dot_general(a, b, NT, preferred_element_type=jnp.float32)


def split_by(values, divisor):
    if divisor & (divisor - 1) == 0:
        shift = divisor.bit_length() - 1
        return lax.shift_right_logical(values, shift), values & (divisor - 1)
    quotient = lax.div(values, divisor)
    return quotient, values - quotient * divisor


def three_parts(values):
    high = values.astype(jnp.bfloat16)
    rest = values - high.astype(jnp.float32)
    middle = rest.astype(jnp.bfloat16)
    low = (rest - middle.astype(jnp.float32)).astype(jnp.bfloat16)
    return jnp.concatenate([high, middle, low], axis=0)


def sum_parts(stacked, rows):
    return stacked[:rows] + stacked[rows : 2 * rows] + stacked[2 * rows :]


def pack_body(
    narrow_count, half, slot_ref, kept_hbm, cand_hbm, out_hbm, lane_ref, back_ref, kept_ref, cand_ref, out_ref, sems
):
    requests, shard_len, _ = cand_ref.shape
    kept_count = kept_ref.shape[1]
    kept_copy = pltpu.make_async_copy(kept_hbm, kept_ref, sems.at[0])
    cand_copy = pltpu.make_async_copy(cand_hbm, cand_ref, sems.at[1])
    kept_copy.start()
    cand_copy.start()
    device = lax.axis_index("wide") * narrow_count + lax.axis_index("narrow")
    base = device * shard_len
    ids = base + lax.broadcasted_iota(jnp.int32, (shard_len, kept_count), 0)
    request_rows = lax.broadcasted_iota(jnp.int32, (requests, kept_count), 0)
    kept_copy.wait()
    flags = jnp.zeros((requests, shard_len), jnp.float32)
    for r in range(requests):
        hits = jnp.where(kept_ref[r : r + 1, :] == ids, 1.0, 0.0).astype(jnp.bfloat16)
        row = jnp.where(request_rows == r, 1.0, 0.0).astype(jnp.bfloat16)
        flags = flags + dot_nt(row, hits)
    earlier = lax.broadcasted_iota(jnp.int32, (shard_len, shard_len), 0) < lax.broadcasted_iota(
        jnp.int32, (shard_len, shard_len), 1
    )
    places = dot_f32(
        flags.astype(jnp.bfloat16), jnp.where(earlier, 1.0, 0.0).astype(jnp.bfloat16)
    ).astype(jnp.int32)
    before = jnp.sum((kept_ref[...] < base).astype(jnp.int32), axis=1, keepdims=True)
    _, owner = split_by(before + places, narrow_count)
    within, _ = split_by(places, narrow_count)
    kept_here = flags > 0.5
    lane_ref[...] = jnp.where(kept_here, owner * half + within, -1)
    offset = lax.rem(device * half, LANES)
    back_ref[...] = jnp.where(kept_here, owner * LANES + offset + within, -1)
    rows = narrow_count * half
    row_at = lax.broadcasted_iota(jnp.int32, (rows, shard_len), 0)
    cand_copy.wait()
    sends = []
    for s in range(requests):
        r = slot_ref[s]
        pick = jnp.where(lane_ref[pl.ds(r, 1), :] == row_at, 1.0, 0.0).astype(jnp.bfloat16)
        out_ref[s * rows : (s + 1) * rows, :] = dot_f32(pick, cand_ref[r]).astype(jnp.bfloat16)
        part = pl.ds(s * rows, rows)
        sends.append(pltpu.make_async_copy(out_ref.at[part], out_hbm.at[part], sems.at[2 + s]))
        sends[s].start()
    for send in sends:
        send.wait()


def pack_rows(slot_request, kept_index, candidates, narrow_count, half):
    requests, shard_len, features = candidates.shape
    rows = requests * narrow_count * half
    return pl.pallas_call(
        functools.partial(pack_body, narrow_count, half),
        out_shape=(
            pltpu.HBM((rows, features), jnp.bfloat16),
            jax.ShapeDtypeStruct((requests, shard_len), jnp.int32),
            jax.ShapeDtypeStruct((requests, shard_len), jnp.int32),
        ),
        in_specs=[SMEM, ANY, ANY],
        out_specs=(ANY, VMEM, VMEM),
        scratch_shapes=[
            pltpu.VMEM(kept_index.shape, jnp.int32),
            pltpu.VMEM((requests, shard_len, features), jnp.bfloat16),
            pltpu.VMEM((rows, features), jnp.bfloat16),
            pltpu.SemaphoreType.DMA((2 + requests,)),
        ],
        compiler_params=pltpu.CompilerParams(vmem_limit_bytes=VMEM_LIMIT),
        cost_estimate=pl.CostEstimate(
            flops=2 * rows * shard_len * features, bytes_accessed=4 * rows * features, transcendentals=0
        ),
        name="pack_rows",
    )(in_hbm(slot_request), in_hbm(kept_index), in_hbm(candidates))


def prerank_body(shard_len, cand_ref, inner_ref, bias_ref, outer_ref, user_ref, lane_ref, out_ref):
    requests = user_ref.shape[0]
    step = 2 if requests % 2 == 0 else 1
    for r in range(0, requests, step):
        rows = cand_ref[r * shard_len : (r + step) * shard_len, :]
        hidden = jnp.maximum(dot_f32(rows, inner_ref[...]) + bias_ref[...], 0.0).astype(jnp.bfloat16)
        embedded = dot_f32(hidden, outer_ref[...]).astype(jnp.bfloat16)
        scores = dot_nt(user_ref[...], embedded)
        for i in range(step):
            out_ref[r + i : r + i + 1, :] = scores[r + i : r + i + 1, i * shard_len : (i + 1) * shard_len]


def prerank(candidates, pre_inner, pre_bias, pre_outer, user_vector, lanes):
    requests, shard_len, features = candidates.shape
    rows = requests * shard_len
    return pl.pallas_call(
        functools.partial(prerank_body, shard_len),
        out_shape=jax.ShapeDtypeStruct((requests, shard_len), jnp.float32),
        in_specs=[VMEM] * 6,
        out_specs=VMEM,
        compiler_params=pltpu.CompilerParams(vmem_limit_bytes=VMEM_LIMIT),
        cost_estimate=BRIEF,
        name="prerank",
    )(
        candidates.reshape(rows, features),
        pre_inner,
        pre_bias.reshape(1, -1),
        pre_outer,
        user_vector,
        lanes,
    )


def prepare_body(narrow_count, weight_count, shards, shard_len, slot_at, slot_ref, length_ref, kept_ref, *rest):
    history_refs = rest[:narrow_count]
    bias_refs = rest[narrow_count : 2 * narrow_count]
    tower_outer_refs = rest[2 * narrow_count : 3 * narrow_count]
    pre_bias_ref, gain_ref, gate_bias_ref = rest[3 * narrow_count : 3 * narrow_count + 3]
    rest = rest[3 * narrow_count + 3 :]
    weight_refs = rest[:weight_count]
    placing_ref, keys_hbm, values_hbm, vectors_ref, gate_offsets_ref, tower_columns_ref = rest[weight_count:][:6]
    loaded_refs = rest[weight_count + 6 : -4]
    keys_ref, values_ref, head_sems, sems = rest[-4:]
    copies = [
        pltpu.make_async_copy(source, loaded, sems.at[i])
        for i, (source, loaded) in enumerate(zip(weight_refs, loaded_refs))
    ]
    for copy in copies:
        copy.start()
    group_size, _, span, head_columns = history_refs[0].shape
    heads_here = bias_refs[0].shape[1]
    rows, rows_in = placing_ref.shape
    half = rows_in // shards
    me = lax.axis_index("narrow")
    request = slot_ref[lax.axis_index("wide") * group_size + slot_at]

    vectors_ref[0:1, :] = pre_bias_ref[...]
    vectors_ref[1:2, :] = gain_ref[...]
    tasks, experts = gate_bias_ref.shape
    gate_lane = lax.broadcasted_iota(jnp.int32, (tasks * experts, experts), 1)
    _, gate_row = split_by(lax.broadcasted_iota(jnp.int32, (tasks * experts, experts), 0), experts)
    offsets = jnp.broadcast_to(gate_bias_ref[...][:, None, :], (tasks, experts, experts))
    offsets = jnp.where(gate_row == gate_lane, offsets.reshape(tasks * experts, experts), 0.0)
    gate_offsets_ref[...] = jnp.broadcast_to(jnp.sum(offsets, axis=1, keepdims=True), gate_offsets_ref.shape)
    tasks_here, tower_width = tower_outer_refs[0].shape
    column = lax.broadcasted_iota(jnp.int32, (tower_width, LANES), 1)
    for i in range(narrow_count):
        outer = jnp.transpose(tower_outer_refs[i][...].astype(jnp.float32))
        for t in range(tasks_here):
            task = lax.rem(me + i, narrow_count) * tasks_here + t
            tower_columns_ref[i * tasks_here + t] = jnp.where(
                column == task, outer[:, t : t + 1], 0.0
            ).astype(jnp.bfloat16)

    kept_row = kept_ref[pl.ds(request, 1), :]
    edge = lax.broadcasted_iota(jnp.int32, (shards, kept_row.shape[1]), 0) * shard_len
    starts = jnp.sum((kept_row < edge).astype(jnp.int32), axis=1, keepdims=True)
    ends = jnp.sum((kept_row < edge + shard_len).astype(jnp.int32), axis=1, keepdims=True)
    first, _ = split_by(starts + (narrow_count - 1) - me, narrow_count)
    last, _ = split_by(ends + (narrow_count - 1) - me, narrow_count)
    lane_source, lane_within = split_by(lax.broadcasted_iota(jnp.int32, (shards, rows_in), 1), half)
    mine = lane_source == lax.broadcasted_iota(jnp.int32, (shards, rows_in), 0)
    target = jnp.where(mine & (first + lane_within < last), first + lane_within + 1, 0)
    target = jnp.sum(target, axis=0, keepdims=True) - 1
    placing_ref[...] = jnp.where(
        target == lax.broadcasted_iota(jnp.int32, (rows, rows_in), 0), 1.0, 0.0
    ).astype(jnp.bfloat16)

    head_size = head_columns // heads_here
    tile = 2 * head_size
    visible = lax.broadcasted_iota(jnp.int32, (1, span), 1) < length_ref[slot_at]
    lane = lax.broadcasted_iota(jnp.int32, (span, tile), 1)
    for i in range(narrow_count):
        for t in range(heads_here // 2):
            keys = history_refs[i][slot_at, 0, :, t * tile : (t + 1) * tile]
            keys = jnp.transpose(keys.astype(jnp.float32)).astype(jnp.bfloat16)
            values = history_refs[i][slot_at, 1, :, t * tile : (t + 1) * tile]
            for h in range(2):
                head = 2 * t + h
                at = i * heads_here + head
                bias = jnp.where(visible, bias_refs[i][slot_at, head : head + 1, :], -1e30)
                parts = three_parts(jnp.broadcast_to(bias, (8, span)).astype(jnp.float32))
                row = lax.broadcasted_iota(jnp.int32, (head_size, span), 0)
                high = jnp.broadcast_to(parts[0:1].astype(jnp.float32), (head_size, span))
                middle = jnp.broadcast_to(parts[8:9].astype(jnp.float32), (head_size, span))
                low = jnp.broadcast_to(parts[16:17].astype(jnp.float32), (head_size, span))
                extra = jnp.where(
                    row == 0, high, jnp.where(row == 1, middle, jnp.where(row == 2, low, 0.0))
                ).astype(jnp.bfloat16)
                own = h * head_size
                other = (1 - h) * head_size
                keys_ref[at, own : own + head_size, :] = keys[own : own + head_size, :]
                keys_ref[at, other : other + head_size, :] = extra
                mine = (lane >= own) & (lane < own + head_size)
                values_ref[at] = jnp.where(mine, values.astype(jnp.float32), 1.0).astype(jnp.bfloat16)
                copies.append(pltpu.make_async_copy(keys_ref.at[at], keys_hbm.at[at], head_sems.at[0, at]))
                copies[-1].start()
                copies.append(pltpu.make_async_copy(values_ref.at[at], values_hbm.at[at], head_sems.at[1, at]))
                copies[-1].start()
    for copy in copies:
        copy.wait()


def prepare(
    slot_request,
    lengths,
    kept_index,
    history,
    biases,
    tower_outer,
    pre_bias,
    norm_gain,
    gate_bias,
    weights,
    shards,
    shard_len,
    half,
    slot_at,
):
    narrow_count = len(history)
    _, _, span, head_columns = history[0].shape
    heads_here = biases[0].shape[1]
    heads = narrow_count * heads_here
    tile = 2 * head_columns // heads_here
    rows = kept_index.shape[1] // narrow_count
    tasks, experts = gate_bias.shape
    width = norm_gain.shape[0]
    bf16 = jnp.bfloat16
    return pl.pallas_call(
        functools.partial(prepare_body, narrow_count, len(weights), shards, shard_len, slot_at),
        out_shape=(
            pltpu.VMEM((rows, shards * half), bf16),
            pltpu.HBM((heads, tile, span), bf16),
            pltpu.HBM((heads, span, tile), bf16),
            pltpu.VMEM((8, width), jnp.float32),
            pltpu.VMEM((tasks * experts, LANES), jnp.float32),
            pltpu.VMEM((tasks, tower_outer[0].shape[1], LANES), bf16),
            *[pltpu.VMEM(weight.shape, weight.dtype) for weight in weights],
        ),
        in_specs=[SMEM, SMEM] + [VMEM] * (4 + 3 * narrow_count) + [ANY] * len(weights),
        out_specs=(VMEM, ANY, ANY) + (VMEM,) * (3 + len(weights)),
        scratch_shapes=[
            pltpu.VMEM((heads, tile, span), bf16),
            pltpu.VMEM((heads, span, tile), bf16),
            pltpu.SemaphoreType.DMA((2, heads)),
            pltpu.SemaphoreType.DMA((len(weights),)),
        ],
        compiler_params=pltpu.CompilerParams(vmem_limit_bytes=VMEM_LIMIT),
        cost_estimate=BRIEF,
        name="prepare",
    )(
        slot_request,
        lengths,
        kept_index,
        *history,
        *biases,
        *tower_outer,
        pre_bias.reshape(1, -1),
        norm_gain.reshape(1, -1),
        gate_bias,
        *[in_hbm(weight) for weight in weights],
    )


def rank_body(narrow_count, pieces, shards, spread, heads, *rest):
    arrived_hbm, keys_hbm, values_hbm = rest[:3]
    expert_hbm = rest[3 : 3 + pieces]
    rest = rest[3 + pieces :]
    placing_ref, vectors_ref, gate_offsets_ref, tower_columns_ref, inner_ref, outer_ref, query_ref, gate_ref = rest[:8]
    tower_refs = rest[8 : 8 + narrow_count]
    (
        out_ref,
        embed_ref,
        queries_ref,
        attended_ref,
        expert_out_ref,
        gates_ref,
        mixture_ref,
        arrived_ref,
        keys_ref,
        values_ref,
        expert_refs,
        sems,
    ) = rest[8 + narrow_count :]
    arrival = pltpu.make_async_copy(arrived_hbm, arrived_ref, sems.at[0])
    head_copies = [
        pltpu.make_async_copy(keys_hbm, keys_ref, sems.at[1]),
        pltpu.make_async_copy(values_hbm, values_ref, sems.at[2]),
    ]
    expert_copies = []
    for i in range(pieces):
        at = sum(piece.shape[0] for piece in expert_hbm[:i])
        here = expert_refs.at[pl.ds(at, expert_hbm[i].shape[0])]
        expert_copies.append(pltpu.make_async_copy(expert_hbm[i], here, sems.at[3 + i]))
    for copy in [arrival] + head_copies + expert_copies:
        copy.start()

    rows = embed_ref.shape[0]
    half = arrived_ref.shape[0] // shards
    width = queries_ref.shape[1]
    head_size = width // heads
    experts = expert_refs.shape[0]
    experts_here = experts // narrow_count
    tasks_here = tower_refs[0].shape[0]
    tasks = narrow_count * tasks_here
    block = rows // experts
    blocks = rows // block
    me = lax.axis_index("narrow")

    arrival.wait()
    packed = dot_f32(placing_ref[...], arrived_ref[...]).astype(jnp.bfloat16)
    hidden = jnp.maximum(dot_f32(packed, inner_ref[...]) + vectors_ref[0:1, :], 0.0).astype(jnp.bfloat16)
    embed = dot_f32(hidden, outer_ref[...]).astype(jnp.bfloat16)
    embed_ref[...] = embed
    queries = dot_f32(embed, query_ref[...]).astype(jnp.bfloat16)
    queries_ref[...] = queries

    tile = 2 * head_size
    heads_here = heads // narrow_count
    scale = float(head_size) ** (-0.5)
    lane = lax.broadcasted_iota(jnp.int32, (rows, tile), 1)
    left = lane < head_size
    for copy in head_copies:
        copy.wait()
    for i in range(narrow_count):
        at = lax.rem(me + i, narrow_count) * (width // narrow_count)
        for t in range(heads_here // 2):
            columns = pl.ds(pl.multiple_of(at + t * tile, tile), tile)
            scaled = queries_ref[:, columns].astype(jnp.float32) * scale
            results = []
            for h in range(2):
                head = i * heads_here + 2 * t + h
                other = (1 - h) * head_size
                ones = jnp.where((lane >= other) & (lane < other + 3), 1.0, 0.0)
                query = jnp.where(left if h == 0 else ~left, scaled, ones).astype(jnp.bfloat16)
                scores = dot_f32(query, keys_ref[head])
                powers = jnp.exp(scores - jnp.max(scores, axis=1, keepdims=True))
                results.append(dot_f32(powers.astype(jnp.bfloat16), values_ref[head]))
            sums = pltpu.roll(jnp.where(left, results[1], results[0]), head_size, 1)
            attended_ref[:, columns] = (jnp.where(left, results[0], results[1]) / sums).astype(jnp.bfloat16)

    mixed_in = embed_ref[...].astype(jnp.float32) + attended_ref[...].astype(jnp.float32)
    normed = (
        mixed_in
        * lax.rsqrt(jnp.mean(mixed_in * mixed_in, axis=1, keepdims=True) + 1e-06)
        * vectors_ref[1:2, :]
    ).astype(jnp.bfloat16)

    logits = dot_nt(gate_ref[...], normed) + gate_offsets_ref[:, 0:1]
    by_task = logits.reshape(tasks, experts, rows)
    gate_pow = jnp.exp(by_task - jnp.max(by_task, axis=1, keepdims=True))
    gate_probs = gate_pow / jnp.sum(gate_pow, axis=1, keepdims=True)
    gates = jnp.transpose(gate_probs.reshape(tasks * experts, rows)).astype(jnp.bfloat16)

    for copy in expert_copies:
        copy.wait()
    for e in range(experts):
        result = jnp.maximum(dot_f32(normed, expert_refs[e]), 0.0).astype(jnp.bfloat16)
        for b in range(blocks):
            expert_out_ref[b, e * block : (e + 1) * block, :] = result[b * block : (b + 1) * block, :]

    gate_at = lax.broadcasted_iota(jnp.int32, (tasks * experts, experts * block), 0)
    column = lax.broadcasted_iota(jnp.int32, (tasks * experts, experts * block), 1)
    column_expert, _ = split_by(column, block)
    _, column_expert = split_by(column_expert + me * experts_here, experts)
    _, row_in_block = split_by(lax.broadcasted_iota(jnp.int32, (rows, experts * block), 0), block)
    _, column_row = split_by(lax.broadcasted_iota(jnp.int32, (rows, experts * block), 1), block)
    diagonal = row_in_block == column_row
    for t in range(tasks):
        _, task = split_by(me * tasks_here + t, tasks)
        expand = jnp.where(gate_at == column_expert + task * experts, 1.0, 0.0).astype(jnp.bfloat16)
        wide = jnp.where(diagonal, dot_f32(gates, expand), 0.0).astype(jnp.bfloat16)
        for b in range(blocks):
            gates_ref[b, t * block : (t + 1) * block, :] = wide[b * block : (b + 1) * block, :]
    for b in range(blocks):
        mixture = dot_f32(gates_ref[b], expert_out_ref[b]).astype(jnp.bfloat16)
        for t in range(tasks):
            mixture_ref[t, b * block : (b + 1) * block, :] = mixture[t * block : (t + 1) * block, :]

    logits = jnp.zeros((rows, LANES), jnp.float32)
    for i in range(narrow_count):
        for t in range(tasks_here):
            at = i * tasks_here + t
            act = jnp.maximum(dot_f32(mixture_ref[at], tower_refs[i][t]), 0.0).astype(jnp.bfloat16)
            logits = logits + dot_f32(act, tower_columns_ref[at])
    by_task = jnp.transpose(logits)[:tasks]

    returned = sum_parts(dot_f32(three_parts(by_task), placing_ref[...]), tasks)
    if not spread:
        out_ref[...] = returned
        return
    for s in range(shards):
        at = s * half // LANES * LANES
        out_ref[s] = returned[:, at : at + LANES]


def rank_slot(
    arrived, placing, keys, values, vectors, gate_offsets, tower_columns, weights, experts, towers, shards, spread
):
    inner, outer, query, gate_rows = weights
    narrow_count = len(towers)
    rows, rows_in = placing.shape
    heads = keys.shape[0]
    width = outer.shape[1]
    tasks = tower_columns.shape[0]
    expert_count = gate_rows.shape[0] // tasks
    expert_width = experts[0].shape[2]
    block = rows // expert_count
    if spread:
        out_shape = jax.ShapeDtypeStruct((shards, tasks, LANES), jnp.float32)
    else:
        out_shape = jax.ShapeDtypeStruct((tasks, rows_in), jnp.float32)
    bf16 = jnp.bfloat16
    flops = 2 * rows * (rows_in * width + 3 * width * width + 2 * expert_count * width * expert_width)
    far = [arrived, keys, values, *experts]
    near = [placing, vectors, gate_offsets, tower_columns, *weights, *towers]
    return pl.pallas_call(
        functools.partial(rank_body, narrow_count, len(experts), shards, spread, heads),
        out_shape=out_shape,
        in_specs=[ANY] * len(far) + [VMEM] * len(near),
        out_specs=VMEM,
        scratch_shapes=[
            pltpu.VMEM((rows, width), bf16),
            pltpu.VMEM((rows, query.shape[1]), bf16),
            pltpu.VMEM((rows, query.shape[1]), bf16),
            pltpu.VMEM((rows // block, expert_count * block, expert_width), bf16),
            pltpu.VMEM((rows // block, tasks * block, expert_count * block), bf16),
            pltpu.VMEM((tasks, rows, expert_width), bf16),
            pltpu.VMEM(arrived.shape, bf16),
            pltpu.VMEM(keys.shape, bf16),
            pltpu.VMEM(values.shape, bf16),
            pltpu.VMEM((expert_count,) + experts[0].shape[1:], bf16),
            pltpu.SemaphoreType.DMA((3 + len(experts),)),
        ],
        compiler_params=pltpu.CompilerParams(vmem_limit_bytes=VMEM_LIMIT),
        cost_estimate=pl.CostEstimate(flops=flops, bytes_accessed=6 * 1024 * 1024, transcendentals=0),
        name="rank_slot",
    )(*[in_hbm(array) for array in far], *[in_vmem(array) for array in near])


def unpack_body(narrow_count, slot_ref, back_ref, returned_ref, out_ref):
    requests, shard_len = back_ref.shape
    _, tasks, lanes = returned_ref.shape
    row_at = lax.broadcasted_iota(jnp.int32, (narrow_count * lanes, shard_len), 0)
    for s in range(requests):
        r = slot_ref[s]
        pieces = [returned_ref[s * narrow_count + i] for i in range(narrow_count)]
        parts = three_parts(jnp.concatenate(pieces, axis=1))
        pick = jnp.where(back_ref[pl.ds(r, 1), :] == row_at, 1.0, 0.0).astype(jnp.bfloat16)
        result = sum_parts(dot_f32(parts, pick), tasks)
        for t in range(tasks):
            out_ref[t, pl.ds(r, 1), :] = result[t : t + 1, :]


def unpack_rows(slot_request, back, returned, narrow_count):
    requests, shard_len = back.shape
    tasks = returned.shape[1]
    return pl.pallas_call(
        functools.partial(unpack_body, narrow_count),
        out_shape=jax.ShapeDtypeStruct((tasks, requests, shard_len), jnp.float32),
        in_specs=[SMEM, VMEM, VMEM],
        out_specs=VMEM,
        compiler_params=pltpu.CompilerParams(vmem_limit_bytes=VMEM_LIMIT),
        name="unpack_rows",
    )(slot_request, back, returned)


def lanes_of(kept_index, device_rank, shard_len, narrow_count, half):
    base = device_rank * shard_len
    ids = base + jnp.arange(shard_len, dtype=jnp.int32)
    flags = jnp.any(kept_index[:, :, None] == ids[None, None, :], axis=1)
    places = jnp.cumsum(flags.astype(jnp.int32), axis=1) - flags.astype(jnp.int32)
    before = jnp.sum((kept_index < base).astype(jnp.int32), axis=1, keepdims=True)
    return jnp.where(flags, (before + places) % narrow_count * half + places // narrow_count, -1)


def from_others(values, narrow_count):
    pieces = [values]
    for shift in range(1, narrow_count):
        steps = [((i + shift) % narrow_count, i) for i in range(narrow_count)]
        pieces.append(lax.ppermute(values, "narrow", steps))
    return pieces


def on_device(
    candidates,
    pre_inner,
    pre_bias,
    pre_outer,
    user_vector,
    kept_index,
    slot_request,
    history_kv,
    history_bias,
    history_length,
    query_weight,
    norm_gain,
    expert_weight,
    gate_weight,
    gate_bias,
    tower_inner,
    tower_outer,
):
    wide_count = lax.axis_size("wide")
    narrow_count = lax.axis_size("narrow")
    shards = wide_count * narrow_count
    wide_rank = lax.axis_index("wide")
    narrow_rank = lax.axis_index("narrow")
    device_rank = wide_rank * narrow_count + narrow_rank
    requests, shard_len, features = candidates.shape
    kept_count = kept_index.shape[1]
    capacity = 2 * kept_count // shards
    half = -(-capacity // narrow_count)
    group_size = history_kv.shape[0]
    tasks = narrow_count * tower_inner.shape[0]
    width = pre_outer.shape[1]
    both = ("wide", "narrow")
    blocked = (
        shard_len % 128 == 0
        and requests % 8 == 0
        and half % 16 == 0
        and LANES % half == 0
        and shards * half % LANES == 0
        and group_size == 1
    )

    if blocked:
        packed, lanes, back = pack_rows(slot_request, kept_index, candidates, narrow_count, half)
    else:
        lanes = lanes_of(kept_index, device_rank, shard_len, narrow_count, half)
        picks = lanes[:, None, :] == jnp.arange(narrow_count * half, dtype=jnp.int32)[None, :, None]
        packed = jnp.einsum(
            "rcs,rsd->rcd", picks.astype(jnp.bfloat16), candidates, preferred_element_type=jnp.float32
        ).astype(jnp.bfloat16)[slot_request]
    packed = packed.reshape(wide_count, group_size, narrow_count, half, features)
    packed = jnp.swapaxes(packed, 1, 2).reshape(shards, group_size * half, features)
    arrived = lax.all_to_all(packed, both, split_axis=0, concat_axis=0, tiled=True)
    arrived = jnp.swapaxes(arrived.reshape(shards, group_size, half, features), 0, 1)
    arrived = arrived.reshape(group_size, shards * half, features)

    experts_here = expert_weight.shape[0]
    halves = [expert_weight[: experts_here // 2], expert_weight[experts_here // 2 :]]
    _, halves, *shared = lax.optimization_barrier(
        (packed, halves, history_kv, history_bias, tower_inner, tower_outer)
    )
    history, biases, towers, tower_outs = [from_others(values, narrow_count) for values in shared]
    halves = [from_others(values, narrow_count)[1:] for values in halves]
    experts = [expert_weight] + [piece for pieces in zip(*halves) for piece in pieces]
    if blocked:
        prerank_score = prerank(candidates, pre_inner, pre_bias, pre_outer, user_vector, lanes)
    else:
        hidden = jax.nn.relu(
            dot_f32(candidates.reshape(requests * shard_len, features), pre_inner) + pre_bias
        ).astype(jnp.bfloat16)
        embedded = dot_f32(hidden, pre_outer).astype(jnp.bfloat16)
        prerank_score = jnp.einsum(
            "rsd,rd->rs",
            embedded.reshape(requests, shard_len, width),
            user_vector,
            preferred_element_type=jnp.float32,
        )

    results = []
    for g in range(group_size):
        placing, keys, values, vectors, gate_offsets, tower_columns, *loaded = prepare(
            slot_request,
            history_length,
            kept_index,
            history,
            biases,
            tower_outs,
            pre_bias,
            norm_gain,
            gate_bias,
            [pre_inner, pre_outer, query_weight, gate_weight.T, tower_inner],
            shards,
            shard_len,
            half,
            g,
        )
        placing, prerank_score = lax.optimization_barrier((placing, prerank_score))
        results.append(
            rank_slot(
                arrived[g],
                placing,
                keys,
                values,
                vectors,
                gate_offsets,
                tower_columns,
                loaded[:4],
                experts,
                loaded[4:] + towers[1:],
                shards,
                blocked,
            )
        )

    if blocked:
        returned = lax.all_to_all(results[0], both, split_axis=0, concat_axis=0, tiled=True)
        return (prerank_score, unpack_rows(slot_request, back, returned, narrow_count))
    sending = jnp.stack(results).reshape(group_size, tasks, shards, half)
    sending = jnp.transpose(sending, (2, 0, 1, 3)).reshape(shards, -1)
    returned = lax.all_to_all(sending, both, split_axis=0, concat_axis=0, tiled=True)
    returned = returned.reshape(wide_count, narrow_count, group_size, tasks, half)
    returned = jnp.transpose(returned, (0, 2, 3, 1, 4)).reshape(requests, tasks, narrow_count * half)
    request_ids = jnp.arange(requests, dtype=jnp.int32)
    slot_of = jnp.sum(
        jnp.where(slot_request[None, :] == request_ids[:, None], request_ids[None, :], 0), axis=1
    )
    rank_score = jnp.einsum(
        "rcs,rtc->trs",
        picks.astype(jnp.float32),
        returned[slot_of],
        precision=lax.Precision.HIGHEST,
    )
    return (prerank_score, rank_score)


def solution(mesh):
    return jax.shard_map(
        on_device,
        mesh=mesh,
        in_specs=(
            P("groups", ("wide", "narrow"), None),
            P(),
            P(),
            P(),
            P("groups", None),
            P("groups", None),
            P("groups"),
            P(("groups", "wide"), None, None, "narrow"),
            P(("groups", "wide"), "narrow", None),
            P(("groups", "wide")),
            P(),
            P(),
            P("narrow", None, None),
            P(),
            P(),
            P("narrow", None, None),
            P("narrow", None),
        ),
        out_specs=(P("groups", ("wide", "narrow")), P(None, "groups", ("wide", "narrow"))),
        check_vma=False,
    )
```

```python
import functools

import jax
import jax.numpy as jnp
from jax import lax
from jax.experimental import pallas as pl
from jax.experimental.pallas import tpu as pltpu
from jax.sharding import PartitionSpec as P

NT = (((1,), (1,)), ((), ()))
VMEM = pl.BlockSpec(memory_space=pltpu.VMEM)
SMEM = pl.BlockSpec(memory_space=pltpu.SMEM)
ANY = pl.BlockSpec(memory_space=pl.ANY)
VMEM_LIMIT = 16 * 1024 * 1024
LANES = 128
BIAS_ROWS = 8
BRIEF = pl.CostEstimate(flops=1, bytes_accessed=1, transcendentals=0)


def in_hbm(values):
    return pltpu.with_memory_space_constraint(values, pltpu.HBM)


def in_vmem(values):
    return pltpu.with_memory_space_constraint(values, pltpu.VMEM)


def dot_f32(a, b):
    return jnp.dot(a, b, preferred_element_type=jnp.float32)


def dot_nt(a, b):
    return lax.dot_general(a, b, NT, preferred_element_type=jnp.float32)


def split_by(values, divisor):
    if divisor & (divisor - 1) == 0:
        shift = divisor.bit_length() - 1
        return lax.shift_right_logical(values, shift), values & (divisor - 1)
    quotient = lax.div(values, divisor)
    return quotient, values - quotient * divisor


def three_parts(values):
    high = values.astype(jnp.bfloat16)
    rest = values - high.astype(jnp.float32)
    middle = rest.astype(jnp.bfloat16)
    low = (rest - middle.astype(jnp.float32)).astype(jnp.bfloat16)
    return jnp.concatenate([high, middle, low], axis=0)


def sum_parts(stacked, rows):
    return stacked[:rows] + stacked[rows : 2 * rows] + stacked[2 * rows :]


def pack_body(
    narrow_count,
    half,
    slot_hbm,
    kept_hbm,
    cand_hbm,
    out_hbm,
    lane_ref,
    back_ref,
    slot_ref,
    kept_ref,
    cand_ref,
    out_ref,
    sems,
):
    requests, shard_len, _ = cand_ref.shape
    kept_count = kept_ref.shape[1]
    kept_copy = pltpu.make_async_copy(kept_hbm, kept_ref, sems.at[0])
    cand_copy = pltpu.make_async_copy(cand_hbm, cand_ref, sems.at[1])
    slot_copy = pltpu.make_async_copy(slot_hbm, slot_ref, sems.at[2])
    for copy in (kept_copy, slot_copy, cand_copy):
        copy.start()
    device = lax.axis_index("wide") * narrow_count + lax.axis_index("narrow")
    base = device * shard_len
    ids = base + lax.broadcasted_iota(jnp.int32, (shard_len, kept_count), 0)
    request_rows = lax.broadcasted_iota(jnp.int32, (requests, kept_count), 0)
    kept_copy.wait()
    flags = jnp.zeros((requests, shard_len), jnp.float32)
    for r in range(requests):
        hits = jnp.where(kept_ref[r : r + 1, :] == ids, 1.0, 0.0).astype(jnp.bfloat16)
        row = jnp.where(request_rows == r, 1.0, 0.0).astype(jnp.bfloat16)
        flags = flags + dot_nt(row, hits)
    earlier = lax.broadcasted_iota(jnp.int32, (shard_len, shard_len), 0) < lax.broadcasted_iota(
        jnp.int32, (shard_len, shard_len), 1
    )
    places = dot_f32(
        flags.astype(jnp.bfloat16), jnp.where(earlier, 1.0, 0.0).astype(jnp.bfloat16)
    ).astype(jnp.int32)
    before = jnp.sum((kept_ref[...] < base).astype(jnp.int32), axis=1, keepdims=True)
    _, owner = split_by(before + places, narrow_count)
    within, _ = split_by(places, narrow_count)
    kept_here = flags > 0.5
    lane_ref[...] = jnp.where(kept_here, owner * half + within, -1)
    offset = lax.rem(device * half, LANES)
    back_ref[...] = jnp.where(kept_here, owner * LANES + offset + within, -1)
    rows = narrow_count * half
    row_at = lax.broadcasted_iota(jnp.int32, (rows, shard_len), 0)
    slot_copy.wait()
    cand_copy.wait()
    sends = []
    for s in range(requests):
        r = slot_ref[s]
        pick = jnp.where(lane_ref[pl.ds(r, 1), :] == row_at, 1.0, 0.0).astype(jnp.bfloat16)
        out_ref[s * rows : (s + 1) * rows, :] = dot_f32(pick, cand_ref[r]).astype(jnp.bfloat16)
        part = pl.ds(s * rows, rows)
        sends.append(pltpu.make_async_copy(out_ref.at[part], out_hbm.at[part], sems.at[3 + s]))
        sends[s].start()
    for send in sends:
        send.wait()


def pack_rows(slot_request, kept_index, candidates, narrow_count, half):
    requests, shard_len, features = candidates.shape
    rows = requests * narrow_count * half
    return pl.pallas_call(
        functools.partial(pack_body, narrow_count, half),
        out_shape=(
            pltpu.HBM((rows, features), jnp.bfloat16),
            jax.ShapeDtypeStruct((requests, shard_len), jnp.int32),
            jax.ShapeDtypeStruct((requests, shard_len), jnp.int32),
        ),
        in_specs=[ANY, ANY, ANY],
        out_specs=(ANY, VMEM, VMEM),
        scratch_shapes=[
            pltpu.SMEM(slot_request.shape, jnp.int32),
            pltpu.VMEM(kept_index.shape, jnp.int32),
            pltpu.VMEM((requests, shard_len, features), jnp.bfloat16),
            pltpu.VMEM((rows, features), jnp.bfloat16),
            pltpu.SemaphoreType.DMA((3 + requests,)),
        ],
        compiler_params=pltpu.CompilerParams(vmem_limit_bytes=VMEM_LIMIT),
        cost_estimate=pl.CostEstimate(
            flops=2 * rows * shard_len * features, bytes_accessed=4 * rows * features, transcendentals=0
        ),
        name="pack_rows",
    )(in_hbm(slot_request), in_hbm(kept_index), in_hbm(candidates))


def prerank_body(shard_len, cand_ref, inner_ref, bias_ref, outer_ref, user_ref, lane_ref, out_ref):
    requests = user_ref.shape[0]
    step = 2 if requests % 2 == 0 else 1
    for r in range(0, requests, step):
        rows = cand_ref[r * shard_len : (r + step) * shard_len, :]
        hidden = jnp.maximum(dot_f32(rows, inner_ref[...]) + bias_ref[...], 0.0).astype(jnp.bfloat16)
        embedded = dot_f32(hidden, outer_ref[...]).astype(jnp.bfloat16)
        scores = dot_nt(user_ref[...], embedded)
        for i in range(step):
            out_ref[r + i : r + i + 1, :] = scores[r + i : r + i + 1, i * shard_len : (i + 1) * shard_len]


def prerank(candidates, pre_inner, pre_bias, pre_outer, user_vector, lanes):
    requests, shard_len, features = candidates.shape
    rows = requests * shard_len
    return pl.pallas_call(
        functools.partial(prerank_body, shard_len),
        out_shape=jax.ShapeDtypeStruct((requests, shard_len), jnp.float32),
        in_specs=[VMEM] * 6,
        out_specs=VMEM,
        compiler_params=pltpu.CompilerParams(vmem_limit_bytes=VMEM_LIMIT),
        cost_estimate=BRIEF,
        name="prerank",
    )(
        candidates.reshape(rows, features),
        pre_inner,
        pre_bias.reshape(1, -1),
        pre_outer,
        user_vector,
        lanes,
    )


def prepare_body(narrow_count, weight_count, shards, shard_len, slot_at, slot_ref, length_ref, kept_ref, *rest):
    history_refs = rest[:narrow_count]
    bias_refs = rest[narrow_count : 2 * narrow_count]
    tower_outer_refs = rest[2 * narrow_count : 3 * narrow_count]
    pre_bias_ref, gain_ref, gate_bias_ref = rest[3 * narrow_count : 3 * narrow_count + 3]
    rest = rest[3 * narrow_count + 3 :]
    weight_refs = rest[:weight_count]
    placing_ref, keys_hbm, values_hbm, vectors_ref, gate_offsets_ref, tower_columns_ref = rest[weight_count:][:6]
    loaded_refs = rest[weight_count + 6 : -4]
    keys_ref, values_ref, head_sems, sems = rest[-4:]
    copies = [
        pltpu.make_async_copy(source, loaded, sems.at[i])
        for i, (source, loaded) in enumerate(zip(weight_refs, loaded_refs))
    ]
    for copy in copies:
        copy.start()
    group_size, _, span, head_columns = history_refs[0].shape
    heads_here = bias_refs[0].shape[1]
    rows, rows_in = placing_ref.shape
    half = rows_in // shards
    me = lax.axis_index("narrow")
    request = slot_ref[lax.axis_index("wide") * group_size + slot_at]

    vectors_ref[0:1, :] = pre_bias_ref[...]
    vectors_ref[1:2, :] = gain_ref[...]
    tasks, experts = gate_bias_ref.shape
    gate_lane = lax.broadcasted_iota(jnp.int32, (tasks * experts, experts), 1)
    _, gate_row = split_by(lax.broadcasted_iota(jnp.int32, (tasks * experts, experts), 0), experts)
    offsets = jnp.broadcast_to(gate_bias_ref[...][:, None, :], (tasks, experts, experts))
    offsets = jnp.where(gate_row == gate_lane, offsets.reshape(tasks * experts, experts), 0.0)
    gate_offsets_ref[...] = jnp.broadcast_to(jnp.sum(offsets, axis=1, keepdims=True), gate_offsets_ref.shape)
    tasks_here, tower_width = tower_outer_refs[0].shape
    column = lax.broadcasted_iota(jnp.int32, (tower_width, LANES), 1)
    for i in range(narrow_count):
        outer = jnp.transpose(tower_outer_refs[i][...].astype(jnp.float32))
        for t in range(tasks_here):
            task = lax.rem(me + i, narrow_count) * tasks_here + t
            tower_columns_ref[i * tasks_here + t] = jnp.where(
                column == task, outer[:, t : t + 1], 0.0
            ).astype(jnp.bfloat16)

    kept_row = kept_ref[pl.ds(request, 1), :]
    edge = lax.broadcasted_iota(jnp.int32, (shards, kept_row.shape[1]), 0) * shard_len
    starts = jnp.sum((kept_row < edge).astype(jnp.int32), axis=1, keepdims=True)
    ends = jnp.sum((kept_row < edge + shard_len).astype(jnp.int32), axis=1, keepdims=True)
    first, _ = split_by(starts + (narrow_count - 1) - me, narrow_count)
    last, _ = split_by(ends + (narrow_count - 1) - me, narrow_count)
    lane_source, lane_within = split_by(lax.broadcasted_iota(jnp.int32, (shards, rows_in), 1), half)
    mine = lane_source == lax.broadcasted_iota(jnp.int32, (shards, rows_in), 0)
    target = jnp.where(mine & (first + lane_within < last), first + lane_within + 1, 0)
    target = jnp.sum(target, axis=0, keepdims=True) - 1
    placing_ref[...] = jnp.where(
        target == lax.broadcasted_iota(jnp.int32, (rows, rows_in), 0), 1.0, 0.0
    ).astype(jnp.bfloat16)

    head_size = head_columns // heads_here
    tile = 2 * head_size
    pairs_here = heads_here // 2
    visible = lax.broadcasted_iota(jnp.int32, (1, span), 1) < length_ref[slot_at]
    row = lax.broadcasted_iota(jnp.int32, (BIAS_ROWS, span), 0)
    for i in range(narrow_count):
        for t in range(pairs_here):
            at = i * pairs_here + t
            keys = history_refs[i][slot_at, 0, :, t * tile : (t + 1) * tile]
            keys_ref[at, :tile, :] = jnp.transpose(keys.astype(jnp.float32)).astype(jnp.bfloat16)
            bias = jnp.zeros((BIAS_ROWS, span), jnp.float32)
            for h in range(2):
                head = 2 * t + h
                masked = jnp.where(visible, bias_refs[i][slot_at, head : head + 1, :], -1e30)
                bias = jnp.where(row == h, masked, bias)
            parts = three_parts(bias)
            keys_ref[at, tile:, :] = jnp.concatenate(
                [parts, jnp.zeros((tile - parts.shape[0], span), jnp.bfloat16)], axis=0
            )
            values_ref[at, :, :tile] = history_refs[i][slot_at, 1, :, t * tile : (t + 1) * tile]
            values_ref[at, :, tile:] = jnp.ones((span, tile), jnp.bfloat16)
            for j, (source, target) in enumerate([(keys_ref, keys_hbm), (values_ref, values_hbm)]):
                copies.append(pltpu.make_async_copy(source.at[at], target.at[at], head_sems.at[j, at]))
                copies[-1].start()
    for copy in copies:
        copy.wait()


def prepare(
    slot_request,
    lengths,
    kept_index,
    history,
    biases,
    tower_outer,
    pre_bias,
    norm_gain,
    gate_bias,
    weights,
    shards,
    shard_len,
    half,
    slot_at,
):
    narrow_count = len(history)
    _, _, span, head_columns = history[0].shape
    heads_here = biases[0].shape[1]
    pairs = narrow_count * heads_here // 2
    tile = 2 * head_columns // heads_here
    rows = kept_index.shape[1] // narrow_count
    tasks, experts = gate_bias.shape
    width = norm_gain.shape[0]
    bf16 = jnp.bfloat16
    return pl.pallas_call(
        functools.partial(prepare_body, narrow_count, len(weights), shards, shard_len, slot_at),
        out_shape=(
            pltpu.VMEM((rows, shards * half), bf16),
            pltpu.HBM((pairs, 2 * tile, span), bf16),
            pltpu.HBM((pairs, span, 2 * tile), bf16),
            pltpu.VMEM((8, width), jnp.float32),
            pltpu.VMEM((tasks * experts, LANES), jnp.float32),
            pltpu.VMEM((tasks, tower_outer[0].shape[1], LANES), bf16),
            *[pltpu.VMEM(weight.shape, weight.dtype) for weight in weights],
        ),
        in_specs=[SMEM, SMEM] + [VMEM] * (4 + 3 * narrow_count) + [ANY] * len(weights),
        out_specs=(VMEM, ANY, ANY) + (VMEM,) * (3 + len(weights)),
        scratch_shapes=[
            pltpu.VMEM((pairs, 2 * tile, span), bf16),
            pltpu.VMEM((pairs, span, 2 * tile), bf16),
            pltpu.SemaphoreType.DMA((2, pairs)),
            pltpu.SemaphoreType.DMA((len(weights),)),
        ],
        compiler_params=pltpu.CompilerParams(vmem_limit_bytes=VMEM_LIMIT),
        cost_estimate=BRIEF,
        name="prepare",
    )(
        slot_request,
        lengths,
        kept_index,
        *history,
        *biases,
        *tower_outer,
        pre_bias.reshape(1, -1),
        norm_gain.reshape(1, -1),
        gate_bias,
        *[in_hbm(weight) for weight in weights],
    )


def rank_body(narrow_count, pieces, shards, spread, *rest):
    arrived_hbm, keys_hbm, values_hbm = rest[:3]
    expert_hbm = rest[3 : 3 + pieces]
    rest = rest[3 + pieces :]
    placing_ref, vectors_ref, gate_offsets_ref, tower_columns_ref, inner_ref, outer_ref, query_ref, gate_ref = rest[:8]
    tower_refs = rest[8 : 8 + narrow_count]
    (
        out_ref,
        embed_ref,
        queries_ref,
        attended_ref,
        expert_out_ref,
        gates_ref,
        mixture_ref,
        arrived_ref,
        keys_ref,
        values_ref,
        expert_refs,
        sems,
    ) = rest[8 + narrow_count :]
    arrival = pltpu.make_async_copy(arrived_hbm, arrived_ref, sems.at[0])
    head_copies = [
        pltpu.make_async_copy(keys_hbm, keys_ref, sems.at[1]),
        pltpu.make_async_copy(values_hbm, values_ref, sems.at[2]),
    ]
    expert_copies = []
    for i in range(pieces):
        at = sum(piece.shape[0] for piece in expert_hbm[:i])
        here = expert_refs.at[pl.ds(at, expert_hbm[i].shape[0])]
        expert_copies.append(pltpu.make_async_copy(expert_hbm[i], here, sems.at[3 + i]))
    for copy in [arrival] + head_copies + expert_copies:
        copy.start()

    rows = embed_ref.shape[0]
    half = arrived_ref.shape[0] // shards
    experts = expert_refs.shape[0]
    experts_here = experts // narrow_count
    tasks_here = tower_refs[0].shape[0]
    tasks = narrow_count * tasks_here
    block = rows // experts
    blocks = rows // block
    me = lax.axis_index("narrow")

    arrival.wait()
    packed = dot_f32(placing_ref[...], arrived_ref[...]).astype(jnp.bfloat16)
    hidden = jnp.maximum(dot_f32(packed, inner_ref[...]) + vectors_ref[0:1, :], 0.0).astype(jnp.bfloat16)
    embed = dot_f32(hidden, outer_ref[...]).astype(jnp.bfloat16)
    embed_ref[...] = embed
    queries = dot_f32(embed, query_ref[...]).astype(jnp.bfloat16)
    queries_ref[...] = queries

    tile = keys_ref.shape[1] // 2
    pairs = keys_ref.shape[0]
    scale = (tile // 2) ** (-0.5)
    lane = lax.broadcasted_iota(jnp.int32, (rows, tile), 1)
    left = lane < tile // 2
    _, part = split_by(lane, BIAS_ROWS)
    bias_lanes = lane < 3 * BIAS_ROWS
    ones = [jnp.where(bias_lanes & (part == h), 1.0, 0.0).astype(jnp.bfloat16) for h in range(2)]
    for copy in head_copies:
        copy.wait()
    for pair in range(pairs):
        _, place = split_by(me * (pairs // narrow_count) + pair, pairs)
        columns = pl.ds(pl.multiple_of(place * tile, tile), tile)
        scaled = queries_ref[:, columns].astype(jnp.float32) * scale
        query = [jnp.where(own, scaled, 0.0).astype(jnp.bfloat16) for own in (left, ~left)]
        query = jnp.concatenate([jnp.concatenate([query[h], ones[h]], axis=1) for h in range(2)], axis=0)
        scores = dot_f32(query, keys_ref[pair])
        powers = jnp.exp(scores - jnp.max(scores, axis=1, keepdims=True))
        result = dot_f32(powers.astype(jnp.bfloat16), values_ref[pair])
        result = result[:, :tile] / result[:, tile:]
        attended_ref[:, columns] = jnp.where(left, result[:rows], result[rows:]).astype(jnp.bfloat16)

    mixed_in = embed_ref[...].astype(jnp.float32) + attended_ref[...].astype(jnp.float32)
    normed = (
        mixed_in
        * lax.rsqrt(jnp.mean(mixed_in * mixed_in, axis=1, keepdims=True) + 1e-06)
        * vectors_ref[1:2, :]
    ).astype(jnp.bfloat16)

    logits = dot_nt(gate_ref[...], normed) + gate_offsets_ref[:, 0:1]
    by_task = logits.reshape(tasks, experts, rows)
    gate_pow = jnp.exp(by_task - jnp.max(by_task, axis=1, keepdims=True))
    gate_probs = gate_pow / jnp.sum(gate_pow, axis=1, keepdims=True)
    gates = jnp.transpose(gate_probs.reshape(tasks * experts, rows)).astype(jnp.bfloat16)

    for copy in expert_copies:
        copy.wait()
    for e in range(experts):
        result = jnp.maximum(dot_f32(normed, expert_refs[e]), 0.0).astype(jnp.bfloat16)
        for b in range(blocks):
            expert_out_ref[b, e * block : (e + 1) * block, :] = result[b * block : (b + 1) * block, :]

    gate_at = lax.broadcasted_iota(jnp.int32, (tasks * experts, experts * block), 0)
    column = lax.broadcasted_iota(jnp.int32, (tasks * experts, experts * block), 1)
    column_expert, _ = split_by(column, block)
    _, column_expert = split_by(column_expert + me * experts_here, experts)
    _, row_in_block = split_by(lax.broadcasted_iota(jnp.int32, (rows, experts * block), 0), block)
    _, column_row = split_by(lax.broadcasted_iota(jnp.int32, (rows, experts * block), 1), block)
    diagonal = jnp.where(row_in_block == column_row, 1.0, 0.0).astype(jnp.bfloat16)
    for t in range(tasks):
        _, task = split_by(me * tasks_here + t, tasks)
        expand = jnp.where(gate_at == column_expert + task * experts, 1.0, 0.0).astype(jnp.bfloat16)
        wide = dot_f32(gates, expand).astype(jnp.bfloat16) * diagonal
        for b in range(blocks):
            gates_ref[b, t * block : (t + 1) * block, :] = wide[b * block : (b + 1) * block, :]
    for b in range(blocks):
        mixture = dot_f32(gates_ref[b], expert_out_ref[b]).astype(jnp.bfloat16)
        for t in range(tasks):
            mixture_ref[t, b * block : (b + 1) * block, :] = mixture[t * block : (t + 1) * block, :]

    acts = []
    for i in range(narrow_count):
        for t in range(tasks_here):
            at = i * tasks_here + t
            acts.append(jnp.maximum(dot_f32(mixture_ref[at], tower_refs[i][t]), 0.0).astype(jnp.bfloat16))
    columns = tower_columns_ref[...]
    columns = columns.reshape(columns.shape[0] * columns.shape[1], columns.shape[2])
    logits = dot_f32(jnp.concatenate(acts, axis=1), columns)
    by_task = jnp.transpose(logits)[:tasks]

    returned = sum_parts(dot_f32(three_parts(by_task), placing_ref[...]), tasks)
    if not spread:
        out_ref[...] = returned
        return
    for s in range(shards):
        at = s * half // LANES * LANES
        out_ref[s] = returned[:, at : at + LANES]


def rank_slot(
    arrived, placing, keys, values, vectors, gate_offsets, tower_columns, weights, experts, towers, shards, spread
):
    inner, outer, query, gate_rows = weights
    narrow_count = len(towers)
    rows, rows_in = placing.shape
    width = outer.shape[1]
    tasks = tower_columns.shape[0]
    expert_count = gate_rows.shape[0] // tasks
    expert_width = experts[0].shape[2]
    block = rows // expert_count
    if spread:
        out_shape = jax.ShapeDtypeStruct((shards, tasks, LANES), jnp.float32)
    else:
        out_shape = jax.ShapeDtypeStruct((tasks, rows_in), jnp.float32)
    bf16 = jnp.bfloat16
    flops = 2 * rows * (rows_in * width + 3 * width * width + 2 * expert_count * width * expert_width)
    far = [arrived, keys, values, *experts]
    near = [placing, vectors, gate_offsets, tower_columns, *weights, *towers]
    return pl.pallas_call(
        functools.partial(rank_body, narrow_count, len(experts), shards, spread),
        out_shape=out_shape,
        in_specs=[ANY] * len(far) + [VMEM] * len(near),
        out_specs=VMEM,
        scratch_shapes=[
            pltpu.VMEM((rows, width), bf16),
            pltpu.VMEM((rows, query.shape[1]), bf16),
            pltpu.VMEM((rows, query.shape[1]), bf16),
            pltpu.VMEM((rows // block, expert_count * block, expert_width), bf16),
            pltpu.VMEM((rows // block, tasks * block, expert_count * block), bf16),
            pltpu.VMEM((tasks, rows, expert_width), bf16),
            pltpu.VMEM(arrived.shape, bf16),
            pltpu.VMEM(keys.shape, bf16),
            pltpu.VMEM(values.shape, bf16),
            pltpu.VMEM((expert_count,) + experts[0].shape[1:], bf16),
            pltpu.SemaphoreType.DMA((3 + len(experts),)),
        ],
        compiler_params=pltpu.CompilerParams(vmem_limit_bytes=VMEM_LIMIT),
        cost_estimate=pl.CostEstimate(flops=flops, bytes_accessed=6 * 1024 * 1024, transcendentals=0),
        name="rank_slot",
    )(*[in_hbm(array) for array in far], *[in_vmem(array) for array in near])


def unpack_body(narrow_count, slot_ref, back_ref, returned_ref, out_ref):
    requests, shard_len = back_ref.shape
    _, tasks, lanes = returned_ref.shape
    row_at = lax.broadcasted_iota(jnp.int32, (narrow_count * lanes, shard_len), 0)
    for s in range(requests):
        r = slot_ref[s]
        pieces = [returned_ref[s * narrow_count + i] for i in range(narrow_count)]
        parts = three_parts(jnp.concatenate(pieces, axis=1))
        pick = jnp.where(back_ref[pl.ds(r, 1), :] == row_at, 1.0, 0.0).astype(jnp.bfloat16)
        result = sum_parts(dot_f32(parts, pick), tasks)
        for t in range(tasks):
            out_ref[t, pl.ds(r, 1), :] = result[t : t + 1, :]


def unpack_rows(slot_request, back, returned, narrow_count):
    requests, shard_len = back.shape
    tasks = returned.shape[1]
    return pl.pallas_call(
        functools.partial(unpack_body, narrow_count),
        out_shape=jax.ShapeDtypeStruct((tasks, requests, shard_len), jnp.float32),
        in_specs=[SMEM, VMEM, VMEM],
        out_specs=VMEM,
        compiler_params=pltpu.CompilerParams(vmem_limit_bytes=VMEM_LIMIT),
        name="unpack_rows",
    )(slot_request, back, returned)


def lanes_of(kept_index, device_rank, shard_len, narrow_count, half):
    base = device_rank * shard_len
    ids = base + jnp.arange(shard_len, dtype=jnp.int32)
    flags = jnp.any(kept_index[:, :, None] == ids[None, None, :], axis=1)
    places = jnp.cumsum(flags.astype(jnp.int32), axis=1) - flags.astype(jnp.int32)
    before = jnp.sum((kept_index < base).astype(jnp.int32), axis=1, keepdims=True)
    return jnp.where(flags, (before + places) % narrow_count * half + places // narrow_count, -1)


def from_others(values, narrow_count):
    pieces = [values]
    for shift in range(1, narrow_count):
        steps = [((i + shift) % narrow_count, i) for i in range(narrow_count)]
        pieces.append(lax.ppermute(values, "narrow", steps))
    return pieces


def on_device(
    candidates,
    pre_inner,
    pre_bias,
    pre_outer,
    user_vector,
    kept_index,
    slot_request,
    history_kv,
    history_bias,
    history_length,
    query_weight,
    norm_gain,
    expert_weight,
    gate_weight,
    gate_bias,
    tower_inner,
    tower_outer,
):
    wide_count = lax.axis_size("wide")
    narrow_count = lax.axis_size("narrow")
    shards = wide_count * narrow_count
    wide_rank = lax.axis_index("wide")
    narrow_rank = lax.axis_index("narrow")
    device_rank = wide_rank * narrow_count + narrow_rank
    requests, shard_len, features = candidates.shape
    kept_count = kept_index.shape[1]
    capacity = 2 * kept_count // shards
    half = -(-capacity // narrow_count)
    group_size = history_kv.shape[0]
    tasks = narrow_count * tower_inner.shape[0]
    width = pre_outer.shape[1]
    both = ("wide", "narrow")
    blocked = (
        shard_len % 128 == 0
        and requests % 8 == 0
        and half % 16 == 0
        and LANES % half == 0
        and shards * half % LANES == 0
        and group_size == 1
    )

    if blocked:
        packed, lanes, back = pack_rows(slot_request, kept_index, candidates, narrow_count, half)
    else:
        lanes = lanes_of(kept_index, device_rank, shard_len, narrow_count, half)
        picks = lanes[:, None, :] == jnp.arange(narrow_count * half, dtype=jnp.int32)[None, :, None]
        packed = jnp.einsum(
            "rcs,rsd->rcd", picks.astype(jnp.bfloat16), candidates, preferred_element_type=jnp.float32
        ).astype(jnp.bfloat16)[slot_request]
    packed = packed.reshape(wide_count, group_size, narrow_count, half, features)
    packed = jnp.swapaxes(packed, 1, 2).reshape(shards, group_size * half, features)
    arrived = lax.all_to_all(packed, both, split_axis=0, concat_axis=0, tiled=True)
    arrived = jnp.swapaxes(arrived.reshape(shards, group_size, half, features), 0, 1)
    arrived = arrived.reshape(group_size, shards * half, features)

    experts_here = expert_weight.shape[0]
    halves = [expert_weight[: experts_here // 2], expert_weight[experts_here // 2 :]]
    _, halves, *shared = lax.optimization_barrier(
        (packed, halves, history_kv, history_bias, tower_inner, tower_outer)
    )
    history, biases, towers, tower_outs = [from_others(values, narrow_count) for values in shared]
    halves = [from_others(values, narrow_count)[1:] for values in halves]
    experts = [expert_weight] + [piece for pieces in zip(*halves) for piece in pieces]
    if blocked:
        prerank_score = prerank(candidates, pre_inner, pre_bias, pre_outer, user_vector, lanes)
    else:
        hidden = jax.nn.relu(
            dot_f32(candidates.reshape(requests * shard_len, features), pre_inner) + pre_bias
        ).astype(jnp.bfloat16)
        embedded = dot_f32(hidden, pre_outer).astype(jnp.bfloat16)
        prerank_score = jnp.einsum(
            "rsd,rd->rs",
            embedded.reshape(requests, shard_len, width),
            user_vector,
            preferred_element_type=jnp.float32,
        )

    results = []
    for g in range(group_size):
        placing, keys, values, vectors, gate_offsets, tower_columns, *loaded = prepare(
            slot_request,
            history_length,
            kept_index,
            history,
            biases,
            tower_outs,
            pre_bias,
            norm_gain,
            gate_bias,
            [pre_inner, pre_outer, query_weight, gate_weight.T, tower_inner],
            shards,
            shard_len,
            half,
            g,
        )
        placing, prerank_score = lax.optimization_barrier((placing, prerank_score))
        results.append(
            rank_slot(
                arrived[g],
                placing,
                keys,
                values,
                vectors,
                gate_offsets,
                tower_columns,
                loaded[:4],
                experts,
                loaded[4:] + towers[1:],
                shards,
                blocked,
            )
        )

    if blocked:
        returned = lax.all_to_all(results[0], both, split_axis=0, concat_axis=0, tiled=True)
        return (prerank_score, unpack_rows(slot_request, back, returned, narrow_count))
    sending = jnp.stack(results).reshape(group_size, tasks, shards, half)
    sending = jnp.transpose(sending, (2, 0, 1, 3)).reshape(shards, -1)
    returned = lax.all_to_all(sending, both, split_axis=0, concat_axis=0, tiled=True)
    returned = returned.reshape(wide_count, narrow_count, group_size, tasks, half)
    returned = jnp.transpose(returned, (0, 2, 3, 1, 4)).reshape(requests, tasks, narrow_count * half)
    request_ids = jnp.arange(requests, dtype=jnp.int32)
    slot_of = jnp.sum(
        jnp.where(slot_request[None, :] == request_ids[:, None], request_ids[None, :], 0), axis=1
    )
    rank_score = jnp.einsum(
        "rcs,rtc->trs",
        picks.astype(jnp.float32),
        returned[slot_of],
        precision=lax.Precision.HIGHEST,
    )
    return (prerank_score, rank_score)


def solution(mesh):
    return jax.shard_map(
        on_device,
        mesh=mesh,
        in_specs=(
            P("groups", ("wide", "narrow"), None),
            P(),
            P(),
            P(),
            P("groups", None),
            P("groups", None),
            P("groups"),
            P(("groups", "wide"), None, None, "narrow"),
            P(("groups", "wide"), "narrow", None),
            P(("groups", "wide")),
            P(),
            P(),
            P("narrow", None, None),
            P(),
            P(),
            P("narrow", None, None),
            P("narrow", None),
        ),
        out_specs=(P("groups", ("wide", "narrow")), P(None, "groups", ("wide", "narrow"))),
        check_vma=False,
    )
```

```python
import functools

import jax
import jax.numpy as jnp
from jax import lax
from jax.experimental import pallas as pl
from jax.experimental.pallas import tpu as pltpu
from jax.sharding import PartitionSpec as P

NT = (((1,), (1,)), ((), ()))
VMEM = pl.BlockSpec(memory_space=pltpu.VMEM)
SMEM = pl.BlockSpec(memory_space=pltpu.SMEM)
ANY = pl.BlockSpec(memory_space=pl.ANY)
VMEM_LIMIT = 16 * 1024 * 1024
LANES = 128
BIAS_ROWS = 8
BRIEF = pl.CostEstimate(flops=1, bytes_accessed=1, transcendentals=0)


def in_hbm(values):
    return pltpu.with_memory_space_constraint(values, pltpu.HBM)


def in_vmem(values):
    return pltpu.with_memory_space_constraint(values, pltpu.VMEM)


def dot_f32(a, b):
    return jnp.dot(a, b, preferred_element_type=jnp.float32)


def dot_nt(a, b):
    return lax.dot_general(a, b, NT, preferred_element_type=jnp.float32)


def split_by(values, divisor):
    if divisor & (divisor - 1) == 0:
        shift = divisor.bit_length() - 1
        return lax.shift_right_logical(values, shift), values & (divisor - 1)
    quotient = lax.div(values, divisor)
    return quotient, values - quotient * divisor


def three_parts(values):
    high = values.astype(jnp.bfloat16)
    rest = values - high.astype(jnp.float32)
    middle = rest.astype(jnp.bfloat16)
    low = (rest - middle.astype(jnp.float32)).astype(jnp.bfloat16)
    return jnp.concatenate([high, middle, low], axis=0)


def sum_parts(stacked, rows):
    return stacked[:rows] + stacked[rows : 2 * rows] + stacked[2 * rows :]


def pack_body(
    narrow_count,
    half,
    slot_hbm,
    kept_hbm,
    cand_hbm,
    out_hbm,
    lane_ref,
    back_ref,
    order_ref,
    slot_ref,
    kept_ref,
    cand_ref,
    out_ref,
    sems,
):
    requests, shard_len, _ = cand_ref.shape
    kept_count = kept_ref.shape[1]
    kept_copy = pltpu.make_async_copy(kept_hbm, kept_ref, sems.at[0])
    cand_copy = pltpu.make_async_copy(cand_hbm, cand_ref, sems.at[1])
    slot_copy = pltpu.make_async_copy(slot_hbm, slot_ref, sems.at[2])
    for copy in (kept_copy, slot_copy, cand_copy):
        copy.start()
    device = lax.axis_index("wide") * narrow_count + lax.axis_index("narrow")
    base = device * shard_len
    ids = base + lax.broadcasted_iota(jnp.int32, (shard_len, kept_count), 0)
    request_rows = lax.broadcasted_iota(jnp.int32, (requests, kept_count), 0)
    kept_copy.wait()
    flags = jnp.zeros((requests, shard_len), jnp.float32)
    for r in range(requests):
        hits = jnp.where(kept_ref[r : r + 1, :] == ids, 1.0, 0.0).astype(jnp.bfloat16)
        row = jnp.where(request_rows == r, 1.0, 0.0).astype(jnp.bfloat16)
        flags = flags + dot_nt(row, hits)
    earlier = lax.broadcasted_iota(jnp.int32, (shard_len, shard_len), 0) < lax.broadcasted_iota(
        jnp.int32, (shard_len, shard_len), 1
    )
    places = dot_f32(
        flags.astype(jnp.bfloat16), jnp.where(earlier, 1.0, 0.0).astype(jnp.bfloat16)
    ).astype(jnp.int32)
    before = jnp.sum((kept_ref[...] < base).astype(jnp.int32), axis=1, keepdims=True)
    _, owner = split_by(before + places, narrow_count)
    within, _ = split_by(places, narrow_count)
    kept_here = flags > 0.5
    lane_ref[...] = jnp.where(kept_here, owner * half + within, -1)
    offset = lax.rem(device * half, LANES)
    back_ref[...] = jnp.where(kept_here, owner * LANES + offset + within, -1)
    rows = narrow_count * half
    row_at = lax.broadcasted_iota(jnp.int32, (rows, shard_len), 0)
    slot_copy.wait()
    cand_copy.wait()
    sends = []
    for s in range(requests):
        r = slot_ref[s]
        order_ref[s : s + 1, :] = jnp.full((1, LANES), r, jnp.int32)
        pick = jnp.where(lane_ref[pl.ds(r, 1), :] == row_at, 1.0, 0.0).astype(jnp.bfloat16)
        out_ref[s * rows : (s + 1) * rows, :] = dot_f32(pick, cand_ref[r]).astype(jnp.bfloat16)
        part = pl.ds(s * rows, rows)
        sends.append(pltpu.make_async_copy(out_ref.at[part], out_hbm.at[part], sems.at[3 + s]))
        sends[s].start()
    for send in sends:
        send.wait()


def pack_rows(slot_request, kept_index, candidates, narrow_count, half):
    requests, shard_len, features = candidates.shape
    rows = requests * narrow_count * half
    return pl.pallas_call(
        functools.partial(pack_body, narrow_count, half),
        out_shape=(
            pltpu.HBM((rows, features), jnp.bfloat16),
            jax.ShapeDtypeStruct((requests, shard_len), jnp.int32),
            jax.ShapeDtypeStruct((requests, shard_len), jnp.int32),
            jax.ShapeDtypeStruct((requests, LANES), jnp.int32),
        ),
        in_specs=[ANY, ANY, ANY],
        out_specs=(ANY, VMEM, VMEM, VMEM),
        scratch_shapes=[
            pltpu.SMEM(slot_request.shape, jnp.int32),
            pltpu.VMEM(kept_index.shape, jnp.int32),
            pltpu.VMEM((requests, shard_len, features), jnp.bfloat16),
            pltpu.VMEM((rows, features), jnp.bfloat16),
            pltpu.SemaphoreType.DMA((3 + requests,)),
        ],
        compiler_params=pltpu.CompilerParams(vmem_limit_bytes=VMEM_LIMIT),
        cost_estimate=pl.CostEstimate(
            flops=2 * rows * shard_len * features, bytes_accessed=4 * rows * features, transcendentals=0
        ),
        name="pack_rows",
    )(in_hbm(slot_request), in_hbm(kept_index), in_hbm(candidates))


def prerank_body(shard_len, cand_ref, inner_ref, bias_ref, outer_ref, user_ref, lane_ref, out_ref):
    requests = user_ref.shape[0]
    step = 2 if requests % 2 == 0 else 1
    for r in range(0, requests, step):
        rows = cand_ref[r * shard_len : (r + step) * shard_len, :]
        hidden = jnp.maximum(dot_f32(rows, inner_ref[...]) + bias_ref[...], 0.0).astype(jnp.bfloat16)
        embedded = dot_f32(hidden, outer_ref[...]).astype(jnp.bfloat16)
        scores = dot_nt(user_ref[...], embedded)
        for i in range(step):
            out_ref[r + i : r + i + 1, :] = scores[r + i : r + i + 1, i * shard_len : (i + 1) * shard_len]


def prerank(candidates, pre_inner, pre_bias, pre_outer, user_vector, lanes):
    requests, shard_len, features = candidates.shape
    rows = requests * shard_len
    return pl.pallas_call(
        functools.partial(prerank_body, shard_len),
        out_shape=jax.ShapeDtypeStruct((requests, shard_len), jnp.float32),
        in_specs=[VMEM] * 6,
        out_specs=VMEM,
        compiler_params=pltpu.CompilerParams(vmem_limit_bytes=VMEM_LIMIT),
        cost_estimate=BRIEF,
        name="prerank",
    )(
        candidates.reshape(rows, features),
        pre_inner,
        pre_bias.reshape(1, -1),
        pre_outer,
        user_vector,
        lanes,
    )


def prepare_body(narrow_count, weight_count, shards, shard_len, slot_at, slot_ref, length_ref, kept_ref, *rest):
    history_refs = rest[:narrow_count]
    bias_refs = rest[narrow_count : 2 * narrow_count]
    tower_outer_refs = rest[2 * narrow_count : 3 * narrow_count]
    pre_bias_ref, gain_ref, gate_bias_ref = rest[3 * narrow_count : 3 * narrow_count + 3]
    rest = rest[3 * narrow_count + 3 :]
    weight_refs = rest[:weight_count]
    target_ref, keys_ref, values_ref, vectors_ref, gate_offsets_ref, tower_rows_ref = rest[weight_count:][:6]
    loaded_refs = rest[weight_count + 6 : -1]
    sems = rest[-1]
    copies = [
        pltpu.make_async_copy(source, loaded, sems.at[i])
        for i, (source, loaded) in enumerate(zip(weight_refs, loaded_refs))
    ]
    for copy in copies:
        copy.start()
    group_size, _, span, head_columns = history_refs[0].shape
    heads_here = bias_refs[0].shape[1]
    rows_in = target_ref.shape[1]
    half = rows_in // shards
    me = lax.axis_index("narrow")
    request = slot_ref[lax.axis_index("wide") * group_size + slot_at]

    vectors_ref[0:1, :] = pre_bias_ref[...]
    vectors_ref[1:2, :] = gain_ref[...]
    tasks, experts = gate_bias_ref.shape
    gate_lane = lax.broadcasted_iota(jnp.int32, (tasks * experts, experts), 1)
    _, gate_row = split_by(lax.broadcasted_iota(jnp.int32, (tasks * experts, experts), 0), experts)
    offsets = jnp.broadcast_to(gate_bias_ref[...][:, None, :], (tasks, experts, experts))
    offsets = jnp.where(gate_row == gate_lane, offsets.reshape(tasks * experts, experts), 0.0)
    gate_offsets_ref[...] = jnp.broadcast_to(jnp.sum(offsets, axis=1, keepdims=True), gate_offsets_ref.shape)
    tasks_here, tower_width = tower_outer_refs[0].shape
    row = lax.broadcasted_iota(jnp.int32, (tasks, tower_width), 0)
    for i in range(narrow_count):
        for t in range(tasks_here):
            task = lax.rem(me + i, narrow_count) * tasks_here + t
            outer = tower_outer_refs[i][t : t + 1, :].astype(jnp.float32)
            at = (i * tasks_here + t) * tower_width
            tower_rows_ref[:, at : at + tower_width] = jnp.where(row == task, outer, 0.0).astype(jnp.bfloat16)

    kept_row = kept_ref[pl.ds(request, 1), :]
    edge = lax.broadcasted_iota(jnp.int32, (shards, kept_row.shape[1]), 0) * shard_len
    starts = jnp.sum((kept_row < edge).astype(jnp.int32), axis=1, keepdims=True)
    ends = jnp.sum((kept_row < edge + shard_len).astype(jnp.int32), axis=1, keepdims=True)
    first, _ = split_by(starts + (narrow_count - 1) - me, narrow_count)
    last, _ = split_by(ends + (narrow_count - 1) - me, narrow_count)
    lane_source, lane_within = split_by(lax.broadcasted_iota(jnp.int32, (shards, rows_in), 1), half)
    mine = lane_source == lax.broadcasted_iota(jnp.int32, (shards, rows_in), 0)
    target = jnp.where(mine & (first + lane_within < last), first + lane_within + 1, 0)
    target = jnp.sum(target, axis=0, keepdims=True) - 1
    target_ref[...] = jnp.broadcast_to(target, target_ref.shape)

    head_size = head_columns // heads_here
    tile = 2 * head_size
    pairs_here = heads_here // 2
    visible = lax.broadcasted_iota(jnp.int32, (1, span), 1) < length_ref[slot_at]
    row = lax.broadcasted_iota(jnp.int32, (BIAS_ROWS, span), 0)
    for i in range(narrow_count):
        for t in range(pairs_here):
            at = i * pairs_here + t
            keys = history_refs[i][slot_at, 0, :, t * tile : (t + 1) * tile]
            keys_ref[at, :tile, :] = jnp.transpose(keys.astype(jnp.float32)).astype(jnp.bfloat16)
            bias = jnp.zeros((BIAS_ROWS, span), jnp.float32)
            for h in range(2):
                head = 2 * t + h
                masked = jnp.where(visible, bias_refs[i][slot_at, head : head + 1, :], -1e30)
                bias = jnp.where(row == h, masked, bias)
            parts = three_parts(bias)
            keys_ref[at, tile:, :] = jnp.concatenate(
                [parts, jnp.zeros((BIAS_ROWS, span), jnp.bfloat16)], axis=0
            )
            values_ref[at] = history_refs[i][slot_at, 1, :, t * tile : (t + 1) * tile]
    for copy in copies:
        copy.wait()


def prepare(
    slot_request,
    lengths,
    kept_index,
    history,
    biases,
    tower_outer,
    pre_bias,
    norm_gain,
    gate_bias,
    weights,
    shards,
    shard_len,
    half,
    slot_at,
):
    narrow_count = len(history)
    _, _, span, head_columns = history[0].shape
    heads_here = biases[0].shape[1]
    pairs = narrow_count * heads_here // 2
    tile = 2 * head_columns // heads_here
    tasks, experts = gate_bias.shape
    width = norm_gain.shape[0]
    bf16 = jnp.bfloat16
    return pl.pallas_call(
        functools.partial(prepare_body, narrow_count, len(weights), shards, shard_len, slot_at),
        out_shape=(
            pltpu.VMEM((8, shards * half), jnp.int32),
            pltpu.VMEM((pairs, tile + 4 * BIAS_ROWS, span), bf16),
            pltpu.VMEM((pairs, span, tile), bf16),
            pltpu.VMEM((8, width), jnp.float32),
            pltpu.VMEM((tasks * experts, LANES), jnp.float32),
            pltpu.VMEM((tasks, tasks * tower_outer[0].shape[1]), bf16),
            *[pltpu.VMEM(weight.shape, weight.dtype) for weight in weights],
        ),
        in_specs=[SMEM, SMEM] + [VMEM] * (4 + 3 * narrow_count) + [ANY] * len(weights),
        out_specs=(VMEM,) * (6 + len(weights)),
        scratch_shapes=[
            pltpu.SemaphoreType.DMA((len(weights),)),
        ],
        compiler_params=pltpu.CompilerParams(vmem_limit_bytes=VMEM_LIMIT),
        cost_estimate=BRIEF,
        name="prepare",
    )(
        slot_request,
        lengths,
        kept_index,
        *history,
        *biases,
        *tower_outer,
        pre_bias.reshape(1, -1),
        norm_gain.reshape(1, -1),
        gate_bias,
        *[in_hbm(weight) for weight in weights],
    )


def rank_body(narrow_count, pieces, shards, spread, *rest):
    expert_hbm = rest[:pieces]
    tower_hbm = rest[pieces : pieces + narrow_count]
    rest = rest[pieces + narrow_count :]
    arrived_ref, target_ref, vectors_ref, gate_offsets_ref, tower_rows_ref, keys_ref, values_ref = rest[:7]
    inner_ref, outer_ref, query_ref, gate_ref = rest[7:11]
    (
        out_ref,
        embed_ref,
        queries_ref,
        attended_ref,
        expert_out_ref,
        gates_ref,
        mixture_ref,
        expert_refs,
        tower_refs,
        sems,
    ) = rest[11:]
    for i in range(pieces):
        at = sum(piece.shape[0] for piece in expert_hbm[:i])
        here = expert_refs.at[pl.ds(at, expert_hbm[i].shape[0])]
        pltpu.make_async_copy(expert_hbm[i], here, sems.at[0]).start()
    for i in range(narrow_count):
        pltpu.make_async_copy(tower_hbm[i], tower_refs.at[i], sems.at[1]).start()

    rows = embed_ref.shape[0]
    half = arrived_ref.shape[0] // shards
    experts = expert_refs.shape[0]
    experts_here = experts // narrow_count
    tasks_here = tower_refs.shape[1]
    tasks = narrow_count * tasks_here
    block = rows // experts
    blocks = rows // block
    me = lax.axis_index("narrow")

    here = lax.broadcasted_iota(jnp.int32, (rows, target_ref.shape[1]), 0)
    placing = jnp.where(target_ref[0:1, :] == here, 1.0, 0.0).astype(jnp.bfloat16)
    packed = dot_f32(placing, arrived_ref[...]).astype(jnp.bfloat16)
    hidden = jnp.maximum(dot_f32(packed, inner_ref[...]) + vectors_ref[0:1, :], 0.0).astype(jnp.bfloat16)
    embed = dot_f32(hidden, outer_ref[...]).astype(jnp.bfloat16)
    embed_ref[...] = embed
    queries = dot_f32(embed, query_ref[...]).astype(jnp.bfloat16)
    queries_ref[...] = queries

    tile = values_ref.shape[2]
    pairs = keys_ref.shape[0]
    scale = (tile // 2) ** (-0.5)
    left = lax.broadcasted_iota(jnp.int32, (rows, tile), 1) < tile // 2
    lane = lax.broadcasted_iota(jnp.int32, (rows, 4 * BIAS_ROWS), 1)
    _, part = split_by(lane, BIAS_ROWS)
    bias_lanes = lane < 3 * BIAS_ROWS
    ones = [jnp.where(bias_lanes & (part == h), 1.0, 0.0).astype(jnp.bfloat16) for h in range(2)]
    sum_columns = jnp.ones(values_ref.shape[1:], jnp.bfloat16)
    for pair in range(pairs):
        _, place = split_by(me * (pairs // narrow_count) + pair, pairs)
        columns = pl.ds(pl.multiple_of(place * tile, tile), tile)
        scaled = queries_ref[:, columns].astype(jnp.float32) * scale
        query = [jnp.where(own, scaled, 0.0).astype(jnp.bfloat16) for own in (left, ~left)]
        query = jnp.concatenate([jnp.concatenate([query[h], ones[h]], axis=1) for h in range(2)], axis=0)
        scores = dot_f32(query, keys_ref[pair])
        powers = jnp.exp(scores - jnp.max(scores, axis=1, keepdims=True))
        values = jnp.concatenate([values_ref[pair], sum_columns], axis=1)
        result = dot_f32(powers.astype(jnp.bfloat16), values)
        merged = jnp.where(left, result[:rows, :tile], result[rows:, :tile])
        sums = jnp.where(left, result[:rows, tile:], result[rows:, tile:])
        attended_ref[:, columns] = (merged / sums).astype(jnp.bfloat16)

    pltpu.make_async_copy(expert_refs, expert_refs, sems.at[0]).wait()
    mixed_in = embed_ref[...].astype(jnp.float32) + attended_ref[...].astype(jnp.float32)
    normed = (
        mixed_in
        * lax.rsqrt(jnp.mean(mixed_in * mixed_in, axis=1, keepdims=True) + 1e-06)
        * vectors_ref[1:2, :]
    ).astype(jnp.bfloat16)

    logits = dot_nt(gate_ref[...], normed) + gate_offsets_ref[:, 0:1]
    by_task = logits.reshape(tasks, experts, rows)
    gate_pow = jnp.exp(by_task - jnp.max(by_task, axis=1, keepdims=True))
    gate_probs = gate_pow / jnp.sum(gate_pow, axis=1, keepdims=True)
    gates = jnp.transpose(gate_probs.reshape(tasks * experts, rows)).astype(jnp.bfloat16)

    for e in range(experts):
        result = jnp.maximum(dot_f32(normed, expert_refs[e]), 0.0).astype(jnp.bfloat16)
        for b in range(blocks):
            expert_out_ref[b, e * block : (e + 1) * block, :] = result[b * block : (b + 1) * block, :]

    gate_at = lax.broadcasted_iota(jnp.int32, (tasks * experts, experts * block), 0)
    column = lax.broadcasted_iota(jnp.int32, (tasks * experts, experts * block), 1)
    column_expert, _ = split_by(column, block)
    _, column_expert = split_by(column_expert + me * experts_here, experts)
    _, row_in_block = split_by(lax.broadcasted_iota(jnp.int32, (rows, experts * block), 0), block)
    _, column_row = split_by(lax.broadcasted_iota(jnp.int32, (rows, experts * block), 1), block)
    diagonal = jnp.where(row_in_block == column_row, 1.0, 0.0).astype(jnp.bfloat16)
    for t in range(tasks):
        _, task = split_by(me * tasks_here + t, tasks)
        expand = jnp.where(gate_at == column_expert + task * experts, 1.0, 0.0).astype(jnp.bfloat16)
        wide = dot_f32(gates, expand).astype(jnp.bfloat16) * diagonal
        for b in range(blocks):
            gates_ref[b, t * block : (t + 1) * block, :] = wide[b * block : (b + 1) * block, :]
    for b in range(blocks):
        mixture = dot_f32(gates_ref[b], expert_out_ref[b]).astype(jnp.bfloat16)
        for t in range(tasks):
            mixture_ref[t, b * block : (b + 1) * block, :] = mixture[t * block : (t + 1) * block, :]

    pltpu.make_async_copy(tower_refs, tower_refs, sems.at[1]).wait()
    acts = []
    for i in range(narrow_count):
        for t in range(tasks_here):
            at = i * tasks_here + t
            acts.append(jnp.maximum(dot_f32(mixture_ref[at], tower_refs[i, t]), 0.0).astype(jnp.bfloat16))
    by_task = dot_nt(tower_rows_ref[...], jnp.concatenate(acts, axis=1))

    returned = sum_parts(dot_f32(three_parts(by_task), placing), tasks)
    if not spread:
        out_ref[...] = returned
        return
    for s in range(shards):
        at = s * half // LANES * LANES
        out_ref[s] = returned[:, at : at + LANES]


def rank_slot(
    arrived, target, keys, values, vectors, gate_offsets, tower_rows, weights, experts, towers, rows, shards, spread
):
    inner, outer, query, gate_rows = weights
    narrow_count = len(towers)
    rows_in = arrived.shape[0]
    width = outer.shape[1]
    tasks = tower_rows.shape[0]
    expert_count = gate_rows.shape[0] // tasks
    expert_width = experts[0].shape[2]
    block = rows // expert_count
    if spread:
        out_shape = jax.ShapeDtypeStruct((shards, tasks, LANES), jnp.float32)
    else:
        out_shape = jax.ShapeDtypeStruct((tasks, rows_in), jnp.float32)
    bf16 = jnp.bfloat16
    flops = 2 * rows * (rows_in * width + 3 * width * width + 2 * expert_count * width * expert_width)
    far = [*experts, *towers]
    near = [arrived, target, vectors, gate_offsets, tower_rows, keys, values, *weights]
    return pl.pallas_call(
        functools.partial(rank_body, narrow_count, len(experts), shards, spread),
        out_shape=out_shape,
        in_specs=[ANY] * len(far) + [VMEM] * len(near),
        out_specs=VMEM,
        scratch_shapes=[
            pltpu.VMEM((rows, width), bf16),
            pltpu.VMEM((rows, query.shape[1]), bf16),
            pltpu.VMEM((rows, query.shape[1]), bf16),
            pltpu.VMEM((rows // block, expert_count * block, expert_width), bf16),
            pltpu.VMEM((rows // block, tasks * block, expert_count * block), bf16),
            pltpu.VMEM((tasks, rows, expert_width), bf16),
            pltpu.VMEM((expert_count,) + experts[0].shape[1:], bf16),
            pltpu.VMEM((narrow_count,) + towers[0].shape, bf16),
            pltpu.SemaphoreType.DMA((2,)),
        ],
        compiler_params=pltpu.CompilerParams(vmem_limit_bytes=VMEM_LIMIT),
        cost_estimate=pl.CostEstimate(flops=flops, bytes_accessed=6 * 1024 * 1024, transcendentals=0),
        name="rank_slot",
    )(*[in_hbm(array) for array in far], *[in_vmem(array) for array in near])


def unpack_body(narrow_count, order_ref, back_ref, returned_ref, out_ref):
    requests, shard_len = back_ref.shape
    _, tasks, lanes = returned_ref.shape
    row_at = lax.broadcasted_iota(jnp.int32, (narrow_count * lanes, shard_len), 0)
    request_at = lax.broadcasted_iota(jnp.int32, (requests, shard_len), 0)
    results = [jnp.zeros((requests, shard_len), jnp.float32) for t in range(tasks)]
    for s in range(requests):
        mine = request_at == order_ref[s : s + 1, 0:1]
        back = jnp.sum(jnp.where(mine, back_ref[...], 0), axis=0, keepdims=True)
        pieces = [returned_ref[s * narrow_count + i] for i in range(narrow_count)]
        parts = three_parts(jnp.concatenate(pieces, axis=1))
        pick = jnp.where(back == row_at, 1.0, 0.0).astype(jnp.bfloat16)
        result = sum_parts(dot_f32(parts, pick), tasks)
        for t in range(tasks):
            results[t] = jnp.where(mine, result[t : t + 1, :], results[t])
    for t in range(tasks):
        out_ref[t] = results[t]


def unpack_rows(order, back, returned, narrow_count):
    requests, shard_len = back.shape
    tasks = returned.shape[1]
    return pl.pallas_call(
        functools.partial(unpack_body, narrow_count),
        out_shape=jax.ShapeDtypeStruct((tasks, requests, shard_len), jnp.float32),
        in_specs=[VMEM, VMEM, VMEM],
        out_specs=VMEM,
        compiler_params=pltpu.CompilerParams(vmem_limit_bytes=VMEM_LIMIT),
        name="unpack_rows",
    )(order, back, returned)


def lanes_of(kept_index, device_rank, shard_len, narrow_count, half):
    base = device_rank * shard_len
    ids = base + jnp.arange(shard_len, dtype=jnp.int32)
    flags = jnp.any(kept_index[:, :, None] == ids[None, None, :], axis=1)
    places = jnp.cumsum(flags.astype(jnp.int32), axis=1) - flags.astype(jnp.int32)
    before = jnp.sum((kept_index < base).astype(jnp.int32), axis=1, keepdims=True)
    return jnp.where(flags, (before + places) % narrow_count * half + places // narrow_count, -1)


def from_others(values, narrow_count):
    pieces = [values]
    for shift in range(1, narrow_count):
        steps = [((i + shift) % narrow_count, i) for i in range(narrow_count)]
        pieces.append(lax.ppermute(values, "narrow", steps))
    return pieces


def on_device(
    candidates,
    pre_inner,
    pre_bias,
    pre_outer,
    user_vector,
    kept_index,
    slot_request,
    history_kv,
    history_bias,
    history_length,
    query_weight,
    norm_gain,
    expert_weight,
    gate_weight,
    gate_bias,
    tower_inner,
    tower_outer,
):
    wide_count = lax.axis_size("wide")
    narrow_count = lax.axis_size("narrow")
    shards = wide_count * narrow_count
    wide_rank = lax.axis_index("wide")
    narrow_rank = lax.axis_index("narrow")
    device_rank = wide_rank * narrow_count + narrow_rank
    requests, shard_len, features = candidates.shape
    kept_count = kept_index.shape[1]
    capacity = 2 * kept_count // shards
    half = -(-capacity // narrow_count)
    group_size = history_kv.shape[0]
    tasks = narrow_count * tower_inner.shape[0]
    width = pre_outer.shape[1]
    both = ("wide", "narrow")
    blocked = (
        shard_len % 128 == 0
        and requests % 8 == 0
        and half % 16 == 0
        and LANES % half == 0
        and shards * half % LANES == 0
        and group_size == 1
    )

    if blocked:
        packed, lanes, back, order = pack_rows(slot_request, kept_index, candidates, narrow_count, half)
    else:
        lanes = lanes_of(kept_index, device_rank, shard_len, narrow_count, half)
        picks = lanes[:, None, :] == jnp.arange(narrow_count * half, dtype=jnp.int32)[None, :, None]
        packed = jnp.einsum(
            "rcs,rsd->rcd", picks.astype(jnp.bfloat16), candidates, preferred_element_type=jnp.float32
        ).astype(jnp.bfloat16)[slot_request]
    packed = packed.reshape(wide_count, group_size, narrow_count, half, features)
    packed = jnp.swapaxes(packed, 1, 2).reshape(shards, group_size * half, features)
    arrived = lax.all_to_all(packed, both, split_axis=0, concat_axis=0, tiled=True)
    arrived = jnp.swapaxes(arrived.reshape(shards, group_size, half, features), 0, 1)
    arrived = arrived.reshape(group_size, shards * half, features)

    experts_here = expert_weight.shape[0]
    halves = [expert_weight[: experts_here // 2], expert_weight[experts_here // 2 :]]
    _, halves, *shared = lax.optimization_barrier(
        (packed, halves, history_kv, history_bias, tower_inner, tower_outer)
    )
    history, biases, towers, tower_outs = [from_others(values, narrow_count) for values in shared]
    halves = [from_others(values, narrow_count)[1:] for values in halves]
    experts = [expert_weight] + [piece for pieces in zip(*halves) for piece in pieces]
    if blocked:
        prerank_score = prerank(candidates, pre_inner, pre_bias, pre_outer, user_vector, lanes)
    else:
        hidden = jax.nn.relu(
            dot_f32(candidates.reshape(requests * shard_len, features), pre_inner) + pre_bias
        ).astype(jnp.bfloat16)
        embedded = dot_f32(hidden, pre_outer).astype(jnp.bfloat16)
        prerank_score = jnp.einsum(
            "rsd,rd->rs",
            embedded.reshape(requests, shard_len, width),
            user_vector,
            preferred_element_type=jnp.float32,
        )

    results = []
    for g in range(group_size):
        target, keys, values, vectors, gate_offsets, tower_rows, *loaded = prepare(
            slot_request,
            history_length,
            kept_index,
            history,
            biases,
            tower_outs,
            pre_bias,
            norm_gain,
            gate_bias,
            [pre_inner, pre_outer, query_weight, gate_weight.T],
            shards,
            shard_len,
            half,
            g,
        )
        target, prerank_score = lax.optimization_barrier((target, prerank_score))
        results.append(
            rank_slot(
                arrived[g],
                target,
                keys,
                values,
                vectors,
                gate_offsets,
                tower_rows,
                loaded,
                experts,
                towers,
                kept_count // narrow_count,
                shards,
                blocked,
            )
        )

    if blocked:
        returned = lax.all_to_all(results[0], both, split_axis=0, concat_axis=0, tiled=True)
        return (prerank_score, unpack_rows(order, back, returned, narrow_count))
    sending = jnp.stack(results).reshape(group_size, tasks, shards, half)
    sending = jnp.transpose(sending, (2, 0, 1, 3)).reshape(shards, -1)
    returned = lax.all_to_all(sending, both, split_axis=0, concat_axis=0, tiled=True)
    returned = returned.reshape(wide_count, narrow_count, group_size, tasks, half)
    returned = jnp.transpose(returned, (0, 2, 3, 1, 4)).reshape(requests, tasks, narrow_count * half)
    request_ids = jnp.arange(requests, dtype=jnp.int32)
    slot_of = jnp.sum(
        jnp.where(slot_request[None, :] == request_ids[:, None], request_ids[None, :], 0), axis=1
    )
    rank_score = jnp.einsum(
        "rcs,rtc->trs",
        picks.astype(jnp.float32),
        returned[slot_of],
        precision=lax.Precision.HIGHEST,
    )
    return (prerank_score, rank_score)


def solution(mesh):
    return jax.shard_map(
        on_device,
        mesh=mesh,
        in_specs=(
            P("groups", ("wide", "narrow"), None),
            P(),
            P(),
            P(),
            P("groups", None),
            P("groups", None),
            P("groups"),
            P(("groups", "wide"), None, None, "narrow"),
            P(("groups", "wide"), "narrow", None),
            P(("groups", "wide")),
            P(),
            P(),
            P("narrow", None, None),
            P(),
            P(),
            P("narrow", None, None),
            P("narrow", None),
        ),
        out_specs=(P("groups", ("wide", "narrow")), P(None, "groups", ("wide", "narrow"))),
        check_vma=False,
    )
```

```python
import functools

import jax
import jax.numpy as jnp
from jax import lax
from jax.experimental import pallas as pl
from jax.experimental.pallas import tpu as pltpu
from jax.sharding import PartitionSpec as P

NT = (((1,), (1,)), ((), ()))
VMEM = pl.BlockSpec(memory_space=pltpu.VMEM)
SMEM = pl.BlockSpec(memory_space=pltpu.SMEM)
ANY = pl.BlockSpec(memory_space=pl.ANY)
VMEM_LIMIT = 16 * 1024 * 1024
LANES = 128
BIAS_ROWS = 8
BRIEF = pl.CostEstimate(flops=1, bytes_accessed=1, transcendentals=0)


def in_hbm(values):
    return pltpu.with_memory_space_constraint(values, pltpu.HBM)


def in_vmem(values):
    return pltpu.with_memory_space_constraint(values, pltpu.VMEM)


def dot_f32(a, b):
    return jnp.dot(a, b, preferred_element_type=jnp.float32)


def dot_nt(a, b):
    return lax.dot_general(a, b, NT, preferred_element_type=jnp.float32)


def split_by(values, divisor):
    if divisor & (divisor - 1) == 0:
        shift = divisor.bit_length() - 1
        return lax.shift_right_logical(values, shift), values & (divisor - 1)
    quotient = lax.div(values, divisor)
    return quotient, values - quotient * divisor


def three_parts(values):
    high = values.astype(jnp.bfloat16)
    rest = values - high.astype(jnp.float32)
    middle = rest.astype(jnp.bfloat16)
    low = (rest - middle.astype(jnp.float32)).astype(jnp.bfloat16)
    return jnp.concatenate([high, middle, low], axis=0)


def sum_parts(stacked, rows):
    return stacked[:rows] + stacked[rows : 2 * rows] + stacked[2 * rows :]


def pack_body(
    narrow_count,
    half,
    slot_hbm,
    kept_hbm,
    cand_hbm,
    out_hbm,
    lane_ref,
    back_ref,
    order_ref,
    slot_ref,
    kept_ref,
    cand_ref,
    out_ref,
    sems,
):
    requests, shard_len, _ = cand_ref.shape
    kept_count = kept_ref.shape[1]
    kept_copy = pltpu.make_async_copy(kept_hbm, kept_ref, sems.at[0])
    cand_copy = pltpu.make_async_copy(cand_hbm, cand_ref, sems.at[1])
    slot_copy = pltpu.make_async_copy(slot_hbm, slot_ref, sems.at[2])
    for copy in (kept_copy, slot_copy, cand_copy):
        copy.start()
    device = lax.axis_index("wide") * narrow_count + lax.axis_index("narrow")
    base = device * shard_len
    ids = base + lax.broadcasted_iota(jnp.int32, (shard_len, kept_count), 0)
    request_rows = lax.broadcasted_iota(jnp.int32, (requests, kept_count), 0)
    kept_copy.wait()
    flags = jnp.zeros((requests, shard_len), jnp.float32)
    for r in range(requests):
        hits = jnp.where(kept_ref[r : r + 1, :] == ids, 1.0, 0.0).astype(jnp.bfloat16)
        row = jnp.where(request_rows == r, 1.0, 0.0).astype(jnp.bfloat16)
        flags = flags + dot_nt(row, hits)
    earlier = lax.broadcasted_iota(jnp.int32, (shard_len, shard_len), 0) < lax.broadcasted_iota(
        jnp.int32, (shard_len, shard_len), 1
    )
    places = dot_f32(
        flags.astype(jnp.bfloat16), jnp.where(earlier, 1.0, 0.0).astype(jnp.bfloat16)
    ).astype(jnp.int32)
    before = jnp.sum((kept_ref[...] < base).astype(jnp.int32), axis=1, keepdims=True)
    _, owner = split_by(before + places, narrow_count)
    within, _ = split_by(places, narrow_count)
    kept_here = flags > 0.5
    lane_ref[...] = jnp.where(kept_here, owner * half + within, -1)
    offset = lax.rem(device * half, LANES)
    back_ref[...] = jnp.where(kept_here, owner * LANES + offset + within, -1)
    rows = narrow_count * half
    row_at = lax.broadcasted_iota(jnp.int32, (rows, shard_len), 0)
    slot_copy.wait()
    cand_copy.wait()
    zeros = jnp.zeros((rows, shard_len), jnp.bfloat16)
    for s in range(0, requests, 2):
        picks, blocks = [], []
        for i in range(2):
            r = slot_ref[s + i]
            order_ref[s + i : s + i + 1, :] = jnp.full((1, LANES), r, jnp.int32)
            pick = jnp.where(lane_ref[pl.ds(r, 1), :] == row_at, 1.0, 0.0).astype(jnp.bfloat16)
            picks.append(jnp.concatenate([pick, zeros] if i == 0 else [zeros, pick], axis=1))
            blocks.append(cand_ref[r])
        both = dot_f32(jnp.concatenate(picks, axis=0), jnp.concatenate(blocks, axis=0))
        part = pl.ds(s * rows, 2 * rows)
        out_ref[part, :] = both.astype(jnp.bfloat16)
        pltpu.make_async_copy(out_ref.at[part], out_hbm.at[part], sems.at[3]).start()
    pltpu.make_async_copy(out_ref, out_hbm, sems.at[3]).wait()


def pack_rows(slot_request, kept_index, candidates, narrow_count, half):
    requests, shard_len, features = candidates.shape
    rows = requests * narrow_count * half
    return pl.pallas_call(
        functools.partial(pack_body, narrow_count, half),
        out_shape=(
            pltpu.HBM((rows, features), jnp.bfloat16),
            jax.ShapeDtypeStruct((requests, shard_len), jnp.int32),
            jax.ShapeDtypeStruct((requests, shard_len), jnp.int32),
            jax.ShapeDtypeStruct((requests, LANES), jnp.int32),
        ),
        in_specs=[ANY, ANY, ANY],
        out_specs=(ANY, VMEM, VMEM, VMEM),
        scratch_shapes=[
            pltpu.SMEM(slot_request.shape, jnp.int32),
            pltpu.VMEM(kept_index.shape, jnp.int32),
            pltpu.VMEM((requests, shard_len, features), jnp.bfloat16),
            pltpu.VMEM((rows, features), jnp.bfloat16),
            pltpu.SemaphoreType.DMA((4,)),
        ],
        compiler_params=pltpu.CompilerParams(vmem_limit_bytes=VMEM_LIMIT),
        cost_estimate=pl.CostEstimate(
            flops=2 * rows * shard_len * features, bytes_accessed=4 * rows * features, transcendentals=0
        ),
        name="pack_rows",
    )(in_hbm(slot_request), in_hbm(kept_index), in_hbm(candidates))


def prerank_body(shard_len, cand_ref, inner_ref, bias_ref, outer_ref, user_ref, lane_ref, out_ref):
    requests = user_ref.shape[0]
    step = 2 if requests % 2 == 0 else 1
    for r in range(0, requests, step):
        rows = cand_ref[r * shard_len : (r + step) * shard_len, :]
        hidden = jnp.maximum(dot_f32(rows, inner_ref[...]) + bias_ref[...], 0.0).astype(jnp.bfloat16)
        embedded = dot_f32(hidden, outer_ref[...]).astype(jnp.bfloat16)
        scores = dot_nt(user_ref[...], embedded)
        for i in range(step):
            out_ref[r + i : r + i + 1, :] = scores[r + i : r + i + 1, i * shard_len : (i + 1) * shard_len]


def prerank(candidates, pre_inner, pre_bias, pre_outer, user_vector, lanes):
    requests, shard_len, features = candidates.shape
    rows = requests * shard_len
    return pl.pallas_call(
        functools.partial(prerank_body, shard_len),
        out_shape=jax.ShapeDtypeStruct((requests, shard_len), jnp.float32),
        in_specs=[VMEM] * 6,
        out_specs=VMEM,
        compiler_params=pltpu.CompilerParams(vmem_limit_bytes=VMEM_LIMIT),
        cost_estimate=BRIEF,
        name="prerank",
    )(
        candidates.reshape(rows, features),
        pre_inner,
        pre_bias.reshape(1, -1),
        pre_outer,
        user_vector,
        lanes,
    )


def prepare_body(narrow_count, weight_count, shards, shard_len, slot_at, slot_ref, length_ref, kept_ref, *rest):
    history_refs = rest[:narrow_count]
    bias_refs = rest[narrow_count : 2 * narrow_count]
    tower_outer_refs = rest[2 * narrow_count : 3 * narrow_count]
    pre_bias_ref, gain_ref, gate_bias_ref = rest[3 * narrow_count : 3 * narrow_count + 3]
    rest = rest[3 * narrow_count + 3 :]
    weight_refs = rest[:weight_count]
    target_ref, keys_ref, values_ref, vectors_ref, gate_offsets_ref, tower_rows_ref = rest[weight_count:][:6]
    loaded_refs = rest[weight_count + 6 : -1]
    sems = rest[-1]
    copies = [
        pltpu.make_async_copy(source, loaded, sems.at[i])
        for i, (source, loaded) in enumerate(zip(weight_refs, loaded_refs))
    ]
    for copy in copies:
        copy.start()
    group_size, _, span, head_columns = history_refs[0].shape
    heads_here = bias_refs[0].shape[1]
    rows_in = target_ref.shape[1]
    half = rows_in // shards
    me = lax.axis_index("narrow")
    request = slot_ref[lax.axis_index("wide") * group_size + slot_at]

    vectors_ref[0:1, :] = pre_bias_ref[...]
    vectors_ref[1:2, :] = gain_ref[...]
    tasks, experts = gate_bias_ref.shape
    gate_lane = lax.broadcasted_iota(jnp.int32, (tasks * experts, experts), 1)
    _, gate_row = split_by(lax.broadcasted_iota(jnp.int32, (tasks * experts, experts), 0), experts)
    offsets = jnp.broadcast_to(gate_bias_ref[...][:, None, :], (tasks, experts, experts))
    offsets = jnp.where(gate_row == gate_lane, offsets.reshape(tasks * experts, experts), 0.0)
    gate_offsets_ref[...] = jnp.broadcast_to(jnp.sum(offsets, axis=1, keepdims=True), gate_offsets_ref.shape)
    tasks_here, tower_width = tower_outer_refs[0].shape
    row = lax.broadcasted_iota(jnp.int32, (tasks, tower_width), 0)
    for i in range(narrow_count):
        for t in range(tasks_here):
            task = lax.rem(me + i, narrow_count) * tasks_here + t
            outer = tower_outer_refs[i][t : t + 1, :].astype(jnp.float32)
            at = (i * tasks_here + t) * tower_width
            tower_rows_ref[:, at : at + tower_width] = jnp.where(row == task, outer, 0.0).astype(jnp.bfloat16)

    kept_row = kept_ref[pl.ds(request, 1), :]
    edge = lax.broadcasted_iota(jnp.int32, (shards, kept_row.shape[1]), 0) * shard_len
    starts = jnp.sum((kept_row < edge).astype(jnp.int32), axis=1, keepdims=True)
    ends = jnp.sum((kept_row < edge + shard_len).astype(jnp.int32), axis=1, keepdims=True)
    first, _ = split_by(starts + (narrow_count - 1) - me, narrow_count)
    last, _ = split_by(ends + (narrow_count - 1) - me, narrow_count)
    lane_source, lane_within = split_by(lax.broadcasted_iota(jnp.int32, (shards, rows_in), 1), half)
    mine = lane_source == lax.broadcasted_iota(jnp.int32, (shards, rows_in), 0)
    target = jnp.where(mine & (first + lane_within < last), first + lane_within + 1, 0)
    target = jnp.sum(target, axis=0, keepdims=True) - 1
    target_ref[...] = jnp.broadcast_to(target, target_ref.shape)

    head_size = head_columns // heads_here
    tile = 2 * head_size
    pairs_here = heads_here // 2
    visible = lax.broadcasted_iota(jnp.int32, (1, span), 1) < length_ref[slot_at]
    row = lax.broadcasted_iota(jnp.int32, (BIAS_ROWS, span), 0)
    for i in range(narrow_count):
        for t in range(pairs_here):
            at = i * pairs_here + t
            keys = history_refs[i][slot_at, 0, :, t * tile : (t + 1) * tile]
            keys_ref[at, :tile, :] = jnp.transpose(keys.astype(jnp.float32)).astype(jnp.bfloat16)
            bias = jnp.zeros((BIAS_ROWS, span), jnp.float32)
            for h in range(2):
                head = 2 * t + h
                masked = jnp.where(visible, bias_refs[i][slot_at, head : head + 1, :], -1e30)
                bias = jnp.where(row == h, masked, bias)
            parts = three_parts(bias)
            keys_ref[at, tile:, :] = jnp.concatenate(
                [parts, jnp.zeros((BIAS_ROWS, span), jnp.bfloat16)], axis=0
            )
            values_ref[at] = history_refs[i][slot_at, 1, :, t * tile : (t + 1) * tile]
    for copy in copies:
        copy.wait()


def prepare(
    slot_request,
    lengths,
    kept_index,
    history,
    biases,
    tower_outer,
    pre_bias,
    norm_gain,
    gate_bias,
    weights,
    shards,
    shard_len,
    half,
    slot_at,
):
    narrow_count = len(history)
    _, _, span, head_columns = history[0].shape
    heads_here = biases[0].shape[1]
    pairs = narrow_count * heads_here // 2
    tile = 2 * head_columns // heads_here
    tasks, experts = gate_bias.shape
    width = norm_gain.shape[0]
    bf16 = jnp.bfloat16
    return pl.pallas_call(
        functools.partial(prepare_body, narrow_count, len(weights), shards, shard_len, slot_at),
        out_shape=(
            pltpu.VMEM((8, shards * half), jnp.int32),
            pltpu.VMEM((pairs, tile + 4 * BIAS_ROWS, span), bf16),
            pltpu.VMEM((pairs, span, tile), bf16),
            pltpu.VMEM((8, width), jnp.float32),
            pltpu.VMEM((tasks * experts, LANES), jnp.float32),
            pltpu.VMEM((tasks, tasks * tower_outer[0].shape[1]), bf16),
            *[pltpu.VMEM(weight.shape, weight.dtype) for weight in weights],
        ),
        in_specs=[SMEM, SMEM] + [VMEM] * (4 + 3 * narrow_count) + [ANY] * len(weights),
        out_specs=(VMEM,) * (6 + len(weights)),
        scratch_shapes=[
            pltpu.SemaphoreType.DMA((len(weights),)),
        ],
        compiler_params=pltpu.CompilerParams(vmem_limit_bytes=VMEM_LIMIT),
        cost_estimate=BRIEF,
        name="prepare",
    )(
        slot_request,
        lengths,
        kept_index,
        *history,
        *biases,
        *tower_outer,
        pre_bias.reshape(1, -1),
        norm_gain.reshape(1, -1),
        gate_bias,
        *[in_hbm(weight) for weight in weights],
    )


def rank_body(narrow_count, pieces, shards, spread, *rest):
    expert_hbm = rest[:pieces]
    tower_hbm = rest[pieces : pieces + narrow_count]
    rest = rest[pieces + narrow_count :]
    arrived_ref, target_ref, vectors_ref, gate_offsets_ref, tower_rows_ref, keys_ref, values_ref = rest[:7]
    inner_ref, outer_ref, query_ref, gate_ref = rest[7:11]
    (
        out_ref,
        embed_ref,
        queries_ref,
        attended_ref,
        expert_out_ref,
        gates_ref,
        mixture_ref,
        expert_refs,
        tower_refs,
        sems,
    ) = rest[11:]
    own = expert_hbm[0].shape[0]
    own_copy = pltpu.make_async_copy(expert_hbm[0], expert_refs.at[pl.ds(0, own)], sems.at[0])
    own_copy.start()
    late_copies = []
    for i in range(1, pieces):
        at = sum(piece.shape[0] for piece in expert_hbm[:i])
        here = expert_refs.at[pl.ds(at, expert_hbm[i].shape[0])]
        late_copies.append(pltpu.make_async_copy(expert_hbm[i], here, sems.at[1]))
    for i in range(narrow_count):
        late_copies.append(pltpu.make_async_copy(tower_hbm[i], tower_refs.at[i], sems.at[2]))
    for copy in late_copies:
        copy.start()

    rows = embed_ref.shape[0]
    half = arrived_ref.shape[0] // shards
    experts = expert_refs.shape[0]
    experts_here = experts // narrow_count
    tasks_here = tower_refs.shape[1]
    tasks = narrow_count * tasks_here
    block = rows // experts
    blocks = rows // block
    me = lax.axis_index("narrow")

    here = lax.broadcasted_iota(jnp.int32, (rows, target_ref.shape[1]), 0)
    placing = jnp.where(target_ref[0:1, :] == here, 1.0, 0.0).astype(jnp.bfloat16)
    packed = dot_f32(placing, arrived_ref[...]).astype(jnp.bfloat16)
    hidden = jnp.maximum(dot_f32(packed, inner_ref[...]) + vectors_ref[0:1, :], 0.0).astype(jnp.bfloat16)
    embed = dot_f32(hidden, outer_ref[...]).astype(jnp.bfloat16)
    embed_ref[...] = embed
    queries = dot_f32(embed, query_ref[...]).astype(jnp.bfloat16)
    queries_ref[...] = queries

    tile = values_ref.shape[2]
    pairs = keys_ref.shape[0]
    scale = (tile // 2) ** (-0.5)
    left = lax.broadcasted_iota(jnp.int32, (rows, tile), 1) < tile // 2
    lane = lax.broadcasted_iota(jnp.int32, (rows, 4 * BIAS_ROWS), 1)
    _, part = split_by(lane, BIAS_ROWS)
    bias_lanes = lane < 3 * BIAS_ROWS
    ones = [jnp.where(bias_lanes & (part == h), 1.0, 0.0).astype(jnp.bfloat16) for h in range(2)]
    sum_columns = jnp.ones(values_ref.shape[1:], jnp.bfloat16)
    for pair in range(pairs):
        if pair == pairs - 1:
            own_copy.wait()
        _, place = split_by(me * (pairs // narrow_count) + pair, pairs)
        columns = pl.ds(pl.multiple_of(place * tile, tile), tile)
        scaled = queries_ref[:, columns].astype(jnp.float32) * scale
        query = [jnp.where(own, scaled, 0.0).astype(jnp.bfloat16) for own in (left, ~left)]
        query = jnp.concatenate([jnp.concatenate([query[h], ones[h]], axis=1) for h in range(2)], axis=0)
        scores = dot_f32(query, keys_ref[pair])
        powers = jnp.exp(scores - jnp.max(scores, axis=1, keepdims=True))
        values = jnp.concatenate([values_ref[pair], sum_columns], axis=1)
        result = dot_f32(powers.astype(jnp.bfloat16), values)
        merged = jnp.where(left, result[:rows, :tile], result[rows:, :tile])
        sums = jnp.where(left, result[:rows, tile:], result[rows:, tile:])
        attended_ref[:, columns] = (merged / sums).astype(jnp.bfloat16)

    mixed_in = embed_ref[...].astype(jnp.float32) + attended_ref[...].astype(jnp.float32)
    normed = (
        mixed_in
        * lax.rsqrt(jnp.mean(mixed_in * mixed_in, axis=1, keepdims=True) + 1e-06)
        * vectors_ref[1:2, :]
    ).astype(jnp.bfloat16)

    logits = dot_nt(gate_ref[...], normed) + gate_offsets_ref[:, 0:1]
    by_task = logits.reshape(tasks, experts, rows)
    gate_pow = jnp.exp(by_task - jnp.max(by_task, axis=1, keepdims=True))
    gate_probs = gate_pow / jnp.sum(gate_pow, axis=1, keepdims=True)
    gates = jnp.transpose(gate_probs.reshape(tasks * experts, rows)).astype(jnp.bfloat16)

    for e in range(experts):
        if e == own:
            here = expert_refs.at[pl.ds(own, experts - own)]
            pltpu.make_async_copy(here, here, sems.at[1]).wait()
            pltpu.make_async_copy(tower_refs, tower_refs, sems.at[2]).wait()
        result = jnp.maximum(dot_f32(normed, expert_refs[e]), 0.0).astype(jnp.bfloat16)
        for b in range(blocks):
            expert_out_ref[b, e * block : (e + 1) * block, :] = result[b * block : (b + 1) * block, :]

    gate_at = lax.broadcasted_iota(jnp.int32, (tasks * experts, experts * block), 0)
    column = lax.broadcasted_iota(jnp.int32, (tasks * experts, experts * block), 1)
    column_expert, _ = split_by(column, block)
    _, column_expert = split_by(column_expert + me * experts_here, experts)
    _, row_in_block = split_by(lax.broadcasted_iota(jnp.int32, (rows, experts * block), 0), block)
    _, column_row = split_by(lax.broadcasted_iota(jnp.int32, (rows, experts * block), 1), block)
    diagonal = jnp.where(row_in_block == column_row, 1.0, 0.0).astype(jnp.bfloat16)
    for t in range(tasks):
        _, task = split_by(me * tasks_here + t, tasks)
        expand = jnp.where(gate_at == column_expert + task * experts, 1.0, 0.0).astype(jnp.bfloat16)
        wide = dot_f32(gates, expand).astype(jnp.bfloat16) * diagonal
        for b in range(blocks):
            gates_ref[b, t * block : (t + 1) * block, :] = wide[b * block : (b + 1) * block, :]
    for b in range(blocks):
        mixture = dot_f32(gates_ref[b], expert_out_ref[b]).astype(jnp.bfloat16)
        for t in range(tasks):
            mixture_ref[t, b * block : (b + 1) * block, :] = mixture[t * block : (t + 1) * block, :]

    acts = []
    for i in range(narrow_count):
        for t in range(tasks_here):
            at = i * tasks_here + t
            acts.append(jnp.maximum(dot_f32(mixture_ref[at], tower_refs[i, t]), 0.0).astype(jnp.bfloat16))
    by_task = dot_nt(tower_rows_ref[...], jnp.concatenate(acts, axis=1))

    returned = sum_parts(dot_f32(three_parts(by_task), placing), tasks)
    if not spread:
        out_ref[...] = returned
        return
    for s in range(shards):
        at = s * half // LANES * LANES
        out_ref[s] = returned[:, at : at + LANES]


def rank_slot(
    arrived, target, keys, values, vectors, gate_offsets, tower_rows, weights, experts, towers, rows, shards, spread
):
    inner, outer, query, gate_rows = weights
    narrow_count = len(towers)
    rows_in = arrived.shape[0]
    width = outer.shape[1]
    tasks = tower_rows.shape[0]
    expert_count = gate_rows.shape[0] // tasks
    expert_width = experts[0].shape[2]
    block = rows // expert_count
    if spread:
        out_shape = jax.ShapeDtypeStruct((shards, tasks, LANES), jnp.float32)
    else:
        out_shape = jax.ShapeDtypeStruct((tasks, rows_in), jnp.float32)
    bf16 = jnp.bfloat16
    flops = 2 * rows * (rows_in * width + 3 * width * width + 2 * expert_count * width * expert_width)
    far = [*experts, *towers]
    near = [arrived, target, vectors, gate_offsets, tower_rows, keys, values, *weights]
    return pl.pallas_call(
        functools.partial(rank_body, narrow_count, len(experts), shards, spread),
        out_shape=out_shape,
        in_specs=[ANY] * len(far) + [VMEM] * len(near),
        out_specs=VMEM,
        scratch_shapes=[
            pltpu.VMEM((rows, width), bf16),
            pltpu.VMEM((rows, query.shape[1]), bf16),
            pltpu.VMEM((rows, query.shape[1]), bf16),
            pltpu.VMEM((rows // block, expert_count * block, expert_width), bf16),
            pltpu.VMEM((rows // block, tasks * block, expert_count * block), bf16),
            pltpu.VMEM((tasks, rows, expert_width), bf16),
            pltpu.VMEM((expert_count,) + experts[0].shape[1:], bf16),
            pltpu.VMEM((narrow_count,) + towers[0].shape, bf16),
            pltpu.SemaphoreType.DMA((3,)),
        ],
        compiler_params=pltpu.CompilerParams(vmem_limit_bytes=VMEM_LIMIT),
        cost_estimate=pl.CostEstimate(flops=flops, bytes_accessed=6 * 1024 * 1024, transcendentals=0),
        name="rank_slot",
    )(*[in_hbm(array) for array in far], *[in_vmem(array) for array in near])


def unpack_body(narrow_count, order_ref, back_ref, returned_ref, out_ref):
    requests, shard_len = back_ref.shape
    _, tasks, lanes = returned_ref.shape
    row_at = lax.broadcasted_iota(jnp.int32, (narrow_count * lanes, shard_len), 0)
    request_at = lax.broadcasted_iota(jnp.int32, (requests, shard_len), 0)
    results = [jnp.zeros((requests, shard_len), jnp.float32) for t in range(tasks)]
    for s in range(requests):
        mine = request_at == order_ref[s : s + 1, 0:1]
        back = jnp.sum(jnp.where(mine, back_ref[...], 0), axis=0, keepdims=True)
        pieces = [returned_ref[s * narrow_count + i] for i in range(narrow_count)]
        parts = three_parts(jnp.concatenate(pieces, axis=1))
        pick = jnp.where(back == row_at, 1.0, 0.0).astype(jnp.bfloat16)
        result = sum_parts(dot_f32(parts, pick), tasks)
        for t in range(tasks):
            results[t] = jnp.where(mine, result[t : t + 1, :], results[t])
    for t in range(tasks):
        out_ref[t] = results[t]


def unpack_rows(order, back, returned, narrow_count):
    requests, shard_len = back.shape
    tasks = returned.shape[1]
    return pl.pallas_call(
        functools.partial(unpack_body, narrow_count),
        out_shape=jax.ShapeDtypeStruct((tasks, requests, shard_len), jnp.float32),
        in_specs=[VMEM, VMEM, VMEM],
        out_specs=VMEM,
        compiler_params=pltpu.CompilerParams(vmem_limit_bytes=VMEM_LIMIT),
        name="unpack_rows",
    )(order, back, returned)


def lanes_of(kept_index, device_rank, shard_len, narrow_count, half):
    base = device_rank * shard_len
    ids = base + jnp.arange(shard_len, dtype=jnp.int32)
    flags = jnp.any(kept_index[:, :, None] == ids[None, None, :], axis=1)
    places = jnp.cumsum(flags.astype(jnp.int32), axis=1) - flags.astype(jnp.int32)
    before = jnp.sum((kept_index < base).astype(jnp.int32), axis=1, keepdims=True)
    return jnp.where(flags, (before + places) % narrow_count * half + places // narrow_count, -1)


def from_others(values, narrow_count):
    pieces = [values]
    for shift in range(1, narrow_count):
        steps = [((i + shift) % narrow_count, i) for i in range(narrow_count)]
        pieces.append(lax.ppermute(values, "narrow", steps))
    return pieces


def on_device(
    candidates,
    pre_inner,
    pre_bias,
    pre_outer,
    user_vector,
    kept_index,
    slot_request,
    history_kv,
    history_bias,
    history_length,
    query_weight,
    norm_gain,
    expert_weight,
    gate_weight,
    gate_bias,
    tower_inner,
    tower_outer,
):
    wide_count = lax.axis_size("wide")
    narrow_count = lax.axis_size("narrow")
    shards = wide_count * narrow_count
    wide_rank = lax.axis_index("wide")
    narrow_rank = lax.axis_index("narrow")
    device_rank = wide_rank * narrow_count + narrow_rank
    requests, shard_len, features = candidates.shape
    kept_count = kept_index.shape[1]
    capacity = 2 * kept_count // shards
    half = -(-capacity // narrow_count)
    group_size = history_kv.shape[0]
    tasks = narrow_count * tower_inner.shape[0]
    width = pre_outer.shape[1]
    both = ("wide", "narrow")
    blocked = (
        shard_len % 128 == 0
        and requests % 8 == 0
        and half % 16 == 0
        and LANES % half == 0
        and shards * half % LANES == 0
        and group_size == 1
    )

    if blocked:
        packed, lanes, back, order = pack_rows(slot_request, kept_index, candidates, narrow_count, half)
    else:
        lanes = lanes_of(kept_index, device_rank, shard_len, narrow_count, half)
        picks = lanes[:, None, :] == jnp.arange(narrow_count * half, dtype=jnp.int32)[None, :, None]
        packed = jnp.einsum(
            "rcs,rsd->rcd", picks.astype(jnp.bfloat16), candidates, preferred_element_type=jnp.float32
        ).astype(jnp.bfloat16)[slot_request]
    packed = packed.reshape(wide_count, group_size, narrow_count, half, features)
    packed = jnp.swapaxes(packed, 1, 2).reshape(shards, group_size * half, features)
    arrived = lax.all_to_all(packed, both, split_axis=0, concat_axis=0, tiled=True)
    arrived = jnp.swapaxes(arrived.reshape(shards, group_size, half, features), 0, 1)
    arrived = arrived.reshape(group_size, shards * half, features)

    experts_here = expert_weight.shape[0]
    halves = [expert_weight[: experts_here // 2], expert_weight[experts_here // 2 :]]
    _, halves, *shared = lax.optimization_barrier(
        (packed, halves, history_kv, history_bias, tower_inner, tower_outer)
    )
    history, biases, towers, tower_outs = [from_others(values, narrow_count) for values in shared]
    halves = [from_others(values, narrow_count)[1:] for values in halves]
    experts = [expert_weight] + [piece for pieces in zip(*halves) for piece in pieces]
    if blocked:
        prerank_score = prerank(candidates, pre_inner, pre_bias, pre_outer, user_vector, lanes)
    else:
        hidden = jax.nn.relu(
            dot_f32(candidates.reshape(requests * shard_len, features), pre_inner) + pre_bias
        ).astype(jnp.bfloat16)
        embedded = dot_f32(hidden, pre_outer).astype(jnp.bfloat16)
        prerank_score = jnp.einsum(
            "rsd,rd->rs",
            embedded.reshape(requests, shard_len, width),
            user_vector,
            preferred_element_type=jnp.float32,
        )

    results = []
    for g in range(group_size):
        target, keys, values, vectors, gate_offsets, tower_rows, *loaded = prepare(
            slot_request,
            history_length,
            kept_index,
            history,
            biases,
            tower_outs,
            pre_bias,
            norm_gain,
            gate_bias,
            [pre_inner, pre_outer, query_weight, gate_weight.T],
            shards,
            shard_len,
            half,
            g,
        )
        target, prerank_score = lax.optimization_barrier((target, prerank_score))
        results.append(
            rank_slot(
                arrived[g],
                target,
                keys,
                values,
                vectors,
                gate_offsets,
                tower_rows,
                loaded,
                experts,
                towers,
                kept_count // narrow_count,
                shards,
                blocked,
            )
        )

    if blocked:
        returned = lax.all_to_all(results[0], both, split_axis=0, concat_axis=0, tiled=True)
        return (prerank_score, unpack_rows(order, back, returned, narrow_count))
    sending = jnp.stack(results).reshape(group_size, tasks, shards, half)
    sending = jnp.transpose(sending, (2, 0, 1, 3)).reshape(shards, -1)
    returned = lax.all_to_all(sending, both, split_axis=0, concat_axis=0, tiled=True)
    returned = returned.reshape(wide_count, narrow_count, group_size, tasks, half)
    returned = jnp.transpose(returned, (0, 2, 3, 1, 4)).reshape(requests, tasks, narrow_count * half)
    request_ids = jnp.arange(requests, dtype=jnp.int32)
    slot_of = jnp.sum(
        jnp.where(slot_request[None, :] == request_ids[:, None], request_ids[None, :], 0), axis=1
    )
    rank_score = jnp.einsum(
        "rcs,rtc->trs",
        picks.astype(jnp.float32),
        returned[slot_of],
        precision=lax.Precision.HIGHEST,
    )
    return (prerank_score, rank_score)


def solution(mesh):
    return jax.shard_map(
        on_device,
        mesh=mesh,
        in_specs=(
            P("groups", ("wide", "narrow"), None),
            P(),
            P(),
            P(),
            P("groups", None),
            P("groups", None),
            P("groups"),
            P(("groups", "wide"), None, None, "narrow"),
            P(("groups", "wide"), "narrow", None),
            P(("groups", "wide")),
            P(),
            P(),
            P("narrow", None, None),
            P(),
            P(),
            P("narrow", None, None),
            P("narrow", None),
        ),
        out_specs=(P("groups", ("wide", "narrow")), P(None, "groups", ("wide", "narrow"))),
        check_vma=False,
    )
```

```python
import functools

import jax
import jax.numpy as jnp
from jax import lax
from jax.experimental import pallas as pl
from jax.experimental.pallas import tpu as pltpu
from jax.sharding import PartitionSpec as P

NT = (((1,), (1,)), ((), ()))
VMEM = pl.BlockSpec(memory_space=pltpu.VMEM)
SMEM = pl.BlockSpec(memory_space=pltpu.SMEM)
ANY = pl.BlockSpec(memory_space=pl.ANY)
VMEM_LIMIT = 16 * 1024 * 1024
LANES = 128
BIAS_ROWS = 8
BRIEF = pl.CostEstimate(flops=1, bytes_accessed=1, transcendentals=0)


def in_hbm(values):
    return pltpu.with_memory_space_constraint(values, pltpu.HBM)


def in_vmem(values):
    return pltpu.with_memory_space_constraint(values, pltpu.VMEM)


def dot_f32(a, b):
    return jnp.dot(a, b, preferred_element_type=jnp.float32)


def dot_nt(a, b):
    return lax.dot_general(a, b, NT, preferred_element_type=jnp.float32)


def split_by(values, divisor):
    if divisor & (divisor - 1) == 0:
        shift = divisor.bit_length() - 1
        return lax.shift_right_logical(values, shift), values & (divisor - 1)
    quotient = lax.div(values, divisor)
    return quotient, values - quotient * divisor


def three_parts(values):
    high = values.astype(jnp.bfloat16)
    rest = values - high.astype(jnp.float32)
    middle = rest.astype(jnp.bfloat16)
    low = (rest - middle.astype(jnp.float32)).astype(jnp.bfloat16)
    return jnp.concatenate([high, middle, low], axis=0)


def sum_parts(stacked, rows):
    return stacked[:rows] + stacked[rows : 2 * rows] + stacked[2 * rows :]


def pack_body(
    narrow_count,
    half,
    slot_hbm,
    kept_hbm,
    cand_hbm,
    out_hbm,
    lane_ref,
    back_ref,
    order_ref,
    slot_ref,
    kept_ref,
    cand_ref,
    out_ref,
    sems,
):
    requests, shard_len, _ = cand_ref.shape
    kept_count = kept_ref.shape[1]
    kept_copy = pltpu.make_async_copy(kept_hbm, kept_ref, sems.at[0])
    cand_copy = pltpu.make_async_copy(cand_hbm, cand_ref, sems.at[1])
    slot_copy = pltpu.make_async_copy(slot_hbm, slot_ref, sems.at[2])
    for copy in (kept_copy, slot_copy, cand_copy):
        copy.start()
    device = lax.axis_index("wide") * narrow_count + lax.axis_index("narrow")
    base = device * shard_len
    ids = base + lax.broadcasted_iota(jnp.int32, (shard_len, kept_count), 0)
    request_rows = lax.broadcasted_iota(jnp.int32, (requests, kept_count), 0)
    kept_copy.wait()
    flags = jnp.zeros((requests, shard_len), jnp.float32)
    for r in range(requests):
        hits = jnp.where(kept_ref[r : r + 1, :] == ids, 1.0, 0.0).astype(jnp.bfloat16)
        row = jnp.where(request_rows == r, 1.0, 0.0).astype(jnp.bfloat16)
        flags = flags + dot_nt(row, hits)
    earlier = lax.broadcasted_iota(jnp.int32, (shard_len, shard_len), 0) < lax.broadcasted_iota(
        jnp.int32, (shard_len, shard_len), 1
    )
    places = dot_f32(
        flags.astype(jnp.bfloat16), jnp.where(earlier, 1.0, 0.0).astype(jnp.bfloat16)
    ).astype(jnp.int32)
    before = jnp.sum((kept_ref[...] < base).astype(jnp.int32), axis=1, keepdims=True)
    _, owner = split_by(before + places, narrow_count)
    within, _ = split_by(places, narrow_count)
    kept_here = flags > 0.5
    lane_ref[...] = jnp.where(kept_here, owner * half + within, -1)
    offset = lax.rem(device * half, LANES)
    back_ref[...] = jnp.where(kept_here, owner * LANES + offset + within, -1)
    rows = narrow_count * half
    row_at = lax.broadcasted_iota(jnp.int32, (rows, shard_len), 0)
    slot_copy.wait()
    cand_copy.wait()
    zeros = jnp.zeros((rows, shard_len), jnp.bfloat16)
    for s in range(0, requests, 2):
        picks, blocks = [], []
        for i in range(2):
            r = slot_ref[s + i]
            order_ref[s + i : s + i + 1, :] = jnp.full((1, LANES), r, jnp.int32)
            pick = jnp.where(lane_ref[pl.ds(r, 1), :] == row_at, 1.0, 0.0).astype(jnp.bfloat16)
            picks.append(jnp.concatenate([pick, zeros] if i == 0 else [zeros, pick], axis=1))
            blocks.append(cand_ref[r])
        both = dot_f32(jnp.concatenate(picks, axis=0), jnp.concatenate(blocks, axis=0))
        part = pl.ds(s * rows, 2 * rows)
        out_ref[part, :] = both.astype(jnp.bfloat16)
        pltpu.make_async_copy(out_ref.at[part], out_hbm.at[part], sems.at[3]).start()
    pltpu.make_async_copy(out_ref, out_hbm, sems.at[3]).wait()


def pack_rows(slot_request, kept_index, candidates, narrow_count, half):
    requests, shard_len, features = candidates.shape
    rows = requests * narrow_count * half
    return pl.pallas_call(
        functools.partial(pack_body, narrow_count, half),
        out_shape=(
            pltpu.HBM((rows, features), jnp.bfloat16),
            jax.ShapeDtypeStruct((requests, shard_len), jnp.int32),
            jax.ShapeDtypeStruct((requests, shard_len), jnp.int32),
            jax.ShapeDtypeStruct((requests, LANES), jnp.int32),
        ),
        in_specs=[ANY, ANY, ANY],
        out_specs=(ANY, VMEM, VMEM, VMEM),
        scratch_shapes=[
            pltpu.SMEM(slot_request.shape, jnp.int32),
            pltpu.VMEM(kept_index.shape, jnp.int32),
            pltpu.VMEM((requests, shard_len, features), jnp.bfloat16),
            pltpu.VMEM((rows, features), jnp.bfloat16),
            pltpu.SemaphoreType.DMA((4,)),
        ],
        compiler_params=pltpu.CompilerParams(vmem_limit_bytes=VMEM_LIMIT),
        cost_estimate=pl.CostEstimate(
            flops=2 * rows * shard_len * features, bytes_accessed=4 * rows * features, transcendentals=0
        ),
        name="pack_rows",
    )(in_hbm(slot_request), in_hbm(kept_index), in_hbm(candidates))


def prerank_body(shard_len, cand_ref, inner_ref, bias_ref, outer_ref, user_ref, lane_ref, out_ref):
    requests = user_ref.shape[0]
    step = 2 if requests % 2 == 0 else 1
    for r in range(0, requests, step):
        rows = cand_ref[r * shard_len : (r + step) * shard_len, :]
        hidden = jnp.maximum(dot_f32(rows, inner_ref[...]) + bias_ref[...], 0.0).astype(jnp.bfloat16)
        embedded = dot_f32(hidden, outer_ref[...]).astype(jnp.bfloat16)
        scores = dot_nt(user_ref[...], embedded)
        for i in range(step):
            out_ref[r + i : r + i + 1, :] = scores[r + i : r + i + 1, i * shard_len : (i + 1) * shard_len]


def prerank(candidates, pre_inner, pre_bias, pre_outer, user_vector, lanes):
    requests, shard_len, features = candidates.shape
    rows = requests * shard_len
    return pl.pallas_call(
        functools.partial(prerank_body, shard_len),
        out_shape=jax.ShapeDtypeStruct((requests, shard_len), jnp.float32),
        in_specs=[VMEM] * 6,
        out_specs=VMEM,
        compiler_params=pltpu.CompilerParams(vmem_limit_bytes=VMEM_LIMIT),
        cost_estimate=BRIEF,
        name="prerank",
    )(
        candidates.reshape(rows, features),
        pre_inner,
        pre_bias.reshape(1, -1),
        pre_outer,
        user_vector,
        lanes,
    )


def prepare_body(narrow_count, weight_count, shards, shard_len, slot_at, slot_ref, length_ref, kept_ref, *rest):
    history_refs = rest[:narrow_count]
    bias_refs = rest[narrow_count : 2 * narrow_count]
    tower_outer_refs = rest[2 * narrow_count : 3 * narrow_count]
    pre_bias_ref, gain_ref, gate_bias_ref = rest[3 * narrow_count : 3 * narrow_count + 3]
    rest = rest[3 * narrow_count + 3 :]
    weight_refs = rest[:weight_count]
    target_ref, keys_ref, values_ref, vectors_ref, gate_offsets_ref, tower_rows_ref = rest[weight_count:][:6]
    loaded_refs = rest[weight_count + 6 : -1]
    sems = rest[-1]
    copies = [
        pltpu.make_async_copy(source, loaded, sems.at[i])
        for i, (source, loaded) in enumerate(zip(weight_refs, loaded_refs))
    ]
    for copy in copies:
        copy.start()
    group_size, _, span, head_columns = history_refs[0].shape
    heads_here = bias_refs[0].shape[1]
    rows_in = target_ref.shape[1]
    half = rows_in // shards
    me = lax.axis_index("narrow")
    request = slot_ref[lax.axis_index("wide") * group_size + slot_at]

    vectors_ref[0:1, :] = pre_bias_ref[...]
    vectors_ref[1:2, :] = gain_ref[...]
    tasks, experts = gate_bias_ref.shape
    gate_lane = lax.broadcasted_iota(jnp.int32, (tasks * experts, experts), 1)
    _, gate_row = split_by(lax.broadcasted_iota(jnp.int32, (tasks * experts, experts), 0), experts)
    offsets = jnp.broadcast_to(gate_bias_ref[...][:, None, :], (tasks, experts, experts))
    offsets = jnp.where(gate_row == gate_lane, offsets.reshape(tasks * experts, experts), 0.0)
    gate_offsets_ref[...] = jnp.broadcast_to(jnp.sum(offsets, axis=1, keepdims=True), gate_offsets_ref.shape)
    tasks_here, tower_width = tower_outer_refs[0].shape
    row = lax.broadcasted_iota(jnp.int32, (tasks, tower_width), 0)
    for i in range(narrow_count):
        for t in range(tasks_here):
            task = lax.rem(me + i, narrow_count) * tasks_here + t
            outer = tower_outer_refs[i][t : t + 1, :].astype(jnp.float32)
            at = (i * tasks_here + t) * tower_width
            tower_rows_ref[:, at : at + tower_width] = jnp.where(row == task, outer, 0.0).astype(jnp.bfloat16)

    kept_row = kept_ref[pl.ds(request, 1), :]
    edge = lax.broadcasted_iota(jnp.int32, (shards, kept_row.shape[1]), 0) * shard_len
    starts = jnp.sum((kept_row < edge).astype(jnp.int32), axis=1, keepdims=True)
    ends = jnp.sum((kept_row < edge + shard_len).astype(jnp.int32), axis=1, keepdims=True)
    first, _ = split_by(starts + (narrow_count - 1) - me, narrow_count)
    last, _ = split_by(ends + (narrow_count - 1) - me, narrow_count)
    lane_source, lane_within = split_by(lax.broadcasted_iota(jnp.int32, (shards, rows_in), 1), half)
    mine = lane_source == lax.broadcasted_iota(jnp.int32, (shards, rows_in), 0)
    target = jnp.where(mine & (first + lane_within < last), first + lane_within + 1, 0)
    target = jnp.sum(target, axis=0, keepdims=True) - 1
    target_ref[...] = jnp.broadcast_to(target, target_ref.shape)

    head_size = head_columns // heads_here
    tile = 2 * head_size
    pairs_here = heads_here // 2
    visible = lax.broadcasted_iota(jnp.int32, (1, span), 1) < length_ref[slot_at]
    row = lax.broadcasted_iota(jnp.int32, (BIAS_ROWS, span), 0)
    for i in range(narrow_count):
        for t in range(pairs_here):
            at = i * pairs_here + t
            keys = history_refs[i][slot_at, 0, :, t * tile : (t + 1) * tile]
            keys_ref[at, :tile, :] = jnp.transpose(keys.astype(jnp.float32)).astype(jnp.bfloat16)
            bias = jnp.zeros((BIAS_ROWS, span), jnp.float32)
            for h in range(2):
                head = 2 * t + h
                masked = jnp.where(visible, bias_refs[i][slot_at, head : head + 1, :], -1e30)
                bias = jnp.where(row == h, masked, bias)
            parts = three_parts(bias)
            keys_ref[at, tile:, :] = jnp.concatenate(
                [parts, jnp.zeros((BIAS_ROWS, span), jnp.bfloat16)], axis=0
            )
            values_ref[at] = history_refs[i][slot_at, 1, :, t * tile : (t + 1) * tile]
    for copy in copies:
        copy.wait()


def prepare(
    slot_request,
    lengths,
    kept_index,
    history,
    biases,
    tower_outer,
    pre_bias,
    norm_gain,
    gate_bias,
    weights,
    shards,
    shard_len,
    half,
    slot_at,
):
    narrow_count = len(history)
    _, _, span, head_columns = history[0].shape
    heads_here = biases[0].shape[1]
    pairs = narrow_count * heads_here // 2
    tile = 2 * head_columns // heads_here
    tasks, experts = gate_bias.shape
    width = norm_gain.shape[0]
    bf16 = jnp.bfloat16
    return pl.pallas_call(
        functools.partial(prepare_body, narrow_count, len(weights), shards, shard_len, slot_at),
        out_shape=(
            pltpu.VMEM((8, shards * half), jnp.int32),
            pltpu.VMEM((pairs, tile + 4 * BIAS_ROWS, span), bf16),
            pltpu.VMEM((pairs, span, tile), bf16),
            pltpu.VMEM((8, width), jnp.float32),
            pltpu.VMEM((tasks * experts, LANES), jnp.float32),
            pltpu.VMEM((tasks, tasks * tower_outer[0].shape[1]), bf16),
            *[pltpu.VMEM(weight.shape, weight.dtype) for weight in weights],
        ),
        in_specs=[SMEM, SMEM] + [VMEM] * (4 + 3 * narrow_count) + [ANY] * len(weights),
        out_specs=(VMEM,) * (6 + len(weights)),
        scratch_shapes=[
            pltpu.SemaphoreType.DMA((len(weights),)),
        ],
        compiler_params=pltpu.CompilerParams(vmem_limit_bytes=VMEM_LIMIT),
        cost_estimate=BRIEF,
        name="prepare",
    )(
        slot_request,
        lengths,
        kept_index,
        *history,
        *biases,
        *tower_outer,
        pre_bias.reshape(1, -1),
        norm_gain.reshape(1, -1),
        gate_bias,
        *[in_hbm(weight) for weight in weights],
    )


def rank_body(narrow_count, pieces, shards, spread, *rest):
    expert_hbm = rest[:pieces]
    tower_hbm = rest[pieces : pieces + narrow_count]
    rest = rest[pieces + narrow_count :]
    arrived_ref, target_ref, vectors_ref, gate_offsets_ref, tower_rows_ref, keys_ref, values_ref = rest[:7]
    inner_ref, outer_ref, query_ref, gate_ref = rest[7:11]
    (
        out_ref,
        embed_ref,
        queries_ref,
        attended_ref,
        expert_out_ref,
        gates_ref,
        mixture_ref,
        expert_refs,
        tower_refs,
        sems,
    ) = rest[11:]
    own = expert_hbm[0].shape[0]
    own_copy = pltpu.make_async_copy(expert_hbm[0], expert_refs.at[pl.ds(0, own)], sems.at[0])
    own_copy.start()
    late_copies = []
    for i in range(1, pieces):
        at = sum(piece.shape[0] for piece in expert_hbm[:i])
        here = expert_refs.at[pl.ds(at, expert_hbm[i].shape[0])]
        late_copies.append(pltpu.make_async_copy(expert_hbm[i], here, sems.at[1]))
    for i in range(narrow_count):
        late_copies.append(pltpu.make_async_copy(tower_hbm[i], tower_refs.at[i], sems.at[2]))
    for copy in late_copies:
        copy.start()

    rows = embed_ref.shape[0]
    half = arrived_ref.shape[0] // shards
    experts = expert_refs.shape[0]
    experts_here = experts // narrow_count
    tasks_here = tower_refs.shape[1]
    tasks = narrow_count * tasks_here
    block = rows // experts
    blocks = rows // block
    me = lax.axis_index("narrow")

    here = lax.broadcasted_iota(jnp.int32, (rows, target_ref.shape[1]), 0)
    placing = jnp.where(target_ref[0:1, :] == here, 1.0, 0.0).astype(jnp.bfloat16)
    packed = dot_f32(placing, arrived_ref[...]).astype(jnp.bfloat16)
    hidden = jnp.maximum(dot_f32(packed, inner_ref[...]) + vectors_ref[0:1, :], 0.0).astype(jnp.bfloat16)
    embed = dot_f32(hidden, outer_ref[...]).astype(jnp.bfloat16)
    embed_ref[...] = embed
    queries = dot_f32(embed, query_ref[...]).astype(jnp.bfloat16)
    queries_ref[...] = queries

    tile = values_ref.shape[2]
    pairs = keys_ref.shape[0]
    scale = (tile // 2) ** (-0.5)
    left = lax.broadcasted_iota(jnp.int32, (rows, tile), 1) < tile // 2
    lane = lax.broadcasted_iota(jnp.int32, (rows, 4 * BIAS_ROWS), 1)
    _, part = split_by(lane, BIAS_ROWS)
    bias_lanes = lane < 3 * BIAS_ROWS
    ones = [jnp.where(bias_lanes & (part == h), 1.0, 0.0).astype(jnp.bfloat16) for h in range(2)]
    sum_columns = jnp.ones(values_ref.shape[1:], jnp.bfloat16)
    for pair in range(pairs):
        if pair == pairs - 1:
            own_copy.wait()
        _, place = split_by(me * (pairs // narrow_count) + pair, pairs)
        columns = pl.ds(pl.multiple_of(place * tile, tile), tile)
        scaled = queries_ref[:, columns].astype(jnp.float32) * scale
        query = [jnp.where(own, scaled, 0.0).astype(jnp.bfloat16) for own in (left, ~left)]
        query = jnp.concatenate([jnp.concatenate([query[h], ones[h]], axis=1) for h in range(2)], axis=0)
        scores = dot_f32(query, keys_ref[pair])
        powers = jnp.exp(scores - jnp.max(scores, axis=1, keepdims=True))
        values = jnp.concatenate([values_ref[pair], sum_columns], axis=1)
        result = dot_f32(powers.astype(jnp.bfloat16), values)
        merged = jnp.where(left, result[:rows, :tile], result[rows:, :tile])
        sums = jnp.where(left, result[:rows, tile:], result[rows:, tile:])
        attended_ref[:, columns] = (merged / sums).astype(jnp.bfloat16)

    mixed_in = embed_ref[...].astype(jnp.float32) + attended_ref[...].astype(jnp.float32)
    normed = (
        mixed_in
        * lax.rsqrt(jnp.mean(mixed_in * mixed_in, axis=1, keepdims=True) + 1e-06)
        * vectors_ref[1:2, :]
    ).astype(jnp.bfloat16)

    logits = dot_nt(gate_ref[...], normed) + gate_offsets_ref[:, 0:1]
    by_task = logits.reshape(tasks, experts, rows)
    gate_pow = jnp.exp(by_task - jnp.max(by_task, axis=1, keepdims=True))
    gate_probs = gate_pow / jnp.sum(gate_pow, axis=1, keepdims=True)
    gates = jnp.transpose(gate_probs.reshape(tasks * experts, rows)).astype(jnp.bfloat16)

    for e in range(experts):
        if e == own:
            here = expert_refs.at[pl.ds(own, experts - own)]
            pltpu.make_async_copy(here, here, sems.at[1]).wait()
            pltpu.make_async_copy(tower_refs, tower_refs, sems.at[2]).wait()
        result = jnp.maximum(dot_f32(normed, expert_refs[e]), 0.0).astype(jnp.bfloat16)
        for b in range(blocks):
            expert_out_ref[b, e * block : (e + 1) * block, :] = result[b * block : (b + 1) * block, :]

    gate_at = lax.broadcasted_iota(jnp.int32, (tasks * experts, experts * block), 0)
    column = lax.broadcasted_iota(jnp.int32, (tasks * experts, experts * block), 1)
    column_expert, _ = split_by(column, block)
    _, column_expert = split_by(column_expert + me * experts_here, experts)
    _, row_in_block = split_by(lax.broadcasted_iota(jnp.int32, (rows, experts * block), 0), block)
    _, column_row = split_by(lax.broadcasted_iota(jnp.int32, (rows, experts * block), 1), block)
    diagonal = jnp.where(row_in_block == column_row, 1.0, 0.0).astype(jnp.bfloat16)
    for t in range(tasks):
        _, task = split_by(me * tasks_here + t, tasks)
        expand = jnp.where(gate_at == column_expert + task * experts, 1.0, 0.0).astype(jnp.bfloat16)
        wide = dot_f32(gates, expand).astype(jnp.bfloat16) * diagonal
        for b in range(blocks):
            gates_ref[b, t * block : (t + 1) * block, :] = wide[b * block : (b + 1) * block, :]
    for b in range(blocks):
        mixture = dot_f32(gates_ref[b], expert_out_ref[b]).astype(jnp.bfloat16)
        for t in range(tasks):
            mixture_ref[t, b * block : (b + 1) * block, :] = mixture[t * block : (t + 1) * block, :]

    acts = []
    for i in range(narrow_count):
        for t in range(tasks_here):
            at = i * tasks_here + t
            acts.append(jnp.maximum(dot_f32(mixture_ref[at], tower_refs[i, t]), 0.0).astype(jnp.bfloat16))
    by_task = dot_nt(tower_rows_ref[...], jnp.concatenate(acts, axis=1))

    returned = sum_parts(dot_f32(three_parts(by_task), placing), tasks)
    if not spread:
        out_ref[...] = returned
        return
    rows_out = tasks // 2
    low = lax.broadcasted_iota(jnp.int32, (rows_out, LANES), 1) < LANES // 2
    for first in range(0, shards, LANES // half):
        values = returned[:, first * half : first * half + LANES]
        near, far = values[:rows_out], pltpu.roll(values, LANES // 2, 1)[rows_out:]
        for i in range(LANES // half):
            mixed = jnp.where(low, near, far) if 2 * i * half < LANES else jnp.where(low, far, near)
            out_ref[(first + i) * rows_out : (first + i + 1) * rows_out, :] = mixed


def rank_slot(
    arrived, target, keys, values, vectors, gate_offsets, tower_rows, weights, experts, towers, rows, shards, spread
):
    inner, outer, query, gate_rows = weights
    narrow_count = len(towers)
    rows_in = arrived.shape[0]
    width = outer.shape[1]
    tasks = tower_rows.shape[0]
    expert_count = gate_rows.shape[0] // tasks
    expert_width = experts[0].shape[2]
    block = rows // expert_count
    if spread:
        out_shape = jax.ShapeDtypeStruct((shards * tasks // 2, LANES), jnp.float32)
    else:
        out_shape = jax.ShapeDtypeStruct((tasks, rows_in), jnp.float32)
    bf16 = jnp.bfloat16
    flops = 2 * rows * (rows_in * width + 3 * width * width + 2 * expert_count * width * expert_width)
    far = [*experts, *towers]
    near = [arrived, target, vectors, gate_offsets, tower_rows, keys, values, *weights]
    return pl.pallas_call(
        functools.partial(rank_body, narrow_count, len(experts), shards, spread),
        out_shape=out_shape,
        in_specs=[ANY] * len(far) + [VMEM] * len(near),
        out_specs=VMEM,
        scratch_shapes=[
            pltpu.VMEM((rows, width), bf16),
            pltpu.VMEM((rows, query.shape[1]), bf16),
            pltpu.VMEM((rows, query.shape[1]), bf16),
            pltpu.VMEM((rows // block, expert_count * block, expert_width), bf16),
            pltpu.VMEM((rows // block, tasks * block, expert_count * block), bf16),
            pltpu.VMEM((tasks, rows, expert_width), bf16),
            pltpu.VMEM((expert_count,) + experts[0].shape[1:], bf16),
            pltpu.VMEM((narrow_count,) + towers[0].shape, bf16),
            pltpu.SemaphoreType.DMA((3,)),
        ],
        compiler_params=pltpu.CompilerParams(vmem_limit_bytes=VMEM_LIMIT),
        cost_estimate=pl.CostEstimate(flops=flops, bytes_accessed=6 * 1024 * 1024, transcendentals=0),
        name="rank_slot",
    )(*[in_hbm(array) for array in far], *[in_vmem(array) for array in near])


def unpack_body(narrow_count, order_ref, back_ref, returned_ref, out_ref):
    requests, shard_len = back_ref.shape
    tasks = out_ref.shape[0]
    half_tasks = tasks // 2
    rows = narrow_count * half_tasks
    lanes = returned_ref.shape[1]
    lane_at = lax.broadcasted_iota(jnp.int32, (lanes, shard_len), 0)
    request_at = lax.broadcasted_iota(jnp.int32, (requests, shard_len), 0)
    results = [jnp.zeros((requests, shard_len), jnp.float32) for t in range(tasks)]
    for s in range(requests):
        mine = request_at == order_ref[s : s + 1, 0:1]
        back = jnp.sum(jnp.where(mine, back_ref[...], 0), axis=0, keepdims=True)
        picks = [
            jnp.where(back == lane_at + i * lanes, 1.0, 0.0).astype(jnp.bfloat16) for i in range(narrow_count)
        ]
        near = returned_ref[s * rows : (s + 1) * rows, :]
        parts = three_parts(jnp.concatenate([near, pltpu.roll(near, lanes // 2, 1)], axis=0))
        result = sum_parts(dot_f32(parts, jnp.concatenate(picks, axis=1)), 2 * rows)
        for t in range(tasks):
            at = t // half_tasks * rows + t % half_tasks
            value = result[at : at + 1, :shard_len]
            for i in range(1, narrow_count):
                row = at + i * half_tasks
                value = value + result[row : row + 1, i * shard_len : (i + 1) * shard_len]
            results[t] = jnp.where(mine, value, results[t])
    for t in range(tasks):
        out_ref[t] = results[t]


def unpack_rows(order, back, returned, tasks, narrow_count):
    requests, shard_len = back.shape
    return pl.pallas_call(
        functools.partial(unpack_body, narrow_count),
        out_shape=jax.ShapeDtypeStruct((tasks, requests, shard_len), jnp.float32),
        in_specs=[VMEM, VMEM, VMEM],
        out_specs=VMEM,
        compiler_params=pltpu.CompilerParams(vmem_limit_bytes=VMEM_LIMIT),
        name="unpack_rows",
    )(order, back, returned)


def lanes_of(kept_index, device_rank, shard_len, narrow_count, half):
    base = device_rank * shard_len
    ids = base + jnp.arange(shard_len, dtype=jnp.int32)
    flags = jnp.any(kept_index[:, :, None] == ids[None, None, :], axis=1)
    places = jnp.cumsum(flags.astype(jnp.int32), axis=1) - flags.astype(jnp.int32)
    before = jnp.sum((kept_index < base).astype(jnp.int32), axis=1, keepdims=True)
    return jnp.where(flags, (before + places) % narrow_count * half + places // narrow_count, -1)


def from_others(values, narrow_count):
    pieces = [values]
    for shift in range(1, narrow_count):
        steps = [((i + shift) % narrow_count, i) for i in range(narrow_count)]
        pieces.append(lax.ppermute(values, "narrow", steps))
    return pieces


def on_device(
    candidates,
    pre_inner,
    pre_bias,
    pre_outer,
    user_vector,
    kept_index,
    slot_request,
    history_kv,
    history_bias,
    history_length,
    query_weight,
    norm_gain,
    expert_weight,
    gate_weight,
    gate_bias,
    tower_inner,
    tower_outer,
):
    wide_count = lax.axis_size("wide")
    narrow_count = lax.axis_size("narrow")
    shards = wide_count * narrow_count
    wide_rank = lax.axis_index("wide")
    narrow_rank = lax.axis_index("narrow")
    device_rank = wide_rank * narrow_count + narrow_rank
    requests, shard_len, features = candidates.shape
    kept_count = kept_index.shape[1]
    capacity = 2 * kept_count // shards
    half = -(-capacity // narrow_count)
    group_size = history_kv.shape[0]
    tasks = narrow_count * tower_inner.shape[0]
    width = pre_outer.shape[1]
    both = ("wide", "narrow")
    blocked = (
        shard_len % 128 == 0
        and requests % 8 == 0
        and half % 16 == 0
        and LANES % (2 * half) == 0
        and tasks % 2 == 0
        and narrow_count * tasks // 2 % 8 == 0
        and shards * half % LANES == 0
        and group_size == 1
    )

    if blocked:
        packed, lanes, back, order = pack_rows(slot_request, kept_index, candidates, narrow_count, half)
    else:
        lanes = lanes_of(kept_index, device_rank, shard_len, narrow_count, half)
        picks = lanes[:, None, :] == jnp.arange(narrow_count * half, dtype=jnp.int32)[None, :, None]
        packed = jnp.einsum(
            "rcs,rsd->rcd", picks.astype(jnp.bfloat16), candidates, preferred_element_type=jnp.float32
        ).astype(jnp.bfloat16)[slot_request]
    packed = packed.reshape(wide_count, group_size, narrow_count, half, features)
    packed = jnp.swapaxes(packed, 1, 2).reshape(shards, group_size * half, features)
    arrived = lax.all_to_all(packed, both, split_axis=0, concat_axis=0, tiled=True)
    arrived = jnp.swapaxes(arrived.reshape(shards, group_size, half, features), 0, 1)
    arrived = arrived.reshape(group_size, shards * half, features)

    experts_here = expert_weight.shape[0]
    halves = [expert_weight[: experts_here // 2], expert_weight[experts_here // 2 :]]
    _, halves, *shared = lax.optimization_barrier(
        (packed, halves, history_kv, history_bias, tower_inner, tower_outer)
    )
    history, biases, towers, tower_outs = [from_others(values, narrow_count) for values in shared]
    halves = [from_others(values, narrow_count)[1:] for values in halves]
    experts = [expert_weight] + [piece for pieces in zip(*halves) for piece in pieces]
    if blocked:
        prerank_score = prerank(candidates, pre_inner, pre_bias, pre_outer, user_vector, lanes)
    else:
        hidden = jax.nn.relu(
            dot_f32(candidates.reshape(requests * shard_len, features), pre_inner) + pre_bias
        ).astype(jnp.bfloat16)
        embedded = dot_f32(hidden, pre_outer).astype(jnp.bfloat16)
        prerank_score = jnp.einsum(
            "rsd,rd->rs",
            embedded.reshape(requests, shard_len, width),
            user_vector,
            preferred_element_type=jnp.float32,
        )

    results = []
    for g in range(group_size):
        target, keys, values, vectors, gate_offsets, tower_rows, *loaded = prepare(
            slot_request,
            history_length,
            kept_index,
            history,
            biases,
            tower_outs,
            pre_bias,
            norm_gain,
            gate_bias,
            [pre_inner, pre_outer, query_weight, gate_weight.T],
            shards,
            shard_len,
            half,
            g,
        )
        target, prerank_score = lax.optimization_barrier((target, prerank_score))
        results.append(
            rank_slot(
                arrived[g],
                target,
                keys,
                values,
                vectors,
                gate_offsets,
                tower_rows,
                loaded,
                experts,
                towers,
                kept_count // narrow_count,
                shards,
                blocked,
            )
        )

    if blocked:
        sending = results[0].reshape(shards, tasks // 2, LANES)
        returned = lax.all_to_all(sending, both, split_axis=0, concat_axis=0, tiled=True)
        returned = returned.reshape(shards * tasks // 2, LANES)
        return (prerank_score, unpack_rows(order, back, returned, tasks, narrow_count))
    sending = jnp.stack(results).reshape(group_size, tasks, shards, half)
    sending = jnp.transpose(sending, (2, 0, 1, 3)).reshape(shards, -1)
    returned = lax.all_to_all(sending, both, split_axis=0, concat_axis=0, tiled=True)
    returned = returned.reshape(wide_count, narrow_count, group_size, tasks, half)
    returned = jnp.transpose(returned, (0, 2, 3, 1, 4)).reshape(requests, tasks, narrow_count * half)
    request_ids = jnp.arange(requests, dtype=jnp.int32)
    slot_of = jnp.sum(
        jnp.where(slot_request[None, :] == request_ids[:, None], request_ids[None, :], 0), axis=1
    )
    rank_score = jnp.einsum(
        "rcs,rtc->trs",
        picks.astype(jnp.float32),
        returned[slot_of],
        precision=lax.Precision.HIGHEST,
    )
    return (prerank_score, rank_score)


def solution(mesh):
    return jax.shard_map(
        on_device,
        mesh=mesh,
        in_specs=(
            P("groups", ("wide", "narrow"), None),
            P(),
            P(),
            P(),
            P("groups", None),
            P("groups", None),
            P("groups"),
            P(("groups", "wide"), None, None, "narrow"),
            P(("groups", "wide"), "narrow", None),
            P(("groups", "wide")),
            P(),
            P(),
            P("narrow", None, None),
            P(),
            P(),
            P("narrow", None, None),
            P("narrow", None),
        ),
        out_specs=(P("groups", ("wide", "narrow")), P(None, "groups", ("wide", "narrow"))),
        check_vma=False,
    )
```

```python
import functools

import jax
import jax.numpy as jnp
from jax import lax
from jax.experimental import pallas as pl
from jax.experimental.pallas import tpu as pltpu
from jax.sharding import PartitionSpec as P

NT = (((1,), (1,)), ((), ()))
VMEM = pl.BlockSpec(memory_space=pltpu.VMEM)
SMEM = pl.BlockSpec(memory_space=pltpu.SMEM)
ANY = pl.BlockSpec(memory_space=pl.ANY)
VMEM_LIMIT = 16 * 1024 * 1024
LANES = 128
BIAS_ROWS = 8
BRIEF = pl.CostEstimate(flops=1, bytes_accessed=1, transcendentals=0)


def in_hbm(values):
    return pltpu.with_memory_space_constraint(values, pltpu.HBM)


def in_vmem(values):
    return pltpu.with_memory_space_constraint(values, pltpu.VMEM)


def dot_f32(a, b):
    return jnp.dot(a, b, preferred_element_type=jnp.float32)


def dot_nt(a, b):
    return lax.dot_general(a, b, NT, preferred_element_type=jnp.float32)


def split_by(values, divisor):
    if divisor & (divisor - 1) == 0:
        shift = divisor.bit_length() - 1
        return lax.shift_right_logical(values, shift), values & (divisor - 1)
    quotient = lax.div(values, divisor)
    return quotient, values - quotient * divisor


def three_parts(values):
    high = values.astype(jnp.bfloat16)
    rest = values - high.astype(jnp.float32)
    middle = rest.astype(jnp.bfloat16)
    low = (rest - middle.astype(jnp.float32)).astype(jnp.bfloat16)
    return jnp.concatenate([high, middle, low], axis=0)


def sum_parts(stacked, rows):
    return stacked[:rows] + stacked[rows : 2 * rows] + stacked[2 * rows :]


def pack_body(
    narrow_count,
    half,
    slot_hbm,
    kept_hbm,
    cand_hbm,
    out_hbm,
    lane_ref,
    back_ref,
    order_ref,
    slot_ref,
    kept_ref,
    cand_ref,
    out_ref,
    sems,
):
    requests, shard_len, _ = cand_ref.shape
    kept_count = kept_ref.shape[1]
    kept_copy = pltpu.make_async_copy(kept_hbm, kept_ref, sems.at[0])
    cand_copy = pltpu.make_async_copy(cand_hbm, cand_ref, sems.at[1])
    slot_copy = pltpu.make_async_copy(slot_hbm, slot_ref, sems.at[2])
    for copy in (kept_copy, slot_copy, cand_copy):
        copy.start()
    device = lax.axis_index("wide") * narrow_count + lax.axis_index("narrow")
    base = device * shard_len
    ids = base + lax.broadcasted_iota(jnp.int32, (shard_len, kept_count), 0)
    request_rows = lax.broadcasted_iota(jnp.int32, (requests, kept_count), 0)
    kept_copy.wait()
    flags = jnp.zeros((requests, shard_len), jnp.float32)
    for r in range(requests):
        hits = jnp.where(kept_ref[r : r + 1, :] == ids, 1.0, 0.0).astype(jnp.bfloat16)
        row = jnp.where(request_rows == r, 1.0, 0.0).astype(jnp.bfloat16)
        flags = flags + dot_nt(row, hits)
    earlier = lax.broadcasted_iota(jnp.int32, (shard_len, shard_len), 0) < lax.broadcasted_iota(
        jnp.int32, (shard_len, shard_len), 1
    )
    places = dot_f32(
        flags.astype(jnp.bfloat16), jnp.where(earlier, 1.0, 0.0).astype(jnp.bfloat16)
    ).astype(jnp.int32)
    before = jnp.sum((kept_ref[...] < base).astype(jnp.int32), axis=1, keepdims=True)
    _, owner = split_by(before + places, narrow_count)
    within, _ = split_by(places, narrow_count)
    kept_here = flags > 0.5
    lane_ref[...] = jnp.where(kept_here, owner * half + within, -1)
    offset = lax.rem(device * half, LANES)
    back_ref[...] = jnp.where(kept_here, owner * LANES + offset + within, -1)
    rows = narrow_count * half
    row_at = lax.broadcasted_iota(jnp.int32, (rows, shard_len), 0)
    slot_copy.wait()
    cand_copy.wait()
    zeros = jnp.zeros((rows, shard_len), jnp.bfloat16)
    for s in range(0, requests, 2):
        picks, blocks = [], []
        for i in range(2):
            r = slot_ref[s + i]
            order_ref[s + i : s + i + 1, :] = jnp.full((1, LANES), r, jnp.int32)
            pick = jnp.where(lane_ref[pl.ds(r, 1), :] == row_at, 1.0, 0.0).astype(jnp.bfloat16)
            picks.append(jnp.concatenate([pick, zeros] if i == 0 else [zeros, pick], axis=1))
            blocks.append(cand_ref[r])
        both = dot_f32(jnp.concatenate(picks, axis=0), jnp.concatenate(blocks, axis=0))
        part = pl.ds(s * rows, 2 * rows)
        out_ref[part, :] = both.astype(jnp.bfloat16)
        pltpu.make_async_copy(out_ref.at[part], out_hbm.at[part], sems.at[3]).start()
    pltpu.make_async_copy(out_ref, out_hbm, sems.at[3]).wait()


def pack_rows(slot_request, kept_index, candidates, narrow_count, half):
    requests, shard_len, features = candidates.shape
    rows = requests * narrow_count * half
    return pl.pallas_call(
        functools.partial(pack_body, narrow_count, half),
        out_shape=(
            pltpu.HBM((rows, features), jnp.bfloat16),
            jax.ShapeDtypeStruct((requests, shard_len), jnp.int32),
            jax.ShapeDtypeStruct((requests, shard_len), jnp.int32),
            jax.ShapeDtypeStruct((requests, LANES), jnp.int32),
        ),
        in_specs=[ANY, ANY, ANY],
        out_specs=(ANY, VMEM, VMEM, VMEM),
        scratch_shapes=[
            pltpu.SMEM(slot_request.shape, jnp.int32),
            pltpu.VMEM(kept_index.shape, jnp.int32),
            pltpu.VMEM((requests, shard_len, features), jnp.bfloat16),
            pltpu.VMEM((rows, features), jnp.bfloat16),
            pltpu.SemaphoreType.DMA((4,)),
        ],
        compiler_params=pltpu.CompilerParams(vmem_limit_bytes=VMEM_LIMIT),
        cost_estimate=pl.CostEstimate(
            flops=2 * rows * shard_len * features, bytes_accessed=4 * rows * features, transcendentals=0
        ),
        name="pack_rows",
    )(in_hbm(slot_request), in_hbm(kept_index), in_hbm(candidates))


def prerank_body(shard_len, cand_ref, inner_ref, bias_ref, outer_ref, user_ref, lane_ref, out_ref):
    requests = user_ref.shape[0]
    step = 2 if requests % 2 == 0 else 1
    for r in range(0, requests, step):
        rows = cand_ref[r * shard_len : (r + step) * shard_len, :]
        hidden = jnp.maximum(dot_f32(rows, inner_ref[...]) + bias_ref[...], 0.0).astype(jnp.bfloat16)
        embedded = dot_f32(hidden, outer_ref[...]).astype(jnp.bfloat16)
        scores = dot_nt(user_ref[...], embedded)
        for i in range(step):
            out_ref[r + i : r + i + 1, :] = scores[r + i : r + i + 1, i * shard_len : (i + 1) * shard_len]


def prerank(candidates, pre_inner, pre_bias, pre_outer, user_vector, lanes):
    requests, shard_len, features = candidates.shape
    rows = requests * shard_len
    return pl.pallas_call(
        functools.partial(prerank_body, shard_len),
        out_shape=jax.ShapeDtypeStruct((requests, shard_len), jnp.float32),
        in_specs=[VMEM] * 6,
        out_specs=VMEM,
        compiler_params=pltpu.CompilerParams(vmem_limit_bytes=VMEM_LIMIT),
        cost_estimate=BRIEF,
        name="prerank",
    )(
        candidates.reshape(rows, features),
        pre_inner,
        pre_bias.reshape(1, -1),
        pre_outer,
        user_vector,
        lanes,
    )


def prepare_body(narrow_count, weight_count, shards, shard_len, slot_at, slot_ref, length_ref, kept_ref, *rest):
    history_refs = rest[:narrow_count]
    bias_refs = rest[narrow_count : 2 * narrow_count]
    tower_outer_refs = rest[2 * narrow_count : 3 * narrow_count]
    pre_bias_ref, gain_ref, gate_bias_ref = rest[3 * narrow_count : 3 * narrow_count + 3]
    rest = rest[3 * narrow_count + 3 :]
    weight_refs = rest[:weight_count]
    target_ref, keys_ref, values_ref, vectors_ref, gate_offsets_ref, tower_rows_ref = rest[weight_count:][:6]
    loaded_refs = rest[weight_count + 6 : -1]
    sems = rest[-1]
    copies = [
        pltpu.make_async_copy(source, loaded, sems.at[i])
        for i, (source, loaded) in enumerate(zip(weight_refs, loaded_refs))
    ]
    for copy in copies:
        copy.start()
    group_size, _, span, head_columns = history_refs[0].shape
    heads_here = bias_refs[0].shape[1]
    rows_in = target_ref.shape[1]
    half = rows_in // shards
    me = lax.axis_index("narrow")
    request = slot_ref[lax.axis_index("wide") * group_size + slot_at]

    vectors_ref[0:1, :] = pre_bias_ref[...]
    vectors_ref[1:2, :] = gain_ref[...]
    tasks, experts = gate_bias_ref.shape
    gate_lane = lax.broadcasted_iota(jnp.int32, (tasks * experts, experts), 1)
    _, gate_row = split_by(lax.broadcasted_iota(jnp.int32, (tasks * experts, experts), 0), experts)
    offsets = jnp.broadcast_to(gate_bias_ref[...][:, None, :], (tasks, experts, experts))
    offsets = jnp.where(gate_row == gate_lane, offsets.reshape(tasks * experts, experts), 0.0)
    gate_offsets_ref[...] = jnp.broadcast_to(jnp.sum(offsets, axis=1, keepdims=True), gate_offsets_ref.shape)
    tasks_here, tower_width = tower_outer_refs[0].shape
    row = lax.broadcasted_iota(jnp.int32, (tower_rows_ref.shape[0], tower_width), 0)
    for i in range(narrow_count):
        outer = tower_outer_refs[i][...].astype(jnp.float32)
        for t in range(tasks_here):
            task = lax.rem(me + i, narrow_count) * tasks_here + t
            at = (i * tasks_here + t) * tower_width
            tower_rows_ref[:, at : at + tower_width] = jnp.where(row == task, outer[t : t + 1, :], 0.0).astype(
                jnp.bfloat16
            )

    kept_row = kept_ref[pl.ds(request, 1), :]
    edge = lax.broadcasted_iota(jnp.int32, (shards, kept_row.shape[1]), 0) * shard_len
    starts = jnp.sum((kept_row < edge).astype(jnp.int32), axis=1, keepdims=True)
    ends = jnp.sum((kept_row < edge + shard_len).astype(jnp.int32), axis=1, keepdims=True)
    first, _ = split_by(starts + (narrow_count - 1) - me, narrow_count)
    last, _ = split_by(ends + (narrow_count - 1) - me, narrow_count)
    lane_source, lane_within = split_by(lax.broadcasted_iota(jnp.int32, (shards, rows_in), 1), half)
    mine = lane_source == lax.broadcasted_iota(jnp.int32, (shards, rows_in), 0)
    target = jnp.where(mine & (first + lane_within < last), first + lane_within + 1, 0)
    target = jnp.sum(target, axis=0, keepdims=True) - 1
    target_ref[...] = jnp.broadcast_to(target, target_ref.shape)

    head_size = head_columns // heads_here
    tile = 2 * head_size
    pairs_here = heads_here // 2
    visible = lax.broadcasted_iota(jnp.int32, (1, span), 1) < length_ref[slot_at]
    row = lax.broadcasted_iota(jnp.int32, (BIAS_ROWS, span), 0)
    for i in range(narrow_count):
        for t in range(pairs_here):
            at = i * pairs_here + t
            keys = history_refs[i][slot_at, 0, :, t * tile : (t + 1) * tile]
            keys_ref[at, :tile, :] = jnp.transpose(keys.astype(jnp.float32)).astype(jnp.bfloat16)
            bias = jnp.zeros((BIAS_ROWS, span), jnp.float32)
            for h in range(2):
                head = 2 * t + h
                masked = jnp.where(visible, bias_refs[i][slot_at, head : head + 1, :], -1e30)
                bias = jnp.where(row == h, masked, bias)
            high = bias.astype(jnp.bfloat16).astype(jnp.float32)
            middle = (bias - high).astype(jnp.bfloat16).astype(jnp.float32)
            parts = [high, middle, bias - high - middle, jnp.zeros_like(bias)]
            keys_ref[at, tile:, :] = jnp.concatenate(parts, axis=0).astype(jnp.bfloat16)
            values_ref[at] = history_refs[i][slot_at, 1, :, t * tile : (t + 1) * tile]
    for copy in copies:
        copy.wait()


def prepare(
    slot_request,
    lengths,
    kept_index,
    history,
    biases,
    tower_outer,
    pre_bias,
    norm_gain,
    gate_bias,
    weights,
    shards,
    shard_len,
    half,
    slot_at,
):
    narrow_count = len(history)
    _, _, span, head_columns = history[0].shape
    heads_here = biases[0].shape[1]
    pairs = narrow_count * heads_here // 2
    tile = 2 * head_columns // heads_here
    tasks, experts = gate_bias.shape
    width = norm_gain.shape[0]
    bf16 = jnp.bfloat16
    return pl.pallas_call(
        functools.partial(prepare_body, narrow_count, len(weights), shards, shard_len, slot_at),
        out_shape=(
            pltpu.VMEM((8, shards * half), jnp.int32),
            pltpu.VMEM((pairs, tile + 4 * BIAS_ROWS, span), bf16),
            pltpu.VMEM((pairs, span, tile), bf16),
            pltpu.VMEM((8, width), jnp.float32),
            pltpu.VMEM((tasks * experts, LANES), jnp.float32),
            pltpu.VMEM((-(-tasks // 16) * 16, tasks * tower_outer[0].shape[1]), bf16),
            *[pltpu.VMEM(weight.shape, weight.dtype) for weight in weights],
        ),
        in_specs=[SMEM, SMEM] + [VMEM] * (4 + 3 * narrow_count) + [ANY] * len(weights),
        out_specs=(VMEM,) * (6 + len(weights)),
        scratch_shapes=[
            pltpu.SemaphoreType.DMA((len(weights),)),
        ],
        compiler_params=pltpu.CompilerParams(vmem_limit_bytes=VMEM_LIMIT),
        cost_estimate=BRIEF,
        name="prepare",
    )(
        slot_request,
        lengths,
        kept_index,
        *history,
        *biases,
        *tower_outer,
        pre_bias.reshape(1, -1),
        norm_gain.reshape(1, -1),
        gate_bias,
        *[in_hbm(weight) for weight in weights],
    )


def rank_body(narrow_count, pieces, shards, spread, *rest):
    expert_hbm = rest[:pieces]
    tower_hbm = rest[pieces : pieces + narrow_count]
    rest = rest[pieces + narrow_count :]
    arrived_ref, target_ref, vectors_ref, gate_offsets_ref, tower_rows_ref, keys_ref, values_ref = rest[:7]
    inner_ref, outer_ref, query_ref, gate_ref = rest[7:11]
    (
        out_ref,
        embed_ref,
        queries_ref,
        attended_ref,
        expert_out_ref,
        gates_ref,
        mixture_ref,
        expert_refs,
        tower_refs,
        sems,
    ) = rest[11:]
    own = expert_hbm[0].shape[0]
    own_copy = pltpu.make_async_copy(expert_hbm[0], expert_refs.at[pl.ds(0, own)], sems.at[0])
    own_copy.start()
    late_copies = []
    for i in range(1, pieces):
        at = sum(piece.shape[0] for piece in expert_hbm[:i])
        here = expert_refs.at[pl.ds(at, expert_hbm[i].shape[0])]
        late_copies.append(pltpu.make_async_copy(expert_hbm[i], here, sems.at[1]))
    for i in range(narrow_count):
        late_copies.append(pltpu.make_async_copy(tower_hbm[i], tower_refs.at[i], sems.at[2]))
    for copy in late_copies:
        copy.start()

    rows = embed_ref.shape[0]
    half = arrived_ref.shape[0] // shards
    experts = expert_refs.shape[0]
    experts_here = experts // narrow_count
    tasks_here = tower_refs.shape[1]
    tasks = narrow_count * tasks_here
    block = rows // experts
    blocks = rows // block
    me = lax.axis_index("narrow")

    here = lax.broadcasted_iota(jnp.int32, (rows, target_ref.shape[1]), 0)
    placing = jnp.where(target_ref[0:1, :] == here, 1.0, 0.0).astype(jnp.bfloat16)
    packed = dot_f32(placing, arrived_ref[...]).astype(jnp.bfloat16)
    hidden = jnp.maximum(dot_f32(packed, inner_ref[...]) + vectors_ref[0:1, :], 0.0).astype(jnp.bfloat16)
    embed = dot_f32(hidden, outer_ref[...]).astype(jnp.bfloat16)
    embed_ref[...] = embed
    queries = dot_f32(embed, query_ref[...]).astype(jnp.bfloat16)
    queries_ref[...] = queries

    tile = values_ref.shape[2]
    pairs = keys_ref.shape[0]
    scale = (tile // 2) ** (-0.5)
    left = lax.broadcasted_iota(jnp.int32, (rows, tile), 1) < tile // 2
    lane = lax.broadcasted_iota(jnp.int32, (rows, 4 * BIAS_ROWS), 1)
    _, part = split_by(lane, BIAS_ROWS)
    bias_lanes = lane < 3 * BIAS_ROWS
    ones = [jnp.where(bias_lanes & (part == h), 1.0, 0.0).astype(jnp.bfloat16) for h in range(2)]
    sum_columns = jnp.ones(values_ref.shape[1:], jnp.bfloat16)
    for pair in range(pairs):
        if pair == pairs - 1:
            own_copy.wait()
        _, place = split_by(me * (pairs // narrow_count) + pair, pairs)
        columns = pl.ds(pl.multiple_of(place * tile, tile), tile)
        scaled = queries_ref[:, columns].astype(jnp.float32) * scale
        query = [jnp.where(own, scaled, 0.0).astype(jnp.bfloat16) for own in (left, ~left)]
        query = jnp.concatenate([jnp.concatenate([query[h], ones[h]], axis=1) for h in range(2)], axis=0)
        scores = dot_f32(query, keys_ref[pair])
        powers = jnp.exp(scores - jnp.max(scores, axis=1, keepdims=True))
        values = jnp.concatenate([values_ref[pair], sum_columns], axis=1)
        result = dot_f32(powers.astype(jnp.bfloat16), values)
        merged = jnp.where(left, result[:rows, :tile], result[rows:, :tile])
        sums = jnp.where(left, result[:rows, tile:], result[rows:, tile:])
        attended_ref[:, columns] = (merged / sums).astype(jnp.bfloat16)

    mixed_in = embed_ref[...].astype(jnp.float32) + attended_ref[...].astype(jnp.float32)
    normed = (
        mixed_in
        * lax.rsqrt(jnp.mean(mixed_in * mixed_in, axis=1, keepdims=True) + 1e-06)
        * vectors_ref[1:2, :]
    ).astype(jnp.bfloat16)

    logits = dot_nt(gate_ref[...], normed) + gate_offsets_ref[:, 0:1]
    by_task = logits.reshape(tasks, experts, rows)
    gate_pow = jnp.exp(by_task - jnp.max(by_task, axis=1, keepdims=True))
    gate_probs = gate_pow / jnp.sum(gate_pow, axis=1, keepdims=True)
    gates = jnp.transpose(gate_probs.reshape(tasks * experts, rows)).astype(jnp.bfloat16)

    for e in range(experts):
        if e == own:
            here = expert_refs.at[pl.ds(own, experts - own)]
            pltpu.make_async_copy(here, here, sems.at[1]).wait()
            pltpu.make_async_copy(tower_refs, tower_refs, sems.at[2]).wait()
        result = jnp.maximum(dot_f32(normed, expert_refs[e]), 0.0).astype(jnp.bfloat16)
        for b in range(blocks):
            expert_out_ref[b, e * block : (e + 1) * block, :] = result[b * block : (b + 1) * block, :]

    gate_at = lax.broadcasted_iota(jnp.int32, (tasks * experts, experts * block), 0)
    column = lax.broadcasted_iota(jnp.int32, (tasks * experts, experts * block), 1)
    column_expert, _ = split_by(column, block)
    _, column_expert = split_by(column_expert + me * experts_here, experts)
    _, row_in_block = split_by(lax.broadcasted_iota(jnp.int32, (rows, experts * block), 0), block)
    _, column_row = split_by(lax.broadcasted_iota(jnp.int32, (rows, experts * block), 1), block)
    diagonal = jnp.where(row_in_block == column_row, 1.0, 0.0).astype(jnp.bfloat16)
    for t in range(tasks):
        _, task = split_by(me * tasks_here + t, tasks)
        expand = jnp.where(gate_at == column_expert + task * experts, 1.0, 0.0).astype(jnp.bfloat16)
        wide = dot_f32(gates, expand).astype(jnp.bfloat16) * diagonal
        for b in range(blocks):
            gates_ref[b, t * block : (t + 1) * block, :] = wide[b * block : (b + 1) * block, :]
    for b in range(blocks):
        mixture = dot_f32(gates_ref[b], expert_out_ref[b]).astype(jnp.bfloat16)
        for t in range(tasks):
            mixture_ref[t, b * block : (b + 1) * block, :] = mixture[t * block : (t + 1) * block, :]

    acts = []
    for i in range(narrow_count):
        for t in range(tasks_here):
            at = i * tasks_here + t
            acts.append(jnp.maximum(dot_f32(mixture_ref[at], tower_refs[i, t]), 0.0).astype(jnp.bfloat16))
    by_task = dot_nt(tower_rows_ref[...], jnp.concatenate(acts, axis=1))[:tasks]

    returned = sum_parts(dot_f32(three_parts(by_task), placing), tasks)
    if not spread:
        out_ref[...] = returned
        return
    rows_out = tasks // 2
    low = lax.broadcasted_iota(jnp.int32, (rows_out, LANES), 1) < LANES // 2
    for first in range(0, shards, LANES // half):
        values = returned[:, first * half : first * half + LANES]
        near, far = values[:rows_out], pltpu.roll(values, LANES // 2, 1)[rows_out:]
        for i in range(LANES // half):
            mixed = jnp.where(low, near, far) if 2 * i * half < LANES else jnp.where(low, far, near)
            out_ref[(first + i) * rows_out : (first + i + 1) * rows_out, :] = mixed


def rank_slot(
    arrived, target, keys, values, vectors, gate_offsets, tower_rows, weights, experts, towers, rows, shards, spread
):
    inner, outer, query, gate_rows = weights
    narrow_count = len(towers)
    rows_in = arrived.shape[0]
    width = outer.shape[1]
    tasks = narrow_count * towers[0].shape[0]
    expert_count = gate_rows.shape[0] // tasks
    expert_width = experts[0].shape[2]
    block = rows // expert_count
    if spread:
        out_shape = jax.ShapeDtypeStruct((shards * tasks // 2, LANES), jnp.float32)
    else:
        out_shape = jax.ShapeDtypeStruct((tasks, rows_in), jnp.float32)
    bf16 = jnp.bfloat16
    flops = 2 * rows * (rows_in * width + 3 * width * width + 2 * expert_count * width * expert_width)
    far = [*experts, *towers]
    near = [arrived, target, vectors, gate_offsets, tower_rows, keys, values, *weights]
    return pl.pallas_call(
        functools.partial(rank_body, narrow_count, len(experts), shards, spread),
        out_shape=out_shape,
        in_specs=[ANY] * len(far) + [VMEM] * len(near),
        out_specs=VMEM,
        scratch_shapes=[
            pltpu.VMEM((rows, width), bf16),
            pltpu.VMEM((rows, query.shape[1]), bf16),
            pltpu.VMEM((rows, query.shape[1]), bf16),
            pltpu.VMEM((rows // block, expert_count * block, expert_width), bf16),
            pltpu.VMEM((rows // block, tasks * block, expert_count * block), bf16),
            pltpu.VMEM((tasks, rows, expert_width), bf16),
            pltpu.VMEM((expert_count,) + experts[0].shape[1:], bf16),
            pltpu.VMEM((narrow_count,) + towers[0].shape, bf16),
            pltpu.SemaphoreType.DMA((3,)),
        ],
        compiler_params=pltpu.CompilerParams(vmem_limit_bytes=VMEM_LIMIT),
        cost_estimate=pl.CostEstimate(flops=flops, bytes_accessed=6 * 1024 * 1024, transcendentals=0),
        name="rank_slot",
    )(*[in_hbm(array) for array in far], *[in_vmem(array) for array in near])


def unpack_body(narrow_count, order_ref, back_ref, returned_ref, out_ref):
    requests, shard_len = back_ref.shape
    tasks = out_ref.shape[0]
    half_tasks = tasks // 2
    rows = narrow_count * half_tasks
    lanes = returned_ref.shape[1]
    lane_at = lax.broadcasted_iota(jnp.int32, (lanes, shard_len), 0)
    request_at = lax.broadcasted_iota(jnp.int32, (requests, shard_len), 0)
    results = [jnp.zeros((requests, shard_len), jnp.float32) for t in range(tasks)]
    for s in range(requests):
        mine = request_at == order_ref[s : s + 1, 0:1]
        back = jnp.sum(jnp.where(mine, back_ref[...], 0), axis=0, keepdims=True)
        picks = [
            jnp.where(back == lane_at + i * lanes, 1.0, 0.0).astype(jnp.bfloat16) for i in range(narrow_count)
        ]
        near = returned_ref[s * rows : (s + 1) * rows, :]
        parts = three_parts(jnp.concatenate([near, pltpu.roll(near, lanes // 2, 1)], axis=0))
        result = sum_parts(dot_f32(parts, jnp.concatenate(picks, axis=1)), 2 * rows)
        for t in range(tasks):
            at = t // half_tasks * rows + t % half_tasks
            value = result[at : at + 1, :shard_len]
            for i in range(1, narrow_count):
                row = at + i * half_tasks
                value = value + result[row : row + 1, i * shard_len : (i + 1) * shard_len]
            results[t] = jnp.where(mine, value, results[t])
    for t in range(tasks):
        out_ref[t] = results[t]


def unpack_rows(order, back, returned, tasks, narrow_count):
    requests, shard_len = back.shape
    return pl.pallas_call(
        functools.partial(unpack_body, narrow_count),
        out_shape=jax.ShapeDtypeStruct((tasks, requests, shard_len), jnp.float32),
        in_specs=[VMEM, VMEM, VMEM],
        out_specs=VMEM,
        compiler_params=pltpu.CompilerParams(vmem_limit_bytes=VMEM_LIMIT),
        name="unpack_rows",
    )(order, back, returned)


def lanes_of(kept_index, device_rank, shard_len, narrow_count, half):
    base = device_rank * shard_len
    ids = base + jnp.arange(shard_len, dtype=jnp.int32)
    flags = jnp.any(kept_index[:, :, None] == ids[None, None, :], axis=1)
    places = jnp.cumsum(flags.astype(jnp.int32), axis=1) - flags.astype(jnp.int32)
    before = jnp.sum((kept_index < base).astype(jnp.int32), axis=1, keepdims=True)
    return jnp.where(flags, (before + places) % narrow_count * half + places // narrow_count, -1)


def from_others(values, narrow_count):
    pieces = [values]
    for shift in range(1, narrow_count):
        steps = [((i + shift) % narrow_count, i) for i in range(narrow_count)]
        pieces.append(lax.ppermute(values, "narrow", steps))
    return pieces


def on_device(
    candidates,
    pre_inner,
    pre_bias,
    pre_outer,
    user_vector,
    kept_index,
    slot_request,
    history_kv,
    history_bias,
    history_length,
    query_weight,
    norm_gain,
    expert_weight,
    gate_weight,
    gate_bias,
    tower_inner,
    tower_outer,
):
    wide_count = lax.axis_size("wide")
    narrow_count = lax.axis_size("narrow")
    shards = wide_count * narrow_count
    wide_rank = lax.axis_index("wide")
    narrow_rank = lax.axis_index("narrow")
    device_rank = wide_rank * narrow_count + narrow_rank
    requests, shard_len, features = candidates.shape
    kept_count = kept_index.shape[1]
    capacity = 2 * kept_count // shards
    half = -(-capacity // narrow_count)
    group_size = history_kv.shape[0]
    tasks = narrow_count * tower_inner.shape[0]
    width = pre_outer.shape[1]
    both = ("wide", "narrow")
    blocked = (
        shard_len % 128 == 0
        and requests % 8 == 0
        and half % 16 == 0
        and LANES % (2 * half) == 0
        and tasks % 2 == 0
        and narrow_count * tasks // 2 % 8 == 0
        and shards * half % LANES == 0
        and group_size == 1
    )

    if blocked:
        packed, lanes, back, order = pack_rows(slot_request, kept_index, candidates, narrow_count, half)
    else:
        lanes = lanes_of(kept_index, device_rank, shard_len, narrow_count, half)
        picks = lanes[:, None, :] == jnp.arange(narrow_count * half, dtype=jnp.int32)[None, :, None]
        packed = jnp.einsum(
            "rcs,rsd->rcd", picks.astype(jnp.bfloat16), candidates, preferred_element_type=jnp.float32
        ).astype(jnp.bfloat16)[slot_request]
    packed = packed.reshape(wide_count, group_size, narrow_count, half, features)
    packed = jnp.swapaxes(packed, 1, 2).reshape(shards, group_size * half, features)
    arrived = lax.all_to_all(packed, both, split_axis=0, concat_axis=0, tiled=True)
    arrived = jnp.swapaxes(arrived.reshape(shards, group_size, half, features), 0, 1)
    arrived = arrived.reshape(group_size, shards * half, features)

    experts_here = expert_weight.shape[0]
    halves = [expert_weight[: experts_here // 2], expert_weight[experts_here // 2 :]]
    _, halves, *shared = lax.optimization_barrier(
        (packed, halves, history_kv, history_bias, tower_inner, tower_outer)
    )
    history, biases, towers, tower_outs = [from_others(values, narrow_count) for values in shared]
    halves = [from_others(values, narrow_count)[1:] for values in halves]
    experts = [expert_weight] + [piece for pieces in zip(*halves) for piece in pieces]
    if blocked:
        prerank_score = prerank(candidates, pre_inner, pre_bias, pre_outer, user_vector, lanes)
    else:
        hidden = jax.nn.relu(
            dot_f32(candidates.reshape(requests * shard_len, features), pre_inner) + pre_bias
        ).astype(jnp.bfloat16)
        embedded = dot_f32(hidden, pre_outer).astype(jnp.bfloat16)
        prerank_score = jnp.einsum(
            "rsd,rd->rs",
            embedded.reshape(requests, shard_len, width),
            user_vector,
            preferred_element_type=jnp.float32,
        )

    results = []
    for g in range(group_size):
        target, keys, values, vectors, gate_offsets, tower_rows, *loaded = prepare(
            slot_request,
            history_length,
            kept_index,
            history,
            biases,
            tower_outs,
            pre_bias,
            norm_gain,
            gate_bias,
            [pre_inner, pre_outer, query_weight, gate_weight.T],
            shards,
            shard_len,
            half,
            g,
        )
        target, prerank_score = lax.optimization_barrier((target, prerank_score))
        results.append(
            rank_slot(
                arrived[g],
                target,
                keys,
                values,
                vectors,
                gate_offsets,
                tower_rows,
                loaded,
                experts,
                towers,
                kept_count // narrow_count,
                shards,
                blocked,
            )
        )

    if blocked:
        sending = results[0].reshape(shards, tasks // 2, LANES)
        returned = lax.all_to_all(sending, both, split_axis=0, concat_axis=0, tiled=True)
        returned = returned.reshape(shards * tasks // 2, LANES)
        return (prerank_score, unpack_rows(order, back, returned, tasks, narrow_count))
    sending = jnp.stack(results).reshape(group_size, tasks, shards, half)
    sending = jnp.transpose(sending, (2, 0, 1, 3)).reshape(shards, -1)
    returned = lax.all_to_all(sending, both, split_axis=0, concat_axis=0, tiled=True)
    returned = returned.reshape(wide_count, narrow_count, group_size, tasks, half)
    returned = jnp.transpose(returned, (0, 2, 3, 1, 4)).reshape(requests, tasks, narrow_count * half)
    request_ids = jnp.arange(requests, dtype=jnp.int32)
    slot_of = jnp.sum(
        jnp.where(slot_request[None, :] == request_ids[:, None], request_ids[None, :], 0), axis=1
    )
    rank_score = jnp.einsum(
        "rcs,rtc->trs",
        picks.astype(jnp.float32),
        returned[slot_of],
        precision=lax.Precision.HIGHEST,
    )
    return (prerank_score, rank_score)


def solution(mesh):
    return jax.shard_map(
        on_device,
        mesh=mesh,
        in_specs=(
            P("groups", ("wide", "narrow"), None),
            P(),
            P(),
            P(),
            P("groups", None),
            P("groups", None),
            P("groups"),
            P(("groups", "wide"), None, None, "narrow"),
            P(("groups", "wide"), "narrow", None),
            P(("groups", "wide")),
            P(),
            P(),
            P("narrow", None, None),
            P(),
            P(),
            P("narrow", None, None),
            P("narrow", None),
        ),
        out_specs=(P("groups", ("wide", "narrow")), P(None, "groups", ("wide", "narrow"))),
        check_vma=False,
    )
```

```python
import functools

import jax
import jax.numpy as jnp
from jax import lax
from jax.experimental import pallas as pl
from jax.experimental.pallas import tpu as pltpu
from jax.sharding import PartitionSpec as P

NT = (((1,), (1,)), ((), ()))
VMEM = pl.BlockSpec(memory_space=pltpu.VMEM)
SMEM = pl.BlockSpec(memory_space=pltpu.SMEM)
ANY = pl.BlockSpec(memory_space=pl.ANY)
VMEM_LIMIT = 16 * 1024 * 1024
LANES = 128
BIAS_ROWS = 8
BRIEF = pl.CostEstimate(flops=1, bytes_accessed=1, transcendentals=0)


def in_hbm(values):
    return pltpu.with_memory_space_constraint(values, pltpu.HBM)


def in_vmem(values):
    return pltpu.with_memory_space_constraint(values, pltpu.VMEM)


def dot_f32(a, b):
    return jnp.dot(a, b, preferred_element_type=jnp.float32)


def dot_nt(a, b):
    return lax.dot_general(a, b, NT, preferred_element_type=jnp.float32)


def split_by(values, divisor):
    if divisor & (divisor - 1) == 0:
        shift = divisor.bit_length() - 1
        return lax.shift_right_logical(values, shift), values & (divisor - 1)
    quotient = lax.div(values, divisor)
    return quotient, values - quotient * divisor


def three_parts(values):
    high = values.astype(jnp.bfloat16)
    rest = values - high.astype(jnp.float32)
    middle = rest.astype(jnp.bfloat16)
    low = (rest - middle.astype(jnp.float32)).astype(jnp.bfloat16)
    return jnp.concatenate([high, middle, low], axis=0)


def sum_parts(stacked, rows):
    return stacked[:rows] + stacked[rows : 2 * rows] + stacked[2 * rows :]


def pack_body(
    narrow_count,
    half,
    slot_hbm,
    kept_hbm,
    cand_hbm,
    out_hbm,
    lane_ref,
    back_ref,
    order_ref,
    slot_ref,
    kept_ref,
    cand_ref,
    out_ref,
    sems,
):
    requests, shard_len, _ = cand_ref.shape
    kept_count = kept_ref.shape[1]
    kept_copy = pltpu.make_async_copy(kept_hbm, kept_ref, sems.at[0])
    cand_copy = pltpu.make_async_copy(cand_hbm, cand_ref, sems.at[1])
    slot_copy = pltpu.make_async_copy(slot_hbm, slot_ref, sems.at[2])
    for copy in (kept_copy, slot_copy, cand_copy):
        copy.start()
    device = lax.axis_index("wide") * narrow_count + lax.axis_index("narrow")
    base = device * shard_len
    ids = base + lax.broadcasted_iota(jnp.int32, (shard_len, kept_count), 0)
    request_rows = lax.broadcasted_iota(jnp.int32, (requests, kept_count), 0)
    kept_copy.wait()
    flags = jnp.zeros((requests, shard_len), jnp.float32)
    for r in range(requests):
        hits = jnp.where(kept_ref[r : r + 1, :] == ids, 1.0, 0.0).astype(jnp.bfloat16)
        row = jnp.where(request_rows == r, 1.0, 0.0).astype(jnp.bfloat16)
        flags = flags + dot_nt(row, hits)
    earlier = lax.broadcasted_iota(jnp.int32, (shard_len, shard_len), 0) < lax.broadcasted_iota(
        jnp.int32, (shard_len, shard_len), 1
    )
    places = dot_f32(
        flags.astype(jnp.bfloat16), jnp.where(earlier, 1.0, 0.0).astype(jnp.bfloat16)
    ).astype(jnp.int32)
    before = jnp.sum((kept_ref[...] < base).astype(jnp.int32), axis=1, keepdims=True)
    _, owner = split_by(before + places, narrow_count)
    within, _ = split_by(places, narrow_count)
    kept_here = flags > 0.5
    lane_ref[...] = jnp.where(kept_here, owner * half + within, -1)
    offset = lax.rem(device * half, LANES)
    back_ref[...] = jnp.where(kept_here, owner * LANES + offset + within, -1)
    rows = narrow_count * half
    row_at = lax.broadcasted_iota(jnp.int32, (rows, shard_len), 0)
    slot_copy.wait()
    cand_copy.wait()
    zeros = jnp.zeros((rows, shard_len), jnp.bfloat16)
    for s in range(0, requests, 2):
        picks, blocks = [], []
        for i in range(2):
            r = slot_ref[s + i]
            order_ref[s + i : s + i + 1, :] = jnp.full((1, LANES), r, jnp.int32)
            pick = jnp.where(lane_ref[pl.ds(r, 1), :] == row_at, 1.0, 0.0).astype(jnp.bfloat16)
            picks.append(jnp.concatenate([pick, zeros] if i == 0 else [zeros, pick], axis=1))
            blocks.append(cand_ref[r])
        both = dot_f32(jnp.concatenate(picks, axis=0), jnp.concatenate(blocks, axis=0))
        part = pl.ds(s * rows, 2 * rows)
        out_ref[part, :] = both.astype(jnp.bfloat16)
        pltpu.make_async_copy(out_ref.at[part], out_hbm.at[part], sems.at[3]).start()
    pltpu.make_async_copy(out_ref, out_hbm, sems.at[3]).wait()


def pack_rows(slot_request, kept_index, candidates, narrow_count, half):
    requests, shard_len, features = candidates.shape
    rows = requests * narrow_count * half
    return pl.pallas_call(
        functools.partial(pack_body, narrow_count, half),
        out_shape=(
            pltpu.HBM((rows, features), jnp.bfloat16),
            jax.ShapeDtypeStruct((requests, shard_len), jnp.int32),
            jax.ShapeDtypeStruct((requests, shard_len), jnp.int32),
            jax.ShapeDtypeStruct((requests, LANES), jnp.int32),
        ),
        in_specs=[ANY, ANY, ANY],
        out_specs=(ANY, VMEM, VMEM, VMEM),
        scratch_shapes=[
            pltpu.SMEM(slot_request.shape, jnp.int32),
            pltpu.VMEM(kept_index.shape, jnp.int32),
            pltpu.VMEM((requests, shard_len, features), jnp.bfloat16),
            pltpu.VMEM((rows, features), jnp.bfloat16),
            pltpu.SemaphoreType.DMA((4,)),
        ],
        compiler_params=pltpu.CompilerParams(vmem_limit_bytes=VMEM_LIMIT),
        cost_estimate=pl.CostEstimate(
            flops=2 * rows * shard_len * features, bytes_accessed=4 * rows * features, transcendentals=0
        ),
        name="pack_rows",
    )(in_hbm(slot_request), in_hbm(kept_index), in_hbm(candidates))


def prerank_body(shard_len, cand_ref, inner_ref, bias_ref, outer_ref, user_ref, lane_ref, out_ref):
    requests = user_ref.shape[0]
    step = 2 if requests % 2 == 0 else 1
    for r in range(0, requests, step):
        rows = cand_ref[r * shard_len : (r + step) * shard_len, :]
        hidden = jnp.maximum(dot_f32(rows, inner_ref[...]) + bias_ref[...], 0.0).astype(jnp.bfloat16)
        embedded = dot_f32(hidden, outer_ref[...]).astype(jnp.bfloat16)
        scores = dot_nt(user_ref[...], embedded)
        for i in range(step):
            out_ref[r + i : r + i + 1, :] = scores[r + i : r + i + 1, i * shard_len : (i + 1) * shard_len]


def prerank(candidates, pre_inner, pre_bias, pre_outer, user_vector, lanes):
    requests, shard_len, features = candidates.shape
    rows = requests * shard_len
    return pl.pallas_call(
        functools.partial(prerank_body, shard_len),
        out_shape=jax.ShapeDtypeStruct((requests, shard_len), jnp.float32),
        in_specs=[VMEM] * 6,
        out_specs=VMEM,
        compiler_params=pltpu.CompilerParams(vmem_limit_bytes=VMEM_LIMIT),
        cost_estimate=BRIEF,
        name="prerank",
    )(
        candidates.reshape(rows, features),
        pre_inner,
        pre_bias.reshape(1, -1),
        pre_outer,
        user_vector,
        lanes,
    )


def prepare_body(narrow_count, weight_count, shards, shard_len, slot_at, slot_ref, length_ref, kept_ref, *rest):
    history_refs = rest[:narrow_count]
    bias_refs = rest[narrow_count : 2 * narrow_count]
    tower_outer_refs = rest[2 * narrow_count : 3 * narrow_count]
    pre_bias_ref, gain_ref, gate_bias_ref = rest[3 * narrow_count : 3 * narrow_count + 3]
    rest = rest[3 * narrow_count + 3 :]
    weight_refs = rest[:weight_count]
    target_ref, keys_ref, values_ref, vectors_ref, gate_offsets_ref, tower_rows_ref = rest[weight_count:][:6]
    loaded_refs = rest[weight_count + 6 : -1]
    sems = rest[-1]
    copies = [
        pltpu.make_async_copy(source, loaded, sems.at[i])
        for i, (source, loaded) in enumerate(zip(weight_refs, loaded_refs))
    ]
    for copy in copies:
        copy.start()
    group_size, _, span, head_columns = history_refs[0].shape
    heads_here = bias_refs[0].shape[1]
    rows_in = target_ref.shape[1]
    half = rows_in // shards
    me = lax.axis_index("narrow")
    request = slot_ref[lax.axis_index("wide") * group_size + slot_at]

    vectors_ref[0:1, :] = pre_bias_ref[...]
    vectors_ref[1:2, :] = gain_ref[...]
    tasks, experts = gate_bias_ref.shape
    gate_lane = lax.broadcasted_iota(jnp.int32, (tasks * experts, experts), 1)
    _, gate_row = split_by(lax.broadcasted_iota(jnp.int32, (tasks * experts, experts), 0), experts)
    offsets = jnp.broadcast_to(gate_bias_ref[...][:, None, :], (tasks, experts, experts))
    offsets = jnp.where(gate_row == gate_lane, offsets.reshape(tasks * experts, experts), 0.0)
    gate_offsets_ref[...] = jnp.broadcast_to(jnp.sum(offsets, axis=1, keepdims=True), gate_offsets_ref.shape)
    tasks_here, tower_width = tower_outer_refs[0].shape
    row = lax.broadcasted_iota(jnp.int32, (tower_rows_ref.shape[0], tower_width), 0)
    for i in range(narrow_count):
        outer = tower_outer_refs[i][...].astype(jnp.float32)
        for t in range(tasks_here):
            task = lax.rem(me + i, narrow_count) * tasks_here + t
            at = (i * tasks_here + t) * tower_width
            tower_rows_ref[:, at : at + tower_width] = jnp.where(row == task, outer[t : t + 1, :], 0.0).astype(
                jnp.bfloat16
            )

    kept_row = kept_ref[pl.ds(request, 1), :]
    edge = lax.broadcasted_iota(jnp.int32, (shards, kept_row.shape[1]), 0) * shard_len
    starts = jnp.sum((kept_row < edge).astype(jnp.int32), axis=1, keepdims=True)
    ends = jnp.sum((kept_row < edge + shard_len).astype(jnp.int32), axis=1, keepdims=True)
    first, _ = split_by(starts + (narrow_count - 1) - me, narrow_count)
    last, _ = split_by(ends + (narrow_count - 1) - me, narrow_count)
    lane_source, lane_within = split_by(lax.broadcasted_iota(jnp.int32, (shards, rows_in), 1), half)
    mine = lane_source == lax.broadcasted_iota(jnp.int32, (shards, rows_in), 0)
    target = jnp.where(mine & (first + lane_within < last), first + lane_within + 1, 0)
    target = jnp.sum(target, axis=0, keepdims=True) - 1
    target_ref[...] = jnp.broadcast_to(target, target_ref.shape)

    head_size = head_columns // heads_here
    tile = 2 * head_size
    pairs_here = heads_here // 2
    visible = lax.broadcasted_iota(jnp.int32, (1, span), 1) < length_ref[slot_at]
    row = lax.broadcasted_iota(jnp.int32, (BIAS_ROWS, span), 0)
    for i in range(narrow_count):
        for t in range(pairs_here):
            at = i * pairs_here + t
            keys = history_refs[i][slot_at, 0, :, t * tile : (t + 1) * tile]
            keys_ref[at, :tile, :] = jnp.transpose(keys.astype(jnp.float32)).astype(jnp.bfloat16)
            bias = jnp.zeros((BIAS_ROWS, span), jnp.float32)
            for h in range(2):
                head = 2 * t + h
                masked = jnp.where(visible, bias_refs[i][slot_at, head : head + 1, :], -1e30)
                bias = jnp.where(row == h, masked, bias)
            high = bias.astype(jnp.bfloat16).astype(jnp.float32)
            middle = (bias - high).astype(jnp.bfloat16).astype(jnp.float32)
            parts = [high, middle, bias - high - middle, jnp.zeros_like(bias)]
            keys_ref[at, tile:, :] = jnp.concatenate(parts, axis=0).astype(jnp.bfloat16)
            values_ref[at] = history_refs[i][slot_at, 1, :, t * tile : (t + 1) * tile]
    for copy in copies:
        copy.wait()


def prepare(
    slot_request,
    lengths,
    kept_index,
    history,
    biases,
    tower_outer,
    pre_bias,
    norm_gain,
    gate_bias,
    weights,
    shards,
    shard_len,
    half,
    slot_at,
):
    narrow_count = len(history)
    _, _, span, head_columns = history[0].shape
    heads_here = biases[0].shape[1]
    pairs = narrow_count * heads_here // 2
    tile = 2 * head_columns // heads_here
    tasks, experts = gate_bias.shape
    width = norm_gain.shape[0]
    bf16 = jnp.bfloat16
    return pl.pallas_call(
        functools.partial(prepare_body, narrow_count, len(weights), shards, shard_len, slot_at),
        out_shape=(
            pltpu.VMEM((8, shards * half), jnp.int32),
            pltpu.VMEM((pairs, tile + 4 * BIAS_ROWS, span), bf16),
            pltpu.VMEM((pairs, span, tile), bf16),
            pltpu.VMEM((8, width), jnp.float32),
            pltpu.VMEM((tasks * experts, LANES), jnp.float32),
            pltpu.VMEM((-(-tasks // 16) * 16, tasks * tower_outer[0].shape[1]), bf16),
            *[pltpu.VMEM(weight.shape, weight.dtype) for weight in weights],
        ),
        in_specs=[SMEM, SMEM] + [VMEM] * (4 + 3 * narrow_count) + [ANY] * len(weights),
        out_specs=(VMEM,) * (6 + len(weights)),
        scratch_shapes=[
            pltpu.SemaphoreType.DMA((len(weights),)),
        ],
        compiler_params=pltpu.CompilerParams(vmem_limit_bytes=VMEM_LIMIT),
        cost_estimate=BRIEF,
        name="prepare",
    )(
        slot_request,
        lengths,
        kept_index,
        *history,
        *biases,
        *tower_outer,
        pre_bias.reshape(1, -1),
        norm_gain.reshape(1, -1),
        gate_bias,
        *[in_hbm(weight) for weight in weights],
    )


def rank_body(narrow_count, pieces, shards, spread, *rest):
    expert_hbm = rest[:pieces]
    tower_hbm = rest[pieces : pieces + narrow_count]
    rest = rest[pieces + narrow_count :]
    arrived_ref, target_ref, vectors_ref, gate_offsets_ref, tower_rows_ref, keys_ref, values_ref = rest[:7]
    inner_ref, outer_ref, query_ref, gate_ref = rest[7:11]
    (
        out_ref,
        embed_ref,
        queries_ref,
        attended_ref,
        expert_out_ref,
        gates_ref,
        mixture_ref,
        expert_refs,
        tower_refs,
        sems,
    ) = rest[11:]
    own = expert_hbm[0].shape[0] // 2
    rest_of_own = pl.ds(own, expert_hbm[0].shape[0] - own)
    own_copy = pltpu.make_async_copy(expert_hbm[0].at[pl.ds(0, own)], expert_refs.at[pl.ds(0, own)], sems.at[0])
    own_copy.start()
    late_copies = [pltpu.make_async_copy(expert_hbm[0].at[rest_of_own], expert_refs.at[rest_of_own], sems.at[1])]
    for i in range(1, pieces):
        at = sum(piece.shape[0] for piece in expert_hbm[:i])
        here = expert_refs.at[pl.ds(at, expert_hbm[i].shape[0])]
        late_copies.append(pltpu.make_async_copy(expert_hbm[i], here, sems.at[1]))
    for i in range(narrow_count):
        late_copies.append(pltpu.make_async_copy(tower_hbm[i], tower_refs.at[i], sems.at[2]))
    for copy in late_copies:
        copy.start()

    rows = embed_ref.shape[0]
    half = arrived_ref.shape[0] // shards
    experts = expert_refs.shape[0]
    experts_here = experts // narrow_count
    tasks_here = tower_refs.shape[1]
    tasks = narrow_count * tasks_here
    block = rows // experts
    blocks = rows // block
    me = lax.axis_index("narrow")

    here = lax.broadcasted_iota(jnp.int32, (rows, target_ref.shape[1]), 0)
    placing = jnp.where(target_ref[0:1, :] == here, 1.0, 0.0).astype(jnp.bfloat16)
    packed = dot_f32(placing, arrived_ref[...]).astype(jnp.bfloat16)
    hidden = jnp.maximum(dot_f32(packed, inner_ref[...]) + vectors_ref[0:1, :], 0.0).astype(jnp.bfloat16)
    embed = dot_f32(hidden, outer_ref[...]).astype(jnp.bfloat16)
    embed_ref[...] = embed
    queries = dot_f32(embed, query_ref[...]).astype(jnp.bfloat16)
    queries_ref[...] = queries

    tile = values_ref.shape[2]
    pairs = keys_ref.shape[0]
    scale = (tile // 2) ** (-0.5)
    left = lax.broadcasted_iota(jnp.int32, (rows, tile), 1) < tile // 2
    lane = lax.broadcasted_iota(jnp.int32, (rows, 4 * BIAS_ROWS), 1)
    _, part = split_by(lane, BIAS_ROWS)
    bias_lanes = lane < 3 * BIAS_ROWS
    ones = [jnp.where(bias_lanes & (part == h), 1.0, 0.0).astype(jnp.bfloat16) for h in range(2)]
    sum_columns = jnp.ones(values_ref.shape[1:], jnp.bfloat16)
    for pair in range(pairs):
        if pair == pairs - 1:
            own_copy.wait()
        _, place = split_by(me * (pairs // narrow_count) + pair, pairs)
        columns = pl.ds(pl.multiple_of(place * tile, tile), tile)
        scaled = queries_ref[:, columns].astype(jnp.float32) * scale
        query = [jnp.where(own, scaled, 0.0).astype(jnp.bfloat16) for own in (left, ~left)]
        query = jnp.concatenate([jnp.concatenate([query[h], ones[h]], axis=1) for h in range(2)], axis=0)
        scores = dot_f32(query, keys_ref[pair])
        powers = jnp.exp(scores - jnp.max(scores, axis=1, keepdims=True))
        values = jnp.concatenate([values_ref[pair], sum_columns], axis=1)
        result = dot_f32(powers.astype(jnp.bfloat16), values)
        merged = jnp.where(left, result[:rows, :tile], result[rows:, :tile])
        sums = jnp.where(left, result[:rows, tile:], result[rows:, tile:])
        attended_ref[:, columns] = (merged / sums).astype(jnp.bfloat16)

    mixed_in = embed_ref[...].astype(jnp.float32) + attended_ref[...].astype(jnp.float32)
    normed = (
        mixed_in
        * lax.rsqrt(jnp.mean(mixed_in * mixed_in, axis=1, keepdims=True) + 1e-06)
        * vectors_ref[1:2, :]
    ).astype(jnp.bfloat16)

    logits = dot_nt(gate_ref[...], normed) + gate_offsets_ref[:, 0:1]
    by_task = logits.reshape(tasks, experts, rows)
    gate_pow = jnp.exp(by_task - jnp.max(by_task, axis=1, keepdims=True))
    gate_probs = gate_pow / jnp.sum(gate_pow, axis=1, keepdims=True)
    gates = jnp.transpose(gate_probs.reshape(tasks * experts, rows)).astype(jnp.bfloat16)

    for e in range(experts):
        if e == own:
            here = expert_refs.at[pl.ds(own, experts - own)]
            pltpu.make_async_copy(here, here, sems.at[1]).wait()
            pltpu.make_async_copy(tower_refs, tower_refs, sems.at[2]).wait()
        result = jnp.maximum(dot_f32(normed, expert_refs[e]), 0.0).astype(jnp.bfloat16)
        for b in range(blocks):
            expert_out_ref[b, e * block : (e + 1) * block, :] = result[b * block : (b + 1) * block, :]

    gate_at = lax.broadcasted_iota(jnp.int32, (tasks * experts, experts * block), 0)
    column = lax.broadcasted_iota(jnp.int32, (tasks * experts, experts * block), 1)
    column_expert, _ = split_by(column, block)
    _, column_expert = split_by(column_expert + me * experts_here, experts)
    _, row_in_block = split_by(lax.broadcasted_iota(jnp.int32, (rows, experts * block), 0), block)
    _, column_row = split_by(lax.broadcasted_iota(jnp.int32, (rows, experts * block), 1), block)
    diagonal = jnp.where(row_in_block == column_row, 1.0, 0.0).astype(jnp.bfloat16)
    for t in range(tasks):
        _, task = split_by(me * tasks_here + t, tasks)
        expand = jnp.where(gate_at == column_expert + task * experts, 1.0, 0.0).astype(jnp.bfloat16)
        wide = dot_f32(gates, expand).astype(jnp.bfloat16) * diagonal
        for b in range(blocks):
            gates_ref[b, t * block : (t + 1) * block, :] = wide[b * block : (b + 1) * block, :]
    for b in range(blocks):
        mixture = dot_f32(gates_ref[b], expert_out_ref[b]).astype(jnp.bfloat16)
        for t in range(tasks):
            mixture_ref[t, b * block : (b + 1) * block, :] = mixture[t * block : (t + 1) * block, :]

    acts = []
    for i in range(narrow_count):
        for t in range(tasks_here):
            at = i * tasks_here + t
            acts.append(jnp.maximum(dot_f32(mixture_ref[at], tower_refs[i, t]), 0.0).astype(jnp.bfloat16))
    by_task = dot_nt(tower_rows_ref[...], jnp.concatenate(acts, axis=1))[:tasks]

    returned = sum_parts(dot_f32(three_parts(by_task), placing), tasks)
    if not spread:
        out_ref[...] = returned
        return
    rows_out = tasks // 2
    low = lax.broadcasted_iota(jnp.int32, (rows_out, LANES), 1) < LANES // 2
    for first in range(0, shards, LANES // half):
        values = returned[:, first * half : first * half + LANES]
        near, far = values[:rows_out], pltpu.roll(values, LANES // 2, 1)[rows_out:]
        for i in range(LANES // half):
            mixed = jnp.where(low, near, far) if 2 * i * half < LANES else jnp.where(low, far, near)
            out_ref[(first + i) * rows_out : (first + i + 1) * rows_out, :] = mixed


def rank_slot(
    arrived, target, keys, values, vectors, gate_offsets, tower_rows, weights, experts, towers, rows, shards, spread
):
    inner, outer, query, gate_rows = weights
    narrow_count = len(towers)
    rows_in = arrived.shape[0]
    width = outer.shape[1]
    tasks = narrow_count * towers[0].shape[0]
    expert_count = gate_rows.shape[0] // tasks
    expert_width = experts[0].shape[2]
    block = rows // expert_count
    if spread:
        out_shape = jax.ShapeDtypeStruct((shards * tasks // 2, LANES), jnp.float32)
    else:
        out_shape = jax.ShapeDtypeStruct((tasks, rows_in), jnp.float32)
    bf16 = jnp.bfloat16
    flops = 2 * rows * (rows_in * width + 3 * width * width + 2 * expert_count * width * expert_width)
    far = [*experts, *towers]
    near = [arrived, target, vectors, gate_offsets, tower_rows, keys, values, *weights]
    return pl.pallas_call(
        functools.partial(rank_body, narrow_count, len(experts), shards, spread),
        out_shape=out_shape,
        in_specs=[ANY] * len(far) + [VMEM] * len(near),
        out_specs=VMEM,
        scratch_shapes=[
            pltpu.VMEM((rows, width), bf16),
            pltpu.VMEM((rows, query.shape[1]), bf16),
            pltpu.VMEM((rows, query.shape[1]), bf16),
            pltpu.VMEM((rows // block, expert_count * block, expert_width), bf16),
            pltpu.VMEM((rows // block, tasks * block, expert_count * block), bf16),
            pltpu.VMEM((tasks, rows, expert_width), bf16),
            pltpu.VMEM((expert_count,) + experts[0].shape[1:], bf16),
            pltpu.VMEM((narrow_count,) + towers[0].shape, bf16),
            pltpu.SemaphoreType.DMA((3,)),
        ],
        compiler_params=pltpu.CompilerParams(vmem_limit_bytes=VMEM_LIMIT),
        cost_estimate=pl.CostEstimate(flops=flops, bytes_accessed=6 * 1024 * 1024, transcendentals=0),
        name="rank_slot",
    )(*[in_hbm(array) for array in far], *[in_vmem(array) for array in near])


def unpack_body(narrow_count, order_ref, back_ref, returned_ref, out_ref):
    requests, shard_len = back_ref.shape
    tasks = out_ref.shape[0]
    half_tasks = tasks // 2
    rows = narrow_count * half_tasks
    lanes = returned_ref.shape[1]
    lane_at = lax.broadcasted_iota(jnp.int32, (lanes, shard_len), 0)
    request_at = lax.broadcasted_iota(jnp.int32, (requests, shard_len), 0)
    results = [jnp.zeros((requests, shard_len), jnp.float32) for t in range(tasks)]
    for s in range(requests):
        mine = request_at == order_ref[s : s + 1, 0:1]
        back = jnp.sum(jnp.where(mine, back_ref[...], 0), axis=0, keepdims=True)
        picks = [
            jnp.where(back == lane_at + i * lanes, 1.0, 0.0).astype(jnp.bfloat16) for i in range(narrow_count)
        ]
        near = returned_ref[s * rows : (s + 1) * rows, :]
        parts = three_parts(jnp.concatenate([near, pltpu.roll(near, lanes // 2, 1)], axis=0))
        result = sum_parts(dot_f32(parts, jnp.concatenate(picks, axis=1)), 2 * rows)
        for t in range(tasks):
            at = t // half_tasks * rows + t % half_tasks
            value = result[at : at + 1, :shard_len]
            for i in range(1, narrow_count):
                row = at + i * half_tasks
                value = value + result[row : row + 1, i * shard_len : (i + 1) * shard_len]
            results[t] = jnp.where(mine, value, results[t])
    for t in range(tasks):
        out_ref[t] = results[t]


def unpack_rows(order, back, returned, tasks, narrow_count):
    requests, shard_len = back.shape
    return pl.pallas_call(
        functools.partial(unpack_body, narrow_count),
        out_shape=jax.ShapeDtypeStruct((tasks, requests, shard_len), jnp.float32),
        in_specs=[VMEM, VMEM, VMEM],
        out_specs=VMEM,
        compiler_params=pltpu.CompilerParams(vmem_limit_bytes=VMEM_LIMIT),
        name="unpack_rows",
    )(order, back, returned)


def lanes_of(kept_index, device_rank, shard_len, narrow_count, half):
    base = device_rank * shard_len
    ids = base + jnp.arange(shard_len, dtype=jnp.int32)
    flags = jnp.any(kept_index[:, :, None] == ids[None, None, :], axis=1)
    places = jnp.cumsum(flags.astype(jnp.int32), axis=1) - flags.astype(jnp.int32)
    before = jnp.sum((kept_index < base).astype(jnp.int32), axis=1, keepdims=True)
    return jnp.where(flags, (before + places) % narrow_count * half + places // narrow_count, -1)


def from_others(values, narrow_count):
    pieces = [values]
    for shift in range(1, narrow_count):
        steps = [((i + shift) % narrow_count, i) for i in range(narrow_count)]
        pieces.append(lax.ppermute(values, "narrow", steps))
    return pieces


def on_device(
    candidates,
    pre_inner,
    pre_bias,
    pre_outer,
    user_vector,
    kept_index,
    slot_request,
    history_kv,
    history_bias,
    history_length,
    query_weight,
    norm_gain,
    expert_weight,
    gate_weight,
    gate_bias,
    tower_inner,
    tower_outer,
):
    wide_count = lax.axis_size("wide")
    narrow_count = lax.axis_size("narrow")
    shards = wide_count * narrow_count
    wide_rank = lax.axis_index("wide")
    narrow_rank = lax.axis_index("narrow")
    device_rank = wide_rank * narrow_count + narrow_rank
    requests, shard_len, features = candidates.shape
    kept_count = kept_index.shape[1]
    capacity = 2 * kept_count // shards
    half = -(-capacity // narrow_count)
    group_size = history_kv.shape[0]
    tasks = narrow_count * tower_inner.shape[0]
    width = pre_outer.shape[1]
    both = ("wide", "narrow")
    blocked = (
        shard_len % 128 == 0
        and requests % 8 == 0
        and half % 16 == 0
        and LANES % (2 * half) == 0
        and tasks % 2 == 0
        and narrow_count * tasks // 2 % 8 == 0
        and shards * half % LANES == 0
        and group_size == 1
    )

    if blocked:
        packed, lanes, back, order = pack_rows(slot_request, kept_index, candidates, narrow_count, half)
    else:
        lanes = lanes_of(kept_index, device_rank, shard_len, narrow_count, half)
        picks = lanes[:, None, :] == jnp.arange(narrow_count * half, dtype=jnp.int32)[None, :, None]
        packed = jnp.einsum(
            "rcs,rsd->rcd", picks.astype(jnp.bfloat16), candidates, preferred_element_type=jnp.float32
        ).astype(jnp.bfloat16)[slot_request]
    packed = packed.reshape(wide_count, group_size, narrow_count, half, features)
    packed = jnp.swapaxes(packed, 1, 2).reshape(shards, group_size * half, features)
    arrived = lax.all_to_all(packed, both, split_axis=0, concat_axis=0, tiled=True)
    arrived = jnp.swapaxes(arrived.reshape(shards, group_size, half, features), 0, 1)
    arrived = arrived.reshape(group_size, shards * half, features)

    experts_here = expert_weight.shape[0]
    halves = [expert_weight[: experts_here // 2], expert_weight[experts_here // 2 :]]
    _, halves, *shared = lax.optimization_barrier(
        (packed, halves, history_kv, history_bias, tower_inner, tower_outer)
    )
    history, biases, towers, tower_outs = [from_others(values, narrow_count) for values in shared]
    halves = [from_others(values, narrow_count)[1:] for values in halves]
    experts = [expert_weight] + [piece for pieces in zip(*halves) for piece in pieces]
    if blocked:
        prerank_score = prerank(candidates, pre_inner, pre_bias, pre_outer, user_vector, lanes)
    else:
        hidden = jax.nn.relu(
            dot_f32(candidates.reshape(requests * shard_len, features), pre_inner) + pre_bias
        ).astype(jnp.bfloat16)
        embedded = dot_f32(hidden, pre_outer).astype(jnp.bfloat16)
        prerank_score = jnp.einsum(
            "rsd,rd->rs",
            embedded.reshape(requests, shard_len, width),
            user_vector,
            preferred_element_type=jnp.float32,
        )

    results = []
    for g in range(group_size):
        target, keys, values, vectors, gate_offsets, tower_rows, *loaded = prepare(
            slot_request,
            history_length,
            kept_index,
            history,
            biases,
            tower_outs,
            pre_bias,
            norm_gain,
            gate_bias,
            [pre_inner, pre_outer, query_weight, gate_weight.T],
            shards,
            shard_len,
            half,
            g,
        )
        target, prerank_score = lax.optimization_barrier((target, prerank_score))
        results.append(
            rank_slot(
                arrived[g],
                target,
                keys,
                values,
                vectors,
                gate_offsets,
                tower_rows,
                loaded,
                experts,
                towers,
                kept_count // narrow_count,
                shards,
                blocked,
            )
        )

    if blocked:
        sending = results[0].reshape(shards, tasks // 2, LANES)
        returned = lax.all_to_all(sending, both, split_axis=0, concat_axis=0, tiled=True)
        returned = returned.reshape(shards * tasks // 2, LANES)
        return (prerank_score, unpack_rows(order, back, returned, tasks, narrow_count))
    sending = jnp.stack(results).reshape(group_size, tasks, shards, half)
    sending = jnp.transpose(sending, (2, 0, 1, 3)).reshape(shards, -1)
    returned = lax.all_to_all(sending, both, split_axis=0, concat_axis=0, tiled=True)
    returned = returned.reshape(wide_count, narrow_count, group_size, tasks, half)
    returned = jnp.transpose(returned, (0, 2, 3, 1, 4)).reshape(requests, tasks, narrow_count * half)
    request_ids = jnp.arange(requests, dtype=jnp.int32)
    slot_of = jnp.sum(
        jnp.where(slot_request[None, :] == request_ids[:, None], request_ids[None, :], 0), axis=1
    )
    rank_score = jnp.einsum(
        "rcs,rtc->trs",
        picks.astype(jnp.float32),
        returned[slot_of],
        precision=lax.Precision.HIGHEST,
    )
    return (prerank_score, rank_score)


def solution(mesh):
    return jax.shard_map(
        on_device,
        mesh=mesh,
        in_specs=(
            P("groups", ("wide", "narrow"), None),
            P(),
            P(),
            P(),
            P("groups", None),
            P("groups", None),
            P("groups"),
            P(("groups", "wide"), None, None, "narrow"),
            P(("groups", "wide"), "narrow", None),
            P(("groups", "wide")),
            P(),
            P(),
            P("narrow", None, None),
            P(),
            P(),
            P("narrow", None, None),
            P("narrow", None),
        ),
        out_specs=(P("groups", ("wide", "narrow")), P(None, "groups", ("wide", "narrow"))),
        check_vma=False,
    )
```

```python
import functools

import jax
import jax.numpy as jnp
from jax import lax
from jax.experimental import pallas as pl
from jax.experimental.pallas import tpu as pltpu
from jax.sharding import PartitionSpec as P

NT = (((1,), (1,)), ((), ()))
VMEM = pl.BlockSpec(memory_space=pltpu.VMEM)
SMEM = pl.BlockSpec(memory_space=pltpu.SMEM)
ANY = pl.BlockSpec(memory_space=pl.ANY)
VMEM_LIMIT = 16 * 1024 * 1024
LANES = 128
BIAS_ROWS = 8
BRIEF = pl.CostEstimate(flops=1, bytes_accessed=1, transcendentals=0)


def in_hbm(values):
    return pltpu.with_memory_space_constraint(values, pltpu.HBM)


def in_vmem(values):
    return pltpu.with_memory_space_constraint(values, pltpu.VMEM)


def dot_f32(a, b):
    return jnp.dot(a, b, preferred_element_type=jnp.float32)


def dot_nt(a, b):
    return lax.dot_general(a, b, NT, preferred_element_type=jnp.float32)


def split_by(values, divisor):
    if divisor & (divisor - 1) == 0:
        shift = divisor.bit_length() - 1
        return lax.shift_right_logical(values, shift), values & (divisor - 1)
    quotient = lax.div(values, divisor)
    return quotient, values - quotient * divisor


def three_parts(values):
    high = values.astype(jnp.bfloat16)
    rest = values - high.astype(jnp.float32)
    middle = rest.astype(jnp.bfloat16)
    low = (rest - middle.astype(jnp.float32)).astype(jnp.bfloat16)
    return jnp.concatenate([high, middle, low], axis=0)


def sum_parts(stacked, rows):
    return stacked[:rows] + stacked[rows : 2 * rows] + stacked[2 * rows :]


def pack_body(
    narrow_count,
    half,
    slot_hbm,
    kept_hbm,
    cand_hbm,
    out_hbm,
    lane_ref,
    back_ref,
    order_ref,
    slot_ref,
    kept_ref,
    cand_ref,
    out_ref,
    sems,
):
    requests, shard_len, _ = cand_ref.shape
    kept_count = kept_ref.shape[1]
    kept_copy = pltpu.make_async_copy(kept_hbm, kept_ref, sems.at[0])
    cand_copy = pltpu.make_async_copy(cand_hbm, cand_ref, sems.at[1])
    slot_copy = pltpu.make_async_copy(slot_hbm, slot_ref, sems.at[2])
    for copy in (kept_copy, slot_copy, cand_copy):
        copy.start()
    device = lax.axis_index("wide") * narrow_count + lax.axis_index("narrow")
    base = device * shard_len
    ids = base + lax.broadcasted_iota(jnp.int32, (shard_len, kept_count), 0)
    request_rows = lax.broadcasted_iota(jnp.int32, (requests, kept_count), 0)
    kept_copy.wait()
    flags = jnp.zeros((requests, shard_len), jnp.float32)
    for r in range(requests):
        hits = jnp.where(kept_ref[r : r + 1, :] == ids, 1.0, 0.0).astype(jnp.bfloat16)
        row = jnp.where(request_rows == r, 1.0, 0.0).astype(jnp.bfloat16)
        flags = flags + dot_nt(row, hits)
    earlier = lax.broadcasted_iota(jnp.int32, (shard_len, shard_len), 0) < lax.broadcasted_iota(
        jnp.int32, (shard_len, shard_len), 1
    )
    places = dot_f32(
        flags.astype(jnp.bfloat16), jnp.where(earlier, 1.0, 0.0).astype(jnp.bfloat16)
    ).astype(jnp.int32)
    before = jnp.sum((kept_ref[...] < base).astype(jnp.int32), axis=1, keepdims=True)
    _, owner = split_by(before + places, narrow_count)
    within, _ = split_by(places, narrow_count)
    kept_here = flags > 0.5
    lane_ref[...] = jnp.where(kept_here, owner * half + within, -1)
    offset = lax.rem(device * half, LANES)
    back_ref[...] = jnp.where(kept_here, owner * LANES + offset + within, -1)
    rows = narrow_count * half
    row_at = lax.broadcasted_iota(jnp.int32, (rows, shard_len), 0)
    slot_copy.wait()
    cand_copy.wait()
    zeros = jnp.zeros((rows, shard_len), jnp.bfloat16)
    for s in range(0, requests, 2):
        picks, blocks = [], []
        for i in range(2):
            r = slot_ref[s + i]
            order_ref[s + i : s + i + 1, :] = jnp.full((1, LANES), r, jnp.int32)
            pick = jnp.where(lane_ref[pl.ds(r, 1), :] == row_at, 1.0, 0.0).astype(jnp.bfloat16)
            picks.append(jnp.concatenate([pick, zeros] if i == 0 else [zeros, pick], axis=1))
            blocks.append(cand_ref[r])
        both = dot_f32(jnp.concatenate(picks, axis=0), jnp.concatenate(blocks, axis=0))
        part = pl.ds(s * rows, 2 * rows)
        out_ref[part, :] = both.astype(jnp.bfloat16)
        pltpu.make_async_copy(out_ref.at[part], out_hbm.at[part], sems.at[3]).start()
    pltpu.make_async_copy(out_ref, out_hbm, sems.at[3]).wait()


def pack_rows(slot_request, kept_index, candidates, narrow_count, half):
    requests, shard_len, features = candidates.shape
    rows = requests * narrow_count * half
    return pl.pallas_call(
        functools.partial(pack_body, narrow_count, half),
        out_shape=(
            pltpu.HBM((rows, features), jnp.bfloat16),
            jax.ShapeDtypeStruct((requests, shard_len), jnp.int32),
            jax.ShapeDtypeStruct((requests, shard_len), jnp.int32),
            jax.ShapeDtypeStruct((requests, LANES), jnp.int32),
        ),
        in_specs=[ANY, ANY, ANY],
        out_specs=(ANY, VMEM, VMEM, VMEM),
        scratch_shapes=[
            pltpu.SMEM(slot_request.shape, jnp.int32),
            pltpu.VMEM(kept_index.shape, jnp.int32),
            pltpu.VMEM((requests, shard_len, features), jnp.bfloat16),
            pltpu.VMEM((rows, features), jnp.bfloat16),
            pltpu.SemaphoreType.DMA((4,)),
        ],
        compiler_params=pltpu.CompilerParams(vmem_limit_bytes=VMEM_LIMIT),
        cost_estimate=pl.CostEstimate(
            flops=2 * rows * shard_len * features, bytes_accessed=4 * rows * features, transcendentals=0
        ),
        name="pack_rows",
    )(in_hbm(slot_request), in_hbm(kept_index), in_hbm(candidates))


def prerank_body(shard_len, cand_ref, inner_ref, bias_ref, outer_ref, user_ref, lane_ref, out_ref):
    requests = user_ref.shape[0]
    step = 2 if requests % 2 == 0 else 1
    for r in range(0, requests, step):
        rows = cand_ref[r * shard_len : (r + step) * shard_len, :]
        hidden = jnp.maximum(dot_f32(rows, inner_ref[...]) + bias_ref[...], 0.0).astype(jnp.bfloat16)
        embedded = dot_f32(hidden, outer_ref[...]).astype(jnp.bfloat16)
        scores = dot_nt(user_ref[...], embedded)
        for i in range(step):
            out_ref[r + i : r + i + 1, :] = scores[r + i : r + i + 1, i * shard_len : (i + 1) * shard_len]


def prerank(candidates, pre_inner, pre_bias, pre_outer, user_vector, lanes):
    requests, shard_len, features = candidates.shape
    rows = requests * shard_len
    return pl.pallas_call(
        functools.partial(prerank_body, shard_len),
        out_shape=jax.ShapeDtypeStruct((requests, shard_len), jnp.float32),
        in_specs=[VMEM] * 6,
        out_specs=VMEM,
        compiler_params=pltpu.CompilerParams(vmem_limit_bytes=VMEM_LIMIT),
        cost_estimate=BRIEF,
        name="prerank",
    )(
        candidates.reshape(rows, features),
        pre_inner,
        pre_bias.reshape(1, -1),
        pre_outer,
        user_vector,
        lanes,
    )


def prepare_body(narrow_count, weight_count, shards, shard_len, slot_at, slot_ref, length_ref, kept_ref, *rest):
    history_refs = rest[:narrow_count]
    bias_refs = rest[narrow_count : 2 * narrow_count]
    tower_outer_refs = rest[2 * narrow_count : 3 * narrow_count]
    pre_bias_ref, gain_ref, gate_bias_ref = rest[3 * narrow_count : 3 * narrow_count + 3]
    rest = rest[3 * narrow_count + 3 :]
    weight_refs = rest[:weight_count]
    target_ref, keys_ref, values_ref, vectors_ref, gate_offsets_ref, tower_rows_ref = rest[weight_count:][:6]
    loaded_refs = rest[weight_count + 6 : -1]
    sems = rest[-1]
    copies = [
        pltpu.make_async_copy(source, loaded, sems.at[i])
        for i, (source, loaded) in enumerate(zip(weight_refs, loaded_refs))
    ]
    for copy in copies:
        copy.start()
    group_size, _, span, head_columns = history_refs[0].shape
    heads_here = bias_refs[0].shape[1]
    rows_in = target_ref.shape[1]
    half = rows_in // shards
    me = lax.axis_index("narrow")
    request = slot_ref[lax.axis_index("wide") * group_size + slot_at]

    vectors_ref[0:1, :] = pre_bias_ref[...]
    vectors_ref[1:2, :] = gain_ref[...]
    tasks, experts = gate_bias_ref.shape
    gate_lane = lax.broadcasted_iota(jnp.int32, (tasks * experts, experts), 1)
    _, gate_row = split_by(lax.broadcasted_iota(jnp.int32, (tasks * experts, experts), 0), experts)
    offsets = jnp.broadcast_to(gate_bias_ref[...][:, None, :], (tasks, experts, experts))
    offsets = jnp.where(gate_row == gate_lane, offsets.reshape(tasks * experts, experts), 0.0)
    gate_offsets_ref[...] = jnp.broadcast_to(jnp.sum(offsets, axis=1, keepdims=True), gate_offsets_ref.shape)
    tasks_here, tower_width = tower_outer_refs[0].shape
    row = lax.broadcasted_iota(jnp.int32, (tower_rows_ref.shape[0], tower_width), 0)
    for i in range(narrow_count):
        outer = tower_outer_refs[i][...].astype(jnp.float32)
        for t in range(tasks_here):
            task = lax.rem(me + i, narrow_count) * tasks_here + t
            at = (i * tasks_here + t) * tower_width
            tower_rows_ref[:, at : at + tower_width] = jnp.where(row == task, outer[t : t + 1, :], 0.0).astype(
                jnp.bfloat16
            )

    kept_row = kept_ref[pl.ds(request, 1), :]
    edge = lax.broadcasted_iota(jnp.int32, (shards, kept_row.shape[1]), 0) * shard_len
    starts = jnp.sum((kept_row < edge).astype(jnp.int32), axis=1, keepdims=True)
    ends = jnp.sum((kept_row < edge + shard_len).astype(jnp.int32), axis=1, keepdims=True)
    first, _ = split_by(starts + (narrow_count - 1) - me, narrow_count)
    last, _ = split_by(ends + (narrow_count - 1) - me, narrow_count)
    lane_source, lane_within = split_by(lax.broadcasted_iota(jnp.int32, (shards, rows_in), 1), half)
    mine = lane_source == lax.broadcasted_iota(jnp.int32, (shards, rows_in), 0)
    target = jnp.where(mine & (first + lane_within < last), first + lane_within + 1, 0)
    target = jnp.sum(target, axis=0, keepdims=True) - 1
    target_ref[...] = jnp.broadcast_to(target, target_ref.shape)

    head_size = head_columns // heads_here
    tile = 2 * head_size
    pairs_here = heads_here // 2
    visible = lax.broadcasted_iota(jnp.int32, (1, span), 1) < length_ref[slot_at]
    row = lax.broadcasted_iota(jnp.int32, (BIAS_ROWS, span), 0)
    for i in range(narrow_count):
        for t in range(pairs_here):
            at = i * pairs_here + t
            keys = history_refs[i][slot_at, 0, :, t * tile : (t + 1) * tile]
            keys_ref[at, :tile, :] = jnp.transpose(keys.astype(jnp.float32)).astype(jnp.bfloat16)
            bias = jnp.zeros((BIAS_ROWS, span), jnp.float32)
            for h in range(2):
                head = 2 * t + h
                masked = jnp.where(visible, bias_refs[i][slot_at, head : head + 1, :], -1e30)
                bias = jnp.where(row == h, masked, bias)
            high = bias.astype(jnp.bfloat16).astype(jnp.float32)
            middle = (bias - high).astype(jnp.bfloat16).astype(jnp.float32)
            parts = [high, middle, bias - high - middle, jnp.zeros_like(bias)]
            keys_ref[at, tile:, :] = jnp.concatenate(parts, axis=0).astype(jnp.bfloat16)
            values_ref[at] = history_refs[i][slot_at, 1, :, t * tile : (t + 1) * tile]
    for copy in copies:
        copy.wait()


def prepare(
    slot_request,
    lengths,
    kept_index,
    history,
    biases,
    tower_outer,
    pre_bias,
    norm_gain,
    gate_bias,
    weights,
    shards,
    shard_len,
    half,
    slot_at,
):
    narrow_count = len(history)
    _, _, span, head_columns = history[0].shape
    heads_here = biases[0].shape[1]
    pairs = narrow_count * heads_here // 2
    tile = 2 * head_columns // heads_here
    tasks, experts = gate_bias.shape
    width = norm_gain.shape[0]
    bf16 = jnp.bfloat16
    return pl.pallas_call(
        functools.partial(prepare_body, narrow_count, len(weights), shards, shard_len, slot_at),
        out_shape=(
            pltpu.VMEM((8, shards * half), jnp.int32),
            pltpu.VMEM((pairs, tile + 4 * BIAS_ROWS, span), bf16),
            pltpu.VMEM((pairs, span, tile), bf16),
            pltpu.VMEM((8, width), jnp.float32),
            pltpu.VMEM((tasks * experts, LANES), jnp.float32),
            pltpu.VMEM((-(-tasks // 16) * 16, tasks * tower_outer[0].shape[1]), bf16),
            *[pltpu.VMEM(weight.shape, weight.dtype) for weight in weights],
        ),
        in_specs=[SMEM, SMEM] + [VMEM] * (4 + 3 * narrow_count) + [ANY] * len(weights),
        out_specs=(VMEM,) * (6 + len(weights)),
        scratch_shapes=[
            pltpu.SemaphoreType.DMA((len(weights),)),
        ],
        compiler_params=pltpu.CompilerParams(vmem_limit_bytes=VMEM_LIMIT),
        cost_estimate=BRIEF,
        name="prepare",
    )(
        slot_request,
        lengths,
        kept_index,
        *history,
        *biases,
        *tower_outer,
        pre_bias.reshape(1, -1),
        norm_gain.reshape(1, -1),
        gate_bias,
        *[in_hbm(weight) for weight in weights],
    )


def rank_body(narrow_count, pieces, shards, spread, *rest):
    expert_hbm = rest[:pieces]
    tower_hbm = rest[pieces : pieces + narrow_count]
    rest = rest[pieces + narrow_count :]
    arrived_ref, target_ref, vectors_ref, gate_offsets_ref, tower_rows_ref, keys_ref, values_ref = rest[:7]
    inner_ref, outer_ref, query_ref, gate_ref = rest[7:11]
    (
        out_ref,
        embed_ref,
        queries_ref,
        attended_ref,
        expert_out_ref,
        gates_ref,
        mixture_ref,
        expert_refs,
        tower_refs,
        sems,
    ) = rest[11:]
    own = max(1, expert_hbm[0].shape[0] // 4)
    rest_of_own = pl.ds(own, expert_hbm[0].shape[0] - own)
    own_copy = pltpu.make_async_copy(expert_hbm[0].at[pl.ds(0, own)], expert_refs.at[pl.ds(0, own)], sems.at[0])
    own_copy.start()
    late_copies = [pltpu.make_async_copy(expert_hbm[0].at[rest_of_own], expert_refs.at[rest_of_own], sems.at[1])]
    for i in range(1, pieces):
        at = sum(piece.shape[0] for piece in expert_hbm[:i])
        here = expert_refs.at[pl.ds(at, expert_hbm[i].shape[0])]
        late_copies.append(pltpu.make_async_copy(expert_hbm[i], here, sems.at[1]))
    for i in range(narrow_count):
        late_copies.append(pltpu.make_async_copy(tower_hbm[i], tower_refs.at[i], sems.at[2]))
    for copy in late_copies:
        copy.start()

    rows = embed_ref.shape[0]
    half = arrived_ref.shape[0] // shards
    experts = expert_refs.shape[0]
    experts_here = experts // narrow_count
    tasks_here = tower_refs.shape[1]
    tasks = narrow_count * tasks_here
    block = rows // experts
    blocks = rows // block
    me = lax.axis_index("narrow")

    here = lax.broadcasted_iota(jnp.int32, (rows, target_ref.shape[1]), 0)
    placing = jnp.where(target_ref[0:1, :] == here, 1.0, 0.0).astype(jnp.bfloat16)
    packed = dot_f32(placing, arrived_ref[...]).astype(jnp.bfloat16)
    hidden = jnp.maximum(dot_f32(packed, inner_ref[...]) + vectors_ref[0:1, :], 0.0).astype(jnp.bfloat16)
    embed = dot_f32(hidden, outer_ref[...]).astype(jnp.bfloat16)
    embed_ref[...] = embed
    queries = dot_f32(embed, query_ref[...]).astype(jnp.bfloat16)
    queries_ref[...] = queries

    tile = values_ref.shape[2]
    pairs = keys_ref.shape[0]
    scale = (tile // 2) ** (-0.5)
    left = lax.broadcasted_iota(jnp.int32, (rows, tile), 1) < tile // 2
    lane = lax.broadcasted_iota(jnp.int32, (rows, 4 * BIAS_ROWS), 1)
    _, part = split_by(lane, BIAS_ROWS)
    bias_lanes = lane < 3 * BIAS_ROWS
    ones = [jnp.where(bias_lanes & (part == h), 1.0, 0.0).astype(jnp.bfloat16) for h in range(2)]
    sum_columns = jnp.ones(values_ref.shape[1:], jnp.bfloat16)
    for pair in range(pairs):
        if pair == pairs - 1:
            own_copy.wait()
        _, place = split_by(me * (pairs // narrow_count) + pair, pairs)
        columns = pl.ds(pl.multiple_of(place * tile, tile), tile)
        scaled = queries_ref[:, columns].astype(jnp.float32) * scale
        query = [jnp.where(own, scaled, 0.0).astype(jnp.bfloat16) for own in (left, ~left)]
        query = jnp.concatenate([jnp.concatenate([query[h], ones[h]], axis=1) for h in range(2)], axis=0)
        scores = dot_f32(query, keys_ref[pair])
        powers = jnp.exp(scores - jnp.max(scores, axis=1, keepdims=True))
        values = jnp.concatenate([values_ref[pair], sum_columns], axis=1)
        result = dot_f32(powers.astype(jnp.bfloat16), values)
        merged = jnp.where(left, result[:rows, :tile], result[rows:, :tile])
        sums = jnp.where(left, result[:rows, tile:], result[rows:, tile:])
        attended_ref[:, columns] = (merged / sums).astype(jnp.bfloat16)

    mixed_in = embed_ref[...].astype(jnp.float32) + attended_ref[...].astype(jnp.float32)
    normed = (
        mixed_in
        * lax.rsqrt(jnp.mean(mixed_in * mixed_in, axis=1, keepdims=True) + 1e-06)
        * vectors_ref[1:2, :]
    ).astype(jnp.bfloat16)

    logits = dot_nt(gate_ref[...], normed) + gate_offsets_ref[:, 0:1]
    by_task = logits.reshape(tasks, experts, rows)
    gate_pow = jnp.exp(by_task - jnp.max(by_task, axis=1, keepdims=True))
    gate_probs = gate_pow / jnp.sum(gate_pow, axis=1, keepdims=True)
    gates = jnp.transpose(gate_probs.reshape(tasks * experts, rows)).astype(jnp.bfloat16)

    for e in range(experts):
        if e == own:
            here = expert_refs.at[pl.ds(own, experts - own)]
            pltpu.make_async_copy(here, here, sems.at[1]).wait()
            pltpu.make_async_copy(tower_refs, tower_refs, sems.at[2]).wait()
        result = jnp.maximum(dot_f32(normed, expert_refs[e]), 0.0).astype(jnp.bfloat16)
        for b in range(blocks):
            expert_out_ref[b, e * block : (e + 1) * block, :] = result[b * block : (b + 1) * block, :]

    gate_at = lax.broadcasted_iota(jnp.int32, (tasks * experts, experts * block), 0)
    column = lax.broadcasted_iota(jnp.int32, (tasks * experts, experts * block), 1)
    column_expert, _ = split_by(column, block)
    _, column_expert = split_by(column_expert + me * experts_here, experts)
    _, row_in_block = split_by(lax.broadcasted_iota(jnp.int32, (rows, experts * block), 0), block)
    _, column_row = split_by(lax.broadcasted_iota(jnp.int32, (rows, experts * block), 1), block)
    diagonal = jnp.where(row_in_block == column_row, 1.0, 0.0).astype(jnp.bfloat16)
    for t in range(tasks):
        _, task = split_by(me * tasks_here + t, tasks)
        expand = jnp.where(gate_at == column_expert + task * experts, 1.0, 0.0).astype(jnp.bfloat16)
        wide = dot_f32(gates, expand).astype(jnp.bfloat16) * diagonal
        for b in range(blocks):
            gates_ref[b, t * block : (t + 1) * block, :] = wide[b * block : (b + 1) * block, :]
    for b in range(blocks):
        mixture = dot_f32(gates_ref[b], expert_out_ref[b]).astype(jnp.bfloat16)
        for t in range(tasks):
            mixture_ref[t, b * block : (b + 1) * block, :] = mixture[t * block : (t + 1) * block, :]

    acts = []
    for i in range(narrow_count):
        for t in range(tasks_here):
            at = i * tasks_here + t
            acts.append(jnp.maximum(dot_f32(mixture_ref[at], tower_refs[i, t]), 0.0).astype(jnp.bfloat16))
    by_task = dot_nt(tower_rows_ref[...], jnp.concatenate(acts, axis=1))[:tasks]

    returned = sum_parts(dot_f32(three_parts(by_task), placing), tasks)
    if not spread:
        out_ref[...] = returned
        return
    rows_out = tasks // 2
    low = lax.broadcasted_iota(jnp.int32, (rows_out, LANES), 1) < LANES // 2
    for first in range(0, shards, LANES // half):
        values = returned[:, first * half : first * half + LANES]
        near, far = values[:rows_out], pltpu.roll(values, LANES // 2, 1)[rows_out:]
        for i in range(LANES // half):
            mixed = jnp.where(low, near, far) if 2 * i * half < LANES else jnp.where(low, far, near)
            out_ref[(first + i) * rows_out : (first + i + 1) * rows_out, :] = mixed


def rank_slot(
    arrived, target, keys, values, vectors, gate_offsets, tower_rows, weights, experts, towers, rows, shards, spread
):
    inner, outer, query, gate_rows = weights
    narrow_count = len(towers)
    rows_in = arrived.shape[0]
    width = outer.shape[1]
    tasks = narrow_count * towers[0].shape[0]
    expert_count = gate_rows.shape[0] // tasks
    expert_width = experts[0].shape[2]
    block = rows // expert_count
    if spread:
        out_shape = jax.ShapeDtypeStruct((shards * tasks // 2, LANES), jnp.float32)
    else:
        out_shape = jax.ShapeDtypeStruct((tasks, rows_in), jnp.float32)
    bf16 = jnp.bfloat16
    flops = 2 * rows * (rows_in * width + 3 * width * width + 2 * expert_count * width * expert_width)
    far = [*experts, *towers]
    near = [arrived, target, vectors, gate_offsets, tower_rows, keys, values, *weights]
    return pl.pallas_call(
        functools.partial(rank_body, narrow_count, len(experts), shards, spread),
        out_shape=out_shape,
        in_specs=[ANY] * len(far) + [VMEM] * len(near),
        out_specs=VMEM,
        scratch_shapes=[
            pltpu.VMEM((rows, width), bf16),
            pltpu.VMEM((rows, query.shape[1]), bf16),
            pltpu.VMEM((rows, query.shape[1]), bf16),
            pltpu.VMEM((rows // block, expert_count * block, expert_width), bf16),
            pltpu.VMEM((rows // block, tasks * block, expert_count * block), bf16),
            pltpu.VMEM((tasks, rows, expert_width), bf16),
            pltpu.VMEM((expert_count,) + experts[0].shape[1:], bf16),
            pltpu.VMEM((narrow_count,) + towers[0].shape, bf16),
            pltpu.SemaphoreType.DMA((3,)),
        ],
        compiler_params=pltpu.CompilerParams(vmem_limit_bytes=VMEM_LIMIT),
        cost_estimate=pl.CostEstimate(flops=flops, bytes_accessed=6 * 1024 * 1024, transcendentals=0),
        name="rank_slot",
    )(*[in_hbm(array) for array in far], *[in_vmem(array) for array in near])


def unpack_body(narrow_count, order_ref, back_ref, returned_ref, out_ref):
    requests, shard_len = back_ref.shape
    tasks = out_ref.shape[0]
    half_tasks = tasks // 2
    rows = narrow_count * half_tasks
    lanes = returned_ref.shape[1]
    lane_at = lax.broadcasted_iota(jnp.int32, (lanes, shard_len), 0)
    request_at = lax.broadcasted_iota(jnp.int32, (requests, shard_len), 0)
    results = [jnp.zeros((requests, shard_len), jnp.float32) for t in range(tasks)]
    for s in range(requests):
        mine = request_at == order_ref[s : s + 1, 0:1]
        back = jnp.sum(jnp.where(mine, back_ref[...], 0), axis=0, keepdims=True)
        picks = [
            jnp.where(back == lane_at + i * lanes, 1.0, 0.0).astype(jnp.bfloat16) for i in range(narrow_count)
        ]
        near = returned_ref[s * rows : (s + 1) * rows, :]
        parts = three_parts(jnp.concatenate([near, pltpu.roll(near, lanes // 2, 1)], axis=0))
        result = sum_parts(dot_f32(parts, jnp.concatenate(picks, axis=1)), 2 * rows)
        for t in range(tasks):
            at = t // half_tasks * rows + t % half_tasks
            value = result[at : at + 1, :shard_len]
            for i in range(1, narrow_count):
                row = at + i * half_tasks
                value = value + result[row : row + 1, i * shard_len : (i + 1) * shard_len]
            results[t] = jnp.where(mine, value, results[t])
    for t in range(tasks):
        out_ref[t] = results[t]


def unpack_rows(order, back, returned, tasks, narrow_count):
    requests, shard_len = back.shape
    return pl.pallas_call(
        functools.partial(unpack_body, narrow_count),
        out_shape=jax.ShapeDtypeStruct((tasks, requests, shard_len), jnp.float32),
        in_specs=[VMEM, VMEM, VMEM],
        out_specs=VMEM,
        compiler_params=pltpu.CompilerParams(vmem_limit_bytes=VMEM_LIMIT),
        name="unpack_rows",
    )(order, back, returned)


def lanes_of(kept_index, device_rank, shard_len, narrow_count, half):
    base = device_rank * shard_len
    ids = base + jnp.arange(shard_len, dtype=jnp.int32)
    flags = jnp.any(kept_index[:, :, None] == ids[None, None, :], axis=1)
    places = jnp.cumsum(flags.astype(jnp.int32), axis=1) - flags.astype(jnp.int32)
    before = jnp.sum((kept_index < base).astype(jnp.int32), axis=1, keepdims=True)
    return jnp.where(flags, (before + places) % narrow_count * half + places // narrow_count, -1)


def from_others(values, narrow_count):
    pieces = [values]
    for shift in range(1, narrow_count):
        steps = [((i + shift) % narrow_count, i) for i in range(narrow_count)]
        pieces.append(lax.ppermute(values, "narrow", steps))
    return pieces


def on_device(
    candidates,
    pre_inner,
    pre_bias,
    pre_outer,
    user_vector,
    kept_index,
    slot_request,
    history_kv,
    history_bias,
    history_length,
    query_weight,
    norm_gain,
    expert_weight,
    gate_weight,
    gate_bias,
    tower_inner,
    tower_outer,
):
    wide_count = lax.axis_size("wide")
    narrow_count = lax.axis_size("narrow")
    shards = wide_count * narrow_count
    wide_rank = lax.axis_index("wide")
    narrow_rank = lax.axis_index("narrow")
    device_rank = wide_rank * narrow_count + narrow_rank
    requests, shard_len, features = candidates.shape
    kept_count = kept_index.shape[1]
    capacity = 2 * kept_count // shards
    half = -(-capacity // narrow_count)
    group_size = history_kv.shape[0]
    tasks = narrow_count * tower_inner.shape[0]
    width = pre_outer.shape[1]
    both = ("wide", "narrow")
    blocked = (
        shard_len % 128 == 0
        and requests % 8 == 0
        and half % 16 == 0
        and LANES % (2 * half) == 0
        and tasks % 2 == 0
        and narrow_count * tasks // 2 % 8 == 0
        and shards * half % LANES == 0
        and group_size == 1
    )

    if blocked:
        packed, lanes, back, order = pack_rows(slot_request, kept_index, candidates, narrow_count, half)
    else:
        lanes = lanes_of(kept_index, device_rank, shard_len, narrow_count, half)
        picks = lanes[:, None, :] == jnp.arange(narrow_count * half, dtype=jnp.int32)[None, :, None]
        packed = jnp.einsum(
            "rcs,rsd->rcd", picks.astype(jnp.bfloat16), candidates, preferred_element_type=jnp.float32
        ).astype(jnp.bfloat16)[slot_request]
    packed = packed.reshape(wide_count, group_size, narrow_count, half, features)
    packed = jnp.swapaxes(packed, 1, 2).reshape(shards, group_size * half, features)
    arrived = lax.all_to_all(packed, both, split_axis=0, concat_axis=0, tiled=True)
    arrived = jnp.swapaxes(arrived.reshape(shards, group_size, half, features), 0, 1)
    arrived = arrived.reshape(group_size, shards * half, features)

    experts_here = expert_weight.shape[0]
    halves = [expert_weight[: experts_here // 2], expert_weight[experts_here // 2 :]]
    _, halves, *shared = lax.optimization_barrier(
        (packed, halves, history_kv, history_bias, tower_inner, tower_outer)
    )
    history, biases, towers, tower_outs = [from_others(values, narrow_count) for values in shared]
    halves = [from_others(values, narrow_count)[1:] for values in halves]
    experts = [expert_weight] + [piece for pieces in zip(*halves) for piece in pieces]
    if blocked:
        prerank_score = prerank(candidates, pre_inner, pre_bias, pre_outer, user_vector, lanes)
    else:
        hidden = jax.nn.relu(
            dot_f32(candidates.reshape(requests * shard_len, features), pre_inner) + pre_bias
        ).astype(jnp.bfloat16)
        embedded = dot_f32(hidden, pre_outer).astype(jnp.bfloat16)
        prerank_score = jnp.einsum(
            "rsd,rd->rs",
            embedded.reshape(requests, shard_len, width),
            user_vector,
            preferred_element_type=jnp.float32,
        )

    results = []
    for g in range(group_size):
        target, keys, values, vectors, gate_offsets, tower_rows, *loaded = prepare(
            slot_request,
            history_length,
            kept_index,
            history,
            biases,
            tower_outs,
            pre_bias,
            norm_gain,
            gate_bias,
            [pre_inner, pre_outer, query_weight, gate_weight.T],
            shards,
            shard_len,
            half,
            g,
        )
        target, prerank_score = lax.optimization_barrier((target, prerank_score))
        results.append(
            rank_slot(
                arrived[g],
                target,
                keys,
                values,
                vectors,
                gate_offsets,
                tower_rows,
                loaded,
                experts,
                towers,
                kept_count // narrow_count,
                shards,
                blocked,
            )
        )

    if blocked:
        sending = results[0].reshape(shards, tasks // 2, LANES)
        returned = lax.all_to_all(sending, both, split_axis=0, concat_axis=0, tiled=True)
        returned = returned.reshape(shards * tasks // 2, LANES)
        return (prerank_score, unpack_rows(order, back, returned, tasks, narrow_count))
    sending = jnp.stack(results).reshape(group_size, tasks, shards, half)
    sending = jnp.transpose(sending, (2, 0, 1, 3)).reshape(shards, -1)
    returned = lax.all_to_all(sending, both, split_axis=0, concat_axis=0, tiled=True)
    returned = returned.reshape(wide_count, narrow_count, group_size, tasks, half)
    returned = jnp.transpose(returned, (0, 2, 3, 1, 4)).reshape(requests, tasks, narrow_count * half)
    request_ids = jnp.arange(requests, dtype=jnp.int32)
    slot_of = jnp.sum(
        jnp.where(slot_request[None, :] == request_ids[:, None], request_ids[None, :], 0), axis=1
    )
    rank_score = jnp.einsum(
        "rcs,rtc->trs",
        picks.astype(jnp.float32),
        returned[slot_of],
        precision=lax.Precision.HIGHEST,
    )
    return (prerank_score, rank_score)


def solution(mesh):
    return jax.shard_map(
        on_device,
        mesh=mesh,
        in_specs=(
            P("groups", ("wide", "narrow"), None),
            P(),
            P(),
            P(),
            P("groups", None),
            P("groups", None),
            P("groups"),
            P(("groups", "wide"), None, None, "narrow"),
            P(("groups", "wide"), "narrow", None),
            P(("groups", "wide")),
            P(),
            P(),
            P("narrow", None, None),
            P(),
            P(),
            P("narrow", None, None),
            P("narrow", None),
        ),
        out_specs=(P("groups", ("wide", "narrow")), P(None, "groups", ("wide", "narrow"))),
        check_vma=False,
    )
```
